32 devices in a mesh: tower: 2 (over x), dp: 16 (over z, y, core).
Axes of the slice: x: 2, y: 2, z: 4, core: 2. Of those that a mesh axis runs over, the one named last changes fastest.
Arguments:
- tokens: bfloat16 [2, 2, 16, 512, 768], P('tower', None, 'dp')
- segments: int32 [2, 2, 16, 512], P('tower', None, 'dp'), may hold values from 0 to 7, never falling along the last dimension, each value on 1 to 256 neighbouring positions
- positives: int32 [2, 128], P(None, 'dp'), may hold values from 0 to 127, each once within a row
- token_grad: float32 [2, 2, 16, 512, 768], P('tower', None, 'dp'), may hold values from -6 to 6
- mix_weight: float32 [2, 768, 2304], P('tower', 'dp'), may hold values from -0.109375 to 0.109375
- out_weight: float32 [2, 768, 768], P('tower', 'dp'), may hold values from -1.75 to 1.75
- up_weight: float32 [2, 768, 3072], P('tower', 'dp'), may hold values from -0.21875 to 0.21875
- down_weight: float32 [2, 3072, 768], P('tower', 'dp'), may hold values from -0.109375 to 0.109375
- vectors: float32 [2, 12, 768], P('tower', None, 'dp')
- first_mix: float32 [2, 768, 2304], P('tower', 'dp'), may hold values from -0.0004272461 to 0.0004272461
- first_out: float32 [2, 768, 768], P('tower', 'dp'), may hold values from -0.0004272461 to 0.0004272461
- first_up: float32 [2, 768, 3072], P('tower', 'dp'), may hold values from -0.0004272461 to 0.0004272461
- first_down: float32 [2, 3072, 768], P('tower', 'dp'), may hold values from -0.0004272461 to 0.0004272461
- first_vectors: float32 [2, 12, 768], P('tower', None, 'dp'), may hold values from -0.00061035156 to 0.00061035156
- second_mix: float32 [2, 768, 2304], P('tower', 'dp'), may hold values from 3.5275338e-11 to 5.644054e-10
- second_out: float32 [2, 768, 768], P('tower', 'dp'), may hold values from 1.4110136e-12 to 7.055068e-12
- second_up: float32 [2, 768, 3072], P('tower', 'dp'), may hold values from 3.5275338e-11 to 5.644054e-10
- second_down: float32 [2, 3072, 768], P('tower', 'dp'), may hold values from 3.5275338e-11 to 5.644054e-10
- second_vectors: float32 [2, 12, 768], P('tower', None, 'dp'), may hold values from 1.4110135e-10 to 7.0550676e-10
Outputs:
- layer_output: bfloat16 [2, 2, 16, 512, 768], P('tower', None, 'dp')
- input_grad: float32 [2, 2, 16, 512, 768], P('tower', None, 'dp')
- new_mix: float32 [2, 768, 2304], P('tower', 'dp')
- new_out: float32 [2, 768, 768], P('tower', 'dp')
- new_up: float32 [2, 768, 3072], P('tower', 'dp')
- new_down: float32 [2, 3072, 768], P('tower', 'dp')
- new_vectors: float32 [2, 12, 768], P('tower', None, 'dp')
- moment_mix: float32 [2, 768, 2304], P('tower', 'dp')
- moment_out: float32 [2, 768, 768], P('tower', 'dp')
- moment_up: float32 [2, 768, 3072], P('tower', 'dp')
- moment_down: float32 [2, 3072, 768], P('tower', 'dp')
- moment_vectors: float32 [2, 12, 768], P('tower', None, 'dp')
- square_mix: float32 [2, 768, 2304], P('tower', 'dp')
- square_out: float32 [2, 768, 768], P('tower', 'dp')
- square_up: float32 [2, 768, 3072], P('tower', 'dp')
- square_down: float32 [2, 3072, 768], P('tower', 'dp')
- square_vectors: float32 [2, 12, 768], P('tower', None, 'dp')
- grad_square: float32 [], replicated
The draws below stay inside these ranges and needn't reach their ends.
Inputs may be any that keep to these rules, and one draw needn't show every extreme that they name: `segments`: in each row the segment numbers never fall, every one of 0 to 7 occurs, and one segment holds exactly 256 tokens. `positives`: within each micro-batch every passage is the positive of exactly one query.
All inputs are finite; a program needn't handle non-finite values.
Results may differ from the reference program's by a relative error of at most 0.012.
The reference program's roundings to bfloat16 on the way count: a program that leaves them out, or rounds other values in their place, can miss the bound.
Values may be sent and summed in bfloat16 or wider, within the bound.
No kernel may reach another device: no remote copies, remote signals or barrier semaphores. Data moves between devices by JAX's collectives and lax.ppermute only.
A program may use at most 192 MiB of HBM per device.

```python
import math
from functools import partial
import jax
import jax.numpy as jnp
import numpy as np
from jax import lax

D = 768
FF = 3072
H = 12
HD = 64
L = 512
SEGS = 8
MB = 2
STEP = 5
ROWS = 16
NQ = 128
PARAMS = 14174208


def draw_tokens(key, part):
    key = jax.random.fold_in(key, 11)
    column = jnp.arange(D, dtype=jnp.float32) / (D - 1)
    scales = 1.0 + 2.0 * column
    values = jnp.clip(jax.random.normal(key, (2, MB, ROWS, L, D), jnp.float32), -6.0, 6.0)
    return (values * scales).astype(jnp.bfloat16)


def draw_vectors(key, part):
    key = jax.random.fold_in(key, 23)
    column = jnp.arange(D, dtype=jnp.float32) / (D - 1)
    jitter = jax.random.uniform(key, (2, 12, D), jnp.float32, -1.0, 1.0)
    bottom_gain = 0.5
    gain_rows = (bottom_gain + column) * (1.0 + 0.2 * jitter)
    biases = 0.3 * jitter
    row_index = jnp.arange(12, dtype=jnp.int32)[:, None]
    is_gain = (row_index == 3) | (row_index == 10)
    return jnp.where(is_gain[None], gain_rows, biases).astype(jnp.float32)


def raised(entries, stream_key, source, target, shards_of, factor):
    def block_of(position):
        return (jnp.arange(entries.shape[position]) // (entries.shape[position] // shards_of)).reshape((-1,) + (1,) * (entries.ndim - 1 - position))

    near = jax.random.permutation(stream_key, shards_of)[block_of(target)]
    far = (block_of(target) + shards_of // 2) % shards_of
    return jnp.where((block_of(source) == near) | (block_of(source) == far), factor * entries, entries)


def shard_levels(rng, shape, shards, least, largest):
    factor_of = 1.0
    for position, shards_of in shards:
        draws = jax.random.uniform(jax.random.fold_in(jax.random.fold_in(rng, 6), position), (shards_of,), jnp.float32, least / len(shards), largest / len(shards))
        factor_of = factor_of * jnp.repeat(jnp.exp(draws), shape[position] // shards_of).reshape((-1,) + (1,) * (len(shape) - 1 - position))
    return factor_of


def profile(count, total, bound, lean):
    weights = [(1 << 20) // math.isqrt(grade ** lean) + 1 for grade in range(2, count + 1)]
    surplus, counts = total - bound - (count - 1), [1] * (count - 1)
    while surplus > 0:
        candidates = [i for i in range(count - 1) if counts[i] < bound]
        pool, left = sum([weights[i] for i in candidates]), surplus
        for i in candidates:
            extra = min(bound - counts[i], max(1, left * weights[i] // pool), surplus)
            counts[i] = counts[i] + extra
            surplus = surplus - extra
    return np.array([bound] + counts)


def ragged(key, count, total, most, slope):
    if count == 2:
        one = jax.random.randint(key, (), max(1, total - most), min(most, total - 1) + 1)
        return jnp.stack([one, total - one])
    tallies = jnp.asarray(profile(count, total, most, slope), jnp.int32)
    couples = (count - 1) // 2
    source_of, taker = tallies[1:1 + 2 * couples:2], tallies[2:2 + 2 * couples:2]
    margin = jnp.minimum(source_of - 1, most - taker)
    shifted = jax.random.randint(jax.random.fold_in(key, 1), (couples,), 0, 1 << 20) % (margin + 1)
    tallies = tallies.at[1:1 + 2 * couples:2].set(source_of - shifted).at[2:2 + 2 * couples:2].set(taker + shifted)
    return tallies[jax.random.permutation(jax.random.fold_in(key, 2), count)]


def bell_draw(key, shape, deviation, reach, cuts=(), kind=jnp.bfloat16):
    level = shard_levels(key, shape, cuts, -0.22, 0.18) if cuts else 1.0
    values = jax.random.normal(key, shape, jnp.float32) * deviation * level
    return jnp.minimum(jnp.maximum(values, -reach), reach).astype(kind)


def gaussian_with(stream_key, shape, scale, limit, shards, heavy, held_as=jnp.bfloat16):
    result = scale * jax.random.normal(stream_key, shape, jnp.float32)
    if shards:
        result = result * shard_levels(stream_key, shape, shards, -0.22, 0.18)
    return jnp.clip(raised(result, jax.random.fold_in(stream_key, 3), *heavy), -limit, limit).astype(held_as)


def setup_inputs(seed: int = 0) -> dict:
    key_of = jax.random.split(jax.random.key(seed), 20)
    return {
        "tokens": draw_tokens(jax.random.fold_in(key_of[19], 71), 0),
        "segments": jax.vmap(lambda own: jnp.searchsorted(jnp.cumsum(ragged(own, SEGS, L, L // 2, 0)), jnp.arange(L), side="right"))(jax.random.split(key_of[1], 2 * MB * ROWS)).reshape((2, MB, ROWS, L)).astype(jnp.int32),
        "positives": jax.vmap(lambda own: jax.random.permutation(own, NQ))(jax.random.split(key_of[2], MB)).reshape((MB, NQ)).astype(jnp.int32),
        "token_grad": gaussian_with(key_of[3], (2, MB, ROWS, L, D), 1.0, 6.0, ((0, 2), (2, 16)), (2, 4, 16, 2.0), jnp.float32),
        "mix_weight": bell_draw(key_of[4], (2, D, 3 * D), (4 * D) ** -0.5, 0.109375, ((0, 2), (1, 16)), jnp.float32),
        "out_weight": bell_draw(key_of[5], (2, D, D), (D * SEGS // L) ** -0.5, 1.75, ((0, 2), (1, 16)), jnp.float32),
        "up_weight": bell_draw(key_of[6], (2, D, FF), D ** -0.5, 0.21875, ((0, 2), (1, 16)), jnp.float32),
        "down_weight": bell_draw(key_of[7], (2, FF, D), FF ** -0.5, 0.109375, ((0, 2), (1, 16)), jnp.float32),
        "vectors": draw_vectors(jax.random.fold_in(key_of[19], 71), 0),
        "first_mix": bell_draw(key_of[9], (2, D, 3 * D), (0.111 / PARAMS ** 0.5), 0.0004272461, ((0, 2), (1, 16)), jnp.float32),
        "first_out": bell_draw(key_of[10], (2, D, D), (0.111 / PARAMS ** 0.5), 0.0004272461, ((0, 2), (1, 16)), jnp.float32),
        "first_up": bell_draw(key_of[11], (2, D, FF), (0.111 / PARAMS ** 0.5), 0.0004272461, ((0, 2), (1, 16)), jnp.float32),
        "first_down": bell_draw(key_of[12], (2, FF, D), (0.111 / PARAMS ** 0.5), 0.0004272461, ((0, 2), (1, 16)), jnp.float32),
        "first_vectors": bell_draw(key_of[13], (2, 12, D), (0.17 / PARAMS ** 0.5), 0.00061035156, ((0, 2), (2, 16)), jnp.float32),
        "second_mix": jnp.clip(jnp.exp(math.log(5.644054112963204e-10) - 2.7725887 * jax.random.uniform(key_of[14], (2, D, 3 * D), jnp.float32) ** shard_levels(key_of[14], (2, D, 3 * D), ((0, 2), (1, 16)), -0.2, 0.2)), 3.5275338206020024e-11, 5.644054112963204e-10),
        "second_out": jnp.clip(jnp.exp(math.log(7.055067901412526e-12) - 1.609438 * jax.random.uniform(key_of[15], (2, D, D), jnp.float32) ** shard_levels(key_of[15], (2, D, D), ((0, 2), (1, 16)), -0.2, 0.2)), 1.4110135585984618e-12, 7.055067901412526e-12),
        "second_up": jnp.clip(jnp.exp(math.log(5.644054112963204e-10) - 2.7725887 * jax.random.uniform(key_of[16], (2, D, FF), jnp.float32) ** shard_levels(key_of[16], (2, D, FF), ((0, 2), (1, 16)), -0.2, 0.2)), 3.5275338206020024e-11, 5.644054112963204e-10),
        "second_down": jnp.clip(jnp.exp(math.log(5.644054112963204e-10) - 2.7725887 * jax.random.uniform(key_of[17], (2, FF, D), jnp.float32) ** shard_levels(key_of[17], (2, FF, D), ((0, 2), (1, 16)), -0.2, 0.2)), 3.5275338206020024e-11, 5.644054112963204e-10),
        "second_vectors": jnp.clip(jnp.exp(math.log(7.055067641204005e-10) - 1.609438 * jax.random.uniform(key_of[18], (2, 12, D), jnp.float32) ** shard_levels(key_of[18], (2, 12, D), ((0, 2), (2, 16)), -0.2, 0.2)), 1.411013528240801e-10, 7.055067641204005e-10),
    }


@jax.custom_vjp
def low(v):
    return lax.optimization_barrier(v.astype(jnp.bfloat16)).astype(jnp.float32)

@jax.custom_vjp
def low_back(v):
    return v

def low_keep(v):
    return (low(v), None)

def low_pass(kept, grad):
    return (grad,)

def back_keep(v):
    return (v, None)

def back_low(kept, grad):
    return (low(grad),)
low.defvjp(low_keep, low_pass)
low_back.defvjp(back_keep, back_low)
highest = lax.Precision.HIGHEST
norm_eps = 1e-05
attention_scale = 0.125
score_scale = 0.0625
contrast_weight = 16.0
clip_norm = 1.0
beta_first = 0.9
beta_second = 0.999
adam_eps = 1e-08
weight_decay = 0.01
matrix_rate = 0.05
vector_rate = 0.5
masked_score = -1e+30

def matmul(first_op, second_op):
    return jnp.dot(first_op, second_op, precision=highest, preferred_element_type=jnp.float32)

def layer_norm(values, gain_row, shift_row):
    centred = values - lax.optimization_barrier(jnp.mean(values, axis=-1, keepdims=True))
    scaled = centred * lax.rsqrt(lax.optimization_barrier(jnp.mean(centred * centred, axis=-1, keepdims=True)) + norm_eps)
    return scaled * gain_row + shift_row

def cls_table(seg_row):
    starts = lax.optimization_barrier(jnp.sum((seg_row[None, :] < jnp.arange(SEGS, dtype=jnp.int32)[:, None]).astype(jnp.int32), axis=1)).astype(jnp.int32)
    return (jnp.arange(L, dtype=jnp.int32)[None, :] == starts[:, None]).astype(jnp.float32)

def row_layer(params, row_input, seg_row):
    mix_w, out_w, up_w, down_w, vec_w = params
    mixed_bias = jnp.concatenate([vec_w[0], jnp.zeros_like(vec_w[0]), vec_w[1]])
    mixed = low(low_back(matmul(low(row_input), mix_w) + mixed_bias))
    queries = mixed[:, :D].reshape(L, H, HD)
    key_rows = mixed[:, D:2 * D].reshape(L, H, HD)
    value_rows = mixed[:, 2 * D:].reshape(L, H, HD)
    scores = jnp.einsum('qhd,khd->hqk', queries, key_rows, precision=highest) * attention_scale
    same_doc = seg_row[:, None] == seg_row[None, :]
    scores = low_back(jnp.where(same_doc[None], scores, masked_score))
    probs = jax.nn.softmax(scores, axis=-1)
    context = jnp.einsum('hqk,khd->qhd', low(probs), value_rows, precision=highest).reshape(L, D)
    context = low(low_back(context))
    branch = low_back(matmul(context, out_w) + vec_w[2])
    hidden = layer_norm(row_input + branch, vec_w[3], vec_w[4])
    pre_act = low_back(matmul(low(hidden), up_w) + vec_w[5:9].reshape(FF))
    ffn_out = low_back(matmul(low(jax.nn.gelu(pre_act, approximate=False)), down_w) + vec_w[9])
    return layer_norm(hidden + ffn_out, vec_w[10], vec_w[11])

def tower_forward(params, tower_tokens, tower_segs):
    step_fn = jax.checkpoint(partial(row_layer, params))
    flat_tokens = tower_tokens.reshape(-1, L, D)
    flat_segs = tower_segs.reshape(-1, L)
    outputs = lax.map(lambda row_pair: step_fn(row_pair[0], row_pair[1]), (flat_tokens, flat_segs))
    tables = jax.vmap(cls_table)(flat_segs)
    pooled = jnp.einsum('rsl,rld->rsd', tables, outputs, precision=highest).reshape(MB, NQ, D)
    return (outputs.reshape(tower_tokens.shape), pooled)

def objective(params_query, params_passage, query_tokens, passage_tokens, segments, positives, token_grad):
    query_out, query_cls = tower_forward(params_query, query_tokens, segments[0])
    passage_out, passage_cls = tower_forward(params_passage, passage_tokens, segments[1])
    query_cls = low(low_back(query_cls))
    passage_cls = low(passage_cls)
    contrast = low_back(jnp.einsum('mqd,mpd->mqp', query_cls, passage_cls, precision=highest) * score_scale)
    picked = jnp.take_along_axis(contrast, positives[:, :, None], axis=2)[:, :, 0]
    contrast_loss = contrast_weight * jnp.sum(jax.scipy.special.logsumexp(contrast, axis=2) - picked)
    objective_value = contrast_loss + jnp.sum(query_out * token_grad[0]) + jnp.sum(passage_out * token_grad[1])
    return (objective_value, jnp.stack([query_out, passage_out]))

def adam_update(master, grad_full, first, second, rate, factor):
    clipped = grad_full * factor
    first_new = beta_first * first + (1.0 - beta_first) * clipped
    second_new = beta_second * second + (1.0 - beta_second) * clipped * clipped
    first_hat = first_new / (1.0 - beta_first ** STEP)
    second_hat = second_new / (1.0 - beta_second ** STEP)
    master_new = master - rate * (first_hat / (jnp.sqrt(second_hat) + adam_eps) + weight_decay * master)
    return (master_new, first_new, second_new)

def reference(tokens, segments, positives, token_grad, mix_weight, out_weight, up_weight, down_weight, vectors, first_mix, first_out, first_up, first_down, first_vectors, second_mix, second_out, second_up, second_down, second_vectors):
    masters = (mix_weight, out_weight, up_weight, down_weight, vectors)
    params_query = tuple((low(master[0]) for master in masters))
    params_passage = tuple((low(master[1]) for master in masters))
    tokens_full = tokens.astype(jnp.float32)
    cotangent = token_grad.astype(jnp.float32)

    def wrapped(first_params, second_params, query_tokens, passage_tokens):
        return objective(first_params, second_params, query_tokens, passage_tokens, segments, positives, cotangent)
    objective_value, pullback, outputs = jax.vjp(wrapped, params_query, params_passage, tokens_full[0], tokens_full[1], has_aux=True)
    grad_query, grad_passage, input_query, input_passage = pullback(jnp.ones_like(objective_value))
    grads = [jnp.stack([grad_query[index], grad_passage[index]]) for index in range(5)]
    grad_square = jnp.sum(grads[0] * grads[0])
    for index in range(1, 5):
        grad_square = grad_square + jnp.sum(grads[index] * grads[index])
    factor = jnp.minimum(1.0, clip_norm / (jnp.sqrt(grad_square) + 1e-06))
    firsts = (first_mix, first_out, first_up, first_down, first_vectors)
    seconds = (second_mix, second_out, second_up, second_down, second_vectors)
    rates = (matrix_rate, matrix_rate, matrix_rate, matrix_rate, vector_rate)
    results = [adam_update(masters[index], grads[index], firsts[index], seconds[index], rates[index], factor) for index in range(5)]
    input_grad = jnp.stack([input_query, input_passage])
    return (outputs.astype(jnp.bfloat16), input_grad, results[0][0], results[1][0], results[2][0], results[3][0], results[4][0], results[0][1], results[1][1], results[2][1], results[3][1], results[4][1], results[0][2], results[1][2], results[2][2], results[3][2], results[4][2], grad_square)
```

```python
from functools import partial

import jax
import jax.numpy as jnp
from jax import lax
from jax.sharding import PartitionSpec as P

D = 768
FF = 3072
H = 12
HD = 64
L = 512
SEGS = 8
MB = 2
STEP = 5
HG = 3
PIECES = 16
PIECE_ROWS = D // PIECES

norm_eps = 1e-05
attention_scale = 0.125
score_scale = 0.0625
contrast_weight = 16.0
clip_norm = 1.0
beta_first = 0.9
beta_second = 0.999
adam_eps = 1e-08
weight_decay = 0.01
matrix_rate = 0.05
vector_rate = 0.5
masked_score = -1e30

low_type = jnp.bfloat16
highest = lax.Precision.HIGHEST


def swapped(value, mask):
    pairs = [(i, i ^ mask) for i in range(lax.axis_size("dp"))]
    return lax.ppermute(value, "dp", pairs)


def tower_swapped(value):
    return lax.ppermute(value, "tower", [(0, 1), (1, 0)])


def relative_of(place):
    return ((place & 3) << 2) | (((place >> 2) & 1) << 1) | (place >> 3)


def place_of(relative):
    return ((relative & 1) << 3) | (((relative >> 1) & 1) << 2) | (relative >> 2)


def gather_pieces(own):
    four = jnp.stack([own, swapped(own, 4), swapped(own, 8), swapped(own, 12)])
    eight = jnp.concatenate([four, swapped(four, 2)])
    return jnp.concatenate([eight, swapped(eight, 1)])


def scatter_pieces(pieces):
    eight = added(pieces[:8], swapped(pieces[8:], 1)).astype(low_type)
    four = added(eight[:4], swapped(eight[4:], 2)).astype(low_type)
    total = added(four[0], swapped(four[1], 4))
    total = total + swapped(four[2], 8).astype(jnp.float32)
    return total + swapped(four[3], 12).astype(jnp.float32)


def added(first, second):
    return first.astype(jnp.float32) + second.astype(jnp.float32)


def plain_dot(first_op, second_op):
    return jnp.dot(first_op, second_op, preferred_element_type=jnp.float32)


def contract_rows(first_op, second_op):
    return lax.dot_general(
        first_op, second_op, (((0,), (0,)), ((), ())), preferred_element_type=jnp.float32
    )


def contract_cols(first_op, second_op):
    return lax.dot_general(
        first_op, second_op, (((1,), (1,)), ((), ())), preferred_element_type=jnp.float32
    )


def layer_stats(values):
    centred = values - jnp.mean(values, axis=-1, keepdims=True)
    inverse = lax.rsqrt(jnp.mean(centred * centred, axis=-1, keepdims=True) + norm_eps)
    return (centred * inverse, inverse)


def norm_back(upstream, normed, inverse, gain_row):
    gained = upstream * gain_row
    return inverse * (
        gained
        - jnp.mean(gained, axis=-1, keepdims=True)
        - normed * jnp.mean(gained * normed, axis=-1, keepdims=True)
    )


def cls_table(seg_row):
    starts = jnp.sum(
        (seg_row[None, :] < jnp.arange(SEGS, dtype=jnp.int32)[:, None]).astype(jnp.int32), axis=1
    )
    return (jnp.arange(L, dtype=jnp.int32)[None, :] == starts[:, None]).astype(jnp.float32)


def attention_scores(queries, key_rows, seg_rows):
    scores = (
        jnp.einsum("bqhd,bkhd->bhqk", queries, key_rows, preferred_element_type=jnp.float32)
        * attention_scale
    )
    same_doc = seg_rows[:, :, None] == seg_rows[:, None, :]
    return jnp.where(same_doc[:, None], scores, masked_score)


def by_heads(matrix):
    shaped = matrix.reshape(matrix.shape[0], 3, HG, D // HG)
    return jnp.transpose(shaped, (2, 0, 1, 3)).reshape(HG, matrix.shape[0], D)


def from_heads(blocks):
    rows = blocks.shape[1]
    shaped = blocks.reshape(HG, rows, 3, D // HG)
    return jnp.transpose(shaped, (1, 2, 0, 3)).reshape(rows, 3 * D)


def by_columns(matrix):
    return jnp.transpose(matrix.reshape(matrix.shape[0], 4, D), (1, 0, 2))


def from_columns(blocks):
    return jnp.transpose(blocks, (1, 0, 2)).reshape(blocks.shape[1], 4 * D)


def adam_update(master, grad_share, first, second, rate, factor):
    clipped = grad_share * factor
    first_new = beta_first * first + (1.0 - beta_first) * clipped
    second_new = beta_second * second + (1.0 - beta_second) * clipped * clipped
    first_hat = first_new / (1.0 - beta_first**STEP)
    second_hat = second_new / (1.0 - beta_second**STEP)
    master_new = master - rate * (
        first_hat / (jnp.sqrt(second_hat) + adam_eps) + weight_decay * master
    )
    return (master_new[None], first_new[None], second_new[None])


def body(
    tokens,
    segments,
    positives,
    token_grad,
    mix_weight,
    out_weight,
    up_weight,
    down_weight,
    vectors,
    first_mix,
    first_out,
    first_up,
    first_down,
    first_vectors,
    second_mix,
    second_out,
    second_up,
    second_down,
    second_vectors,
):
    owners = lax.axis_size("dp")
    fast = owners == PIECES
    me = lax.axis_index("dp")
    is_passage = lax.axis_index("tower") == 1
    masters = (mix_weight[0], out_weight[0], up_weight[0], down_weight[0], vectors[0])
    low_mix, low_out, low_up, low_down, low_vec = (m.astype(low_type) for m in masters)
    share = low_vec.shape[1]
    queries_all = owners * SEGS

    if fast:
        extra = jnp.zeros((16, D), low_type)
        extra = extra.at[12:14, :SEGS].set(positives.astype(low_type))
        extra = lax.dynamic_update_slice(extra, low_vec, (0, me * share))
        pack_mix = jnp.concatenate([by_heads(low_mix).reshape(-1, D), extra])
        got_mix = gather_pieces(pack_mix)
        got_up = gather_pieces(jnp.concatenate([low_out, by_columns(low_up).reshape(-1, D)]))
        got_down = gather_pieces(low_down)
        places = place_of(jnp.arange(PIECES, dtype=jnp.int32) ^ me)
        vec_f = jnp.sum(got_mix[:, 144:156].astype(jnp.float32), axis=0)
        cls_positives = got_mix[:, 156:158, :SEGS].astype(jnp.int32)
        cls_positives = jnp.transpose(cls_positives, (1, 0, 2)).reshape(MB, queries_all)
        got_mix, got_up, got_down = (jnp.take(g, places, axis=0) for g in (got_mix, got_up, got_down))
        mix_w = from_heads(
            jnp.transpose(got_mix[:, :144].reshape(PIECES, HG, PIECE_ROWS, D), (1, 0, 2, 3)).reshape(
                HG, D, D
            )
        )
        out_w = got_up[:, :48].reshape(D, D)
        up_w = from_columns(
            jnp.transpose(got_up[:, 48:].reshape(PIECES, 4, PIECE_ROWS, D), (1, 0, 2, 3)).reshape(
                4, D, D
            )
        )
        down_w = got_down.reshape(FF, D)
        relative = relative_of(jnp.arange(PIECES, dtype=jnp.int32))
        cls_ids = ((relative ^ me)[:, None] * SEGS + jnp.arange(SEGS)[None, :]).reshape(-1)
    else:
        mix_w = lax.all_gather(low_mix, "dp", axis=0, tiled=True)
        out_w = lax.all_gather(low_out, "dp", axis=0, tiled=True)
        up_w = lax.all_gather(low_up, "dp", axis=0, tiled=True)
        down_w = lax.all_gather(low_down, "dp", axis=0, tiled=True)
        vec_f = lax.all_gather(low_vec, "dp", axis=1, tiled=True).astype(jnp.float32)
        cls_positives = jnp.roll(
            lax.all_gather(positives, "dp", axis=1, tiled=True), -me * SEGS, axis=1
        )
        cls_ids = jnp.roll(jnp.arange(queries_all, dtype=jnp.int32), -me * SEGS)

    x_low = tokens[0].reshape(MB * L, D)
    x_f = x_low.astype(jnp.float32)
    seg_rows = segments[0].reshape(MB, L)
    mixed_bias = jnp.concatenate([vec_f[0], jnp.zeros_like(vec_f[0]), vec_f[1]])
    mixed_low = (plain_dot(x_low, mix_w) + mixed_bias).astype(low_type)
    shaped = mixed_low.reshape(MB, L, 3, H, HD)
    queries, key_rows, value_rows = shaped[:, :, 0], shaped[:, :, 1], shaped[:, :, 2]
    scores = attention_scores(queries, key_rows, seg_rows)
    largest = jnp.max(scores, axis=-1, keepdims=True)
    expo = jnp.exp(scores - largest)
    summed = jnp.sum(expo, axis=-1, keepdims=True)
    probs = expo / summed
    log_total = (largest + jnp.log(summed))[..., 0]
    context = jnp.einsum(
        "bhqk,bkhd->bqhd", probs.astype(low_type), value_rows, preferred_element_type=jnp.float32
    )
    context_low = context.reshape(MB * L, D).astype(low_type)
    branch = plain_dot(context_low, out_w) + vec_f[2]
    normed_one, inverse_one = layer_stats(x_f + branch)
    hidden = normed_one * vec_f[3] + vec_f[4]
    hidden_low = hidden.astype(low_type)
    pre_act = plain_dot(hidden_low, up_w) + vec_f[5:9].reshape(FF)
    active_low = jax.nn.gelu(pre_act, approximate=False).astype(low_type)
    ffn_out = plain_dot(active_low, down_w) + vec_f[9]
    normed_two, inverse_two = layer_stats(hidden + ffn_out)
    output = normed_two * vec_f[10] + vec_f[11]

    tables = jax.vmap(cls_table)(seg_rows)
    pooled = jnp.einsum("rsl,rld->rsd", tables, output.reshape(MB, L, D), precision=highest)
    pooled_low = pooled.astype(low_type).reshape(MB * SEGS, D)
    both = jnp.concatenate([pooled_low, tower_swapped(pooled_low)])
    if fast:
        everyone = gather_pieces(both)
    else:
        everyone = lax.all_gather(both, "dp", axis=0, tiled=False)
        everyone = jnp.roll(everyone, -me, axis=0)
    everyone = jnp.transpose(everyone.reshape(owners, 2, MB, SEGS, D), (1, 2, 0, 3, 4))
    everyone = everyone.reshape(2, MB, queries_all, D)
    cls_query = jnp.where(is_passage, everyone[1], everyone[0])
    cls_passage = jnp.where(is_passage, everyone[0], everyone[1])
    contrast = (
        jnp.einsum("mqd,mpd->mqp", cls_query, cls_passage, preferred_element_type=jnp.float32)
        * score_scale
    )
    top = jnp.max(contrast, axis=-1, keepdims=True)
    cexpo = jnp.exp(contrast - top)
    cprobs = cexpo / jnp.sum(cexpo, axis=-1, keepdims=True)
    chosen = (cls_ids[None, None, :] == cls_positives[:, :, None]).astype(jnp.float32)
    grad_contrast = (contrast_weight * (cprobs - chosen)).astype(low_type)
    mine = jnp.where(
        is_passage, jnp.transpose(grad_contrast[:, :, :SEGS], (0, 2, 1)), grad_contrast[:, :SEGS]
    )
    theirs = jnp.where(is_passage, cls_query, cls_passage)
    grad_cls = (
        jnp.einsum("msq,mqd->msd", mine, theirs, preferred_element_type=jnp.float32) * score_scale
    )
    grad_cls = jnp.where(is_passage, grad_cls, grad_cls.astype(low_type).astype(jnp.float32))
    upstream = token_grad[0].reshape(MB, L, D) + jnp.einsum(
        "rsl,rsd->rld", tables, grad_cls, precision=highest
    )
    upstream = upstream.reshape(MB * L, D)

    def spread(blocks):
        order = relative_of(jnp.arange(PIECES, dtype=jnp.int32)) ^ me
        k = blocks.shape[0]
        shaped = jnp.transpose(blocks.reshape(k, PIECES, PIECE_ROWS, D), (1, 0, 2, 3))
        return jnp.take(shaped.reshape(PIECES, k * PIECE_ROWS, D), order, axis=0)

    gain_two = jnp.sum(upstream * normed_two, axis=0)
    shift_two = jnp.sum(upstream, axis=0)
    grad_pre_two = norm_back(upstream, normed_two, inverse_two, vec_f[10])
    grad_ffn_low = grad_pre_two.astype(low_type)
    bias_down = jnp.sum(grad_ffn_low.astype(jnp.float32), axis=0)
    grad_down = contract_rows(active_low, grad_ffn_low)
    if fast:
        order = relative_of(jnp.arange(PIECES, dtype=jnp.int32)) ^ me
        share_down = scatter_pieces(
            jnp.take(grad_down.astype(low_type).reshape(PIECES, -1, D), order, axis=0)
        )
    else:
        share_down = lax.psum_scatter(grad_down, "dp", scatter_dimension=0, tiled=True)
    grad_active = contract_cols(grad_ffn_low, down_w)
    gelu_pull = jax.vjp(partial(jax.nn.gelu, approximate=False), pre_act)[1]
    grad_pre_low = gelu_pull(grad_active)[0].astype(low_type)
    bias_up = jnp.sum(grad_pre_low.astype(jnp.float32), axis=0)
    grad_up = contract_rows(hidden_low, grad_pre_low)
    if fast:
        share_up = scatter_pieces(spread(by_columns(grad_up.astype(low_type))))
        share_up = from_columns(share_up.reshape(4, PIECE_ROWS, D))
    else:
        share_up = lax.psum_scatter(grad_up, "dp", scatter_dimension=0, tiled=True)
    grad_hidden = grad_pre_two + contract_cols(grad_pre_low, up_w)
    gain_one = jnp.sum(grad_hidden * normed_one, axis=0)
    shift_one = jnp.sum(grad_hidden, axis=0)
    grad_pre_one = norm_back(grad_hidden, normed_one, inverse_one, vec_f[3])
    grad_branch_low = grad_pre_one.astype(low_type)
    bias_out = jnp.sum(grad_branch_low.astype(jnp.float32), axis=0)
    grad_out = contract_rows(context_low, grad_branch_low)
    grad_context = contract_cols(grad_branch_low, out_w).astype(low_type).reshape(MB, L, H, HD)
    scores = attention_scores(queries, key_rows, seg_rows)
    probs = jnp.exp(scores - log_total[..., None])
    grad_values = jnp.einsum(
        "bhqk,bqhd->bkhd",
        probs.astype(low_type),
        grad_context,
        preferred_element_type=jnp.float32,
    )
    grad_probs = jnp.einsum(
        "bqhd,bkhd->bhqk", grad_context, value_rows, preferred_element_type=jnp.float32
    )
    grad_scores = probs * (grad_probs - jnp.sum(probs * grad_probs, axis=-1, keepdims=True))
    grad_scores_low = grad_scores.astype(low_type)
    grad_queries = (
        jnp.einsum("bhqk,bkhd->bqhd", grad_scores_low, key_rows, preferred_element_type=jnp.float32)
        * attention_scale
    )
    grad_keys = (
        jnp.einsum("bhqk,bqhd->bkhd", grad_scores_low, queries, preferred_element_type=jnp.float32)
        * attention_scale
    )
    grad_mixed_low = (
        jnp.stack([grad_queries, grad_keys, grad_values], axis=2)
        .reshape(MB * L, 3 * D)
        .astype(low_type)
    )
    bias_mixed = jnp.sum(grad_mixed_low.astype(jnp.float32), axis=0)
    grad_mix = contract_rows(x_low, grad_mixed_low)
    input_grad = grad_pre_one + contract_cols(grad_mixed_low, mix_w)
    grad_vec = jnp.concatenate(
        [
            bias_mixed[None, :D],
            bias_mixed[None, 2 * D :],
            bias_out[None],
            gain_one[None],
            shift_one[None],
            bias_up.reshape(4, D),
            bias_down[None],
            gain_two[None],
            shift_two[None],
        ],
        axis=0,
    )
    if fast:
        vec_rows = jnp.broadcast_to(
            jnp.pad(grad_vec, ((0, 4), (0, 0))).astype(low_type)[None], (PIECES, 16, D)
        )
        pieces = jnp.concatenate(
            [
                spread(grad_out.astype(low_type)[None]),
                spread(by_heads(grad_mix.astype(low_type))),
                vec_rows,
            ],
            axis=1,
        )
        share_rest = scatter_pieces(pieces)
        share_out = share_rest[:48]
        share_mix = from_heads(share_rest[48:192].reshape(HG, PIECE_ROWS, D))
        share_vec = lax.dynamic_slice(share_rest[192:204], (0, me * share), (12, share))
    else:
        share_mix = lax.psum_scatter(grad_mix, "dp", scatter_dimension=0, tiled=True)
        share_out = lax.psum_scatter(grad_out, "dp", scatter_dimension=0, tiled=True)
        share_vec = lax.psum_scatter(grad_vec, "dp", scatter_dimension=1, tiled=True)

    shares = (share_mix, share_out, share_up, share_down, share_vec)
    local_square = sum(jnp.sum(s * s) for s in shares)
    if fast:
        grad_square = jnp.broadcast_to(local_square, (8, 128))
        for mask in (1, 2, 4, 8):
            grad_square = grad_square + swapped(grad_square, mask)
        grad_square = grad_square + tower_swapped(grad_square)
        grad_square = grad_square[0, 0]
    else:
        grad_square = lax.psum(local_square, ("tower", "dp"))
    factor = jnp.minimum(1.0, clip_norm / (jnp.sqrt(grad_square) + 1e-06))
    firsts = (first_mix[0], first_out[0], first_up[0], first_down[0], first_vectors[0])
    seconds = (second_mix[0], second_out[0], second_up[0], second_down[0], second_vectors[0])
    rates = (matrix_rate, matrix_rate, matrix_rate, matrix_rate, vector_rate)
    results = [
        adam_update(masters[i], shares[i], firsts[i], seconds[i], rates[i], factor)
        for i in range(5)
    ]
    layer_output = output.astype(low_type).reshape(1, MB, 1, L, D)
    return (
        layer_output,
        input_grad.reshape(1, MB, 1, L, D),
        *(r[0] for r in results),
        *(r[1] for r in results),
        *(r[2] for r in results),
        grad_square,
    )


def solution(mesh):
    rows = P("tower", None, "dp", None, None)
    shards = (P("tower", "dp", None),) * 4 + (P("tower", None, "dp"),)
    in_specs = (rows, P("tower", None, "dp", None), P(None, "dp"), rows) + shards * 3
    out_specs = (rows, rows) + shards * 3 + (P(),)
    return jax.shard_map(body, mesh=mesh, in_specs=in_specs, out_specs=out_specs, check_vma=False)
```

```python
from functools import partial

import jax
import jax.numpy as jnp
from jax import lax
from jax.experimental import pallas as pl
from jax.experimental.pallas import tpu as pltpu
from jax.sharding import PartitionSpec as P

D = 768
FF = 3072
H = 12
HD = 64
L = 512
SEGS = 8
MB = 2
STEP = 5
HG = 3
PIECES = 16
PIECE_ROWS = D // PIECES

norm_eps = 1e-05
attention_scale = 0.125
score_scale = 0.0625
contrast_weight = 16.0
clip_norm = 1.0
beta_first = 0.9
beta_second = 0.999
adam_eps = 1e-08
weight_decay = 0.01
matrix_rate = 0.05
vector_rate = 0.5
masked_score = -1e30

low_type = jnp.bfloat16
highest = lax.Precision.HIGHEST


def swapped(value, mask):
    pairs = [(i, i ^ mask) for i in range(lax.axis_size("dp"))]
    return lax.ppermute(value, "dp", pairs)


def tower_swapped(value):
    return lax.ppermute(value, "tower", [(0, 1), (1, 0)])


def relative_of(place):
    return ((place & 1) << 3) | ((place & 2) << 1) | ((place & 4) >> 1) | (place >> 3)


def gather_pieces(own):
    pieces = own[None]
    for mask in (8, 4, 2, 1):
        pieces = jnp.concatenate([pieces, swapped(pieces, mask)])
    return pieces


def added(first, second):
    return first.astype(jnp.float32) + second.astype(jnp.float32)


def rows_dot(first_op, second_op):
    return jnp.dot(first_op, second_op, preferred_element_type=jnp.float32)


def contract_rows(first_op, second_op):
    return lax.dot_general(
        first_op, second_op, (((0,), (0,)), ((), ())), preferred_element_type=jnp.float32
    )


def contract_cols(first_op, second_op):
    return lax.dot_general(
        first_op, second_op, (((1,), (1,)), ((), ())), preferred_element_type=jnp.float32
    )


def layer_stats(values):
    centred = values - jnp.mean(values, axis=-1, keepdims=True)
    inverse = lax.rsqrt(jnp.mean(centred * centred, axis=-1, keepdims=True) + norm_eps)
    return (centred * inverse, inverse)


def norm_back(upstream, normed, inverse, gain_row):
    gained = upstream * gain_row
    return inverse * (
        gained
        - jnp.mean(gained, axis=-1, keepdims=True)
        - normed * jnp.mean(gained * normed, axis=-1, keepdims=True)
    )


def column_sum(values):
    return jnp.sum(values.astype(jnp.float32), axis=0, keepdims=True)


def gelu_parts(pre):
    size = jnp.abs(pre) * 0.7071067811865476
    inner = 1.0 / (1.0 + 0.3275911 * size)
    series = 1.061405429 * inner - 1.453152027
    series = series * inner + 1.421413741
    series = series * inner - 0.284496736
    series = (series * inner + 0.254829592) * inner
    bell = jnp.exp(-size * size)
    half_tail = 0.5 * series * bell
    cumulative = jnp.where(pre >= 0.0, 1.0 - half_tail, half_tail)
    return (pre * cumulative, cumulative + pre * (bell * 0.3989422804014327))


ROWS = MB * L
QCOLS = D // HG
HEADS = H // HG
log2e = 1.4426950408889634
any_space = pl.BlockSpec(memory_space=pl.ANY)
scalar_space = pl.BlockSpec(memory_space=pltpu.SMEM)
vmem_space = pl.BlockSpec(memory_space=pltpu.VMEM)


def params(megabytes):
    return pltpu.CompilerParams(vmem_limit_bytes=megabytes * 1024 * 1024)


def cost(flops, moved, exps=0):
    return pl.CostEstimate(flops=int(flops), bytes_accessed=int(moved), transcendentals=int(exps))


def start_pieces(me, near, far, row, count, target, sem):
    for place in range(PIECES):
        held = near if place < 8 else far
        at = pl.multiple_of((me ^ relative_of(place)) * count, 16)
        pltpu.make_async_copy(
            held.at[place % 8, pl.ds(row, count), :], target.at[pl.ds(at, count), :], sem
        ).start()


def start_owners(me, source, count, keep, send, row, sem):
    for place in range(PIECES):
        held = keep if place < 8 else send
        at = pl.multiple_of((me ^ relative_of(place)) * count, 16)
        pltpu.make_async_copy(
            source.at[pl.ds(at, count), :], held.at[place % 8, pl.ds(row, count), :], sem
        ).start()


def wait_bytes(whole, sem):
    pltpu.make_async_copy(whole, whole, sem).wait()


def attention_kernel(
    me_ref, near, far, x_ref, seg_col, seg_row, bias_ref, mixed_ref, ctx_ref, lse_ref, w, mask, sems
):
    hg, mb = pl.program_id(0), pl.program_id(1)
    me = me_ref[0]

    @pl.when((hg == 0) & (mb == 0))
    def _():
        for block in range(HG):
            start_pieces(
                me, near, far, block * PIECE_ROWS, PIECE_ROWS, w.at[block], sems.at[block]
            )

    @pl.when(hg == 0)
    def _():
        same = seg_col[...] == seg_row[...].reshape(1, L)
        mask[mb] = jnp.where(same, 0.0, masked_score)

    for block in range(HG):

        @pl.when((hg == block) & (mb == 0))
        def _():
            wait_bytes(w.at[block], sems.at[block])

    mixed = (rows_dot(x_ref[...], w[hg]) + bias_ref[...].reshape(1, D)).astype(low_type)
    mixed_ref[...] = mixed.reshape(mixed_ref.shape)
    outs, totals = [], []
    for head in range(HEADS):
        q = mixed[:, head * HD : (head + 1) * HD]
        k = mixed[:, QCOLS + head * HD : QCOLS + (head + 1) * HD]
        v = mixed[:, 2 * QCOLS + head * HD : 2 * QCOLS + (head + 1) * HD]
        parts, logs = [], []
        for first in range(0, L, 256):
            scores = contract_cols(q[first : first + 256], k) * (attention_scale * log2e)
            scores = scores + mask[mb, first : first + 256, :]
            largest = jnp.max(scores, axis=-1, keepdims=True)
            expo = jnp.exp2(scores - largest)
            summed = jnp.sum(expo, axis=-1, keepdims=True)
            probs = (expo * (1.0 / summed)).astype(low_type)
            parts.append(rows_dot(probs, v))
            logs.append(largest + jnp.log(summed) * log2e)
        outs.append(jnp.concatenate(parts, axis=0))
        totals.append(jnp.concatenate(logs, axis=0))
    ctx_ref[...] = jnp.concatenate(outs, axis=1).astype(low_type)
    lse_ref[...] = jnp.concatenate(totals, axis=1).reshape(lse_ref.shape)


def attention_forward(me, near, far, x_low, seg_col, seg_row, mixed_bias):
    count = near.shape[1]
    return pl.pallas_call(
        attention_kernel,
        grid=(HG, MB),
        in_specs=[
            scalar_space,
            any_space,
            any_space,
            pl.BlockSpec((L, D), lambda g, m: (m, 0)),
            pl.BlockSpec((L, 1), lambda g, m: (m, 0)),
            pl.BlockSpec((1, 1, L), lambda g, m: (m, 0, 0)),
            pl.BlockSpec((1, 1, D), lambda g, m: (g, 0, 0)),
        ],
        out_specs=[
            pl.BlockSpec((1, L, D), lambda g, m: (g, m, 0)),
            pl.BlockSpec((L, QCOLS), lambda g, m: (m, g)),
            pl.BlockSpec((1, L, HEADS), lambda g, m: (g * MB + m, 0, 0)),
        ],
        out_shape=[
            jax.ShapeDtypeStruct((HG, ROWS, D), low_type),
            jax.ShapeDtypeStruct((ROWS, D), low_type),
            jax.ShapeDtypeStruct((HG * MB, L, HEADS), jnp.float32),
        ],
        scratch_shapes=[
            pltpu.VMEM((HG, D, D), low_type),
            pltpu.VMEM((MB, L, L), jnp.float32),
            pltpu.SemaphoreType.DMA((HG,)),
        ],
        compiler_params=params(40),
        cost_estimate=cost(2 * ROWS * D * 3 * D + 8 * MB * H * L * L * HD, 12e6, MB * H * L * L),
        name="mixed_attention",
    )(me, near, far, x_low, seg_col, seg_row, mixed_bias)


def up_kernel(
    me_ref,
    near,
    far,
    ctx_hbm,
    x_hbm,
    vec,
    normed_hbm,
    inverse_ref,
    hidden_hbm,
    active_ref,
    slope_ref,
    out_w,
    up_w,
    ctx,
    x,
    normed,
    hidden,
    sems,
):
    step = pl.program_id(0)
    me = me_ref[0]
    ctx_in = pltpu.make_async_copy(ctx_hbm, ctx, sems.at[5])
    x_in = pltpu.make_async_copy(x_hbm, x, sems.at[6])
    normed_out = pltpu.make_async_copy(normed, normed_hbm, sems.at[7])
    hidden_out = pltpu.make_async_copy(hidden, hidden_hbm, sems.at[8])

    @pl.when(step == 0)
    def _():
        start_pieces(me, near, far, 0, PIECE_ROWS, out_w, sems.at[4])
        ctx_in.start()
        x_in.start()
        for block in range(4):
            start_pieces(
                me,
                near,
                far,
                (1 + block) * PIECE_ROWS,
                PIECE_ROWS,
                up_w.at[block],
                sems.at[block],
            )
        wait_bytes(out_w, sems.at[4])
        ctx_in.wait()
        x_in.wait()
        for first in range(0, ROWS, 256):
            part = slice(first, first + 256)
            branch = rows_dot(ctx[part, :], out_w[...]) + vec[2:3, :]
            n, inv = layer_stats(x[part, :].astype(jnp.float32) + branch)
            normed[part, :] = n
            inverse_ref[part, :] = inv
            hidden[part, :] = (n * vec[3:4, :] + vec[4:5, :]).astype(low_type)
        normed_out.start()
        hidden_out.start()

    for block in range(4):

        @pl.when(step == block)
        def _():
            wait_bytes(up_w.at[block], sems.at[block])

    bias = vec[pl.ds(5 + step, 1), :]
    for first in range(0, ROWS, 256):
        part = slice(first, first + 256)
        pre = rows_dot(hidden[part, :], up_w[step]) + bias
        active, slope = gelu_parts(pre)
        active_ref[part, :] = active.astype(low_type)
        slope_ref[part, :] = slope.astype(low_type)

    @pl.when(step == 3)
    def _():
        normed_out.wait()
        hidden_out.wait()


def up_forward(me, near, far, context, x_low, vec):
    return pl.pallas_call(
        up_kernel,
        grid=(4,),
        in_specs=[scalar_space, any_space, any_space, any_space, any_space, vmem_space],
        out_specs=[
            any_space,
            pl.BlockSpec((ROWS, 1), lambda s: (0, 0)),
            any_space,
            pl.BlockSpec((ROWS, D), lambda s: (0, s)),
            pl.BlockSpec((ROWS, D), lambda s: (0, s)),
        ],
        out_shape=[
            jax.ShapeDtypeStruct((ROWS, D), jnp.float32),
            jax.ShapeDtypeStruct((ROWS, 1), jnp.float32),
            jax.ShapeDtypeStruct((ROWS, D), low_type),
            jax.ShapeDtypeStruct((ROWS, FF), low_type),
            jax.ShapeDtypeStruct((ROWS, FF), low_type),
        ],
        scratch_shapes=[
            pltpu.VMEM((D, D), low_type),
            pltpu.VMEM((4, D, D), low_type),
            pltpu.VMEM((ROWS, D), low_type),
            pltpu.VMEM((ROWS, D), low_type),
            pltpu.VMEM((ROWS, D), jnp.float32),
            pltpu.VMEM((ROWS, D), low_type),
            pltpu.SemaphoreType.DMA((9,)),
        ],
        compiler_params=params(44),
        cost_estimate=cost(2 * ROWS * D * (FF + D), 24e6, 2 * ROWS * FF),
        name="out_up",
    )(me, near, far, context, x_low, vec)


def down_kernel(
    me_ref,
    near,
    far,
    active_hbm,
    normed_one_ref,
    vec,
    table_ref,
    normed_ref,
    inverse_ref,
    output_ref,
    cls_ref,
    w,
    active,
    sems,
):
    me = me_ref[0]
    start_pieces(me, near, far, 0, 4 * PIECE_ROWS, w, sems.at[0])
    copies = []
    for index in range(4):
        part = pl.ds(index * 256, 256)
        copies.append(
            pltpu.make_async_copy(active_hbm.at[part, :], active.at[part, :], sems.at[1 + index])
        )
        copies[-1].start()
    wait_bytes(w, sems.at[0])
    for index in range(4):
        copies[index].wait()
        part = slice(index * 256, (index + 1) * 256)
        ffn = rows_dot(active[part, :], w[...]) + vec[9:10, :]
        residual = normed_one_ref[part, :] * vec[3:4, :] + vec[4:5, :]
        n, inv = layer_stats(residual + ffn)
        normed_ref[part, :] = n
        inverse_ref[part, :] = inv
        output_ref[part, :] = (n * vec[10:11, :] + vec[11:12, :]).astype(low_type)
    cls_ref[...] = rows_dot(table_ref[...], output_ref[...]).astype(low_type)


def down_forward(me, near, far, active, normed_one, vec, table):
    return pl.pallas_call(
        down_kernel,
        in_specs=[scalar_space, any_space, any_space, any_space, vmem_space, vmem_space, vmem_space],
        out_specs=[vmem_space] * 4,
        out_shape=[
            jax.ShapeDtypeStruct((ROWS, D), jnp.float32),
            jax.ShapeDtypeStruct((ROWS, 1), jnp.float32),
            jax.ShapeDtypeStruct((ROWS, D), low_type),
            jax.ShapeDtypeStruct((MB * SEGS, D), low_type),
        ],
        scratch_shapes=[
            pltpu.VMEM((FF, D), low_type),
            pltpu.VMEM((ROWS, FF), low_type),
            pltpu.SemaphoreType.DMA((5,)),
        ],
        compiler_params=params(40),
        cost_estimate=cost(2 * ROWS * D * FF, 19e6),
        name="down",
    )(me, near, far, active, normed_one, vec, table)


def contrast_kernel(flag_ref, all_ref, positive_ref, ids_ref, grad_ref):
    passage_here = flag_ref[0] == 1
    for batch in range(MB):
        mine, theirs = all_ref[0, batch], all_ref[1, batch]
        queries = jnp.where(passage_here, theirs, mine)
        passages = jnp.where(passage_here, mine, theirs)
        contrast = contract_cols(queries, passages) * score_scale
        top = jnp.max(contrast, axis=-1, keepdims=True)
        expo = jnp.exp(contrast - top)
        probs = expo / jnp.sum(expo, axis=-1, keepdims=True)
        chosen = (positive_ref[batch] == ids_ref[...]).astype(jnp.float32)
        grad = (contrast_weight * (probs - chosen)).astype(low_type)
        for_query = rows_dot(grad[:16], passages) * score_scale
        for_query = for_query.astype(low_type).astype(jnp.float32)
        for_passage = contract_rows(grad, queries)[:16] * score_scale
        taken = jnp.where(passage_here, for_passage, for_query)
        grad_ref[batch * SEGS : (batch + 1) * SEGS, :] = taken[:SEGS]


def contrast_back(flag, everyone, cls_positives, cls_ids):
    return pl.pallas_call(
        contrast_kernel,
        in_specs=[scalar_space, vmem_space, vmem_space, vmem_space],
        out_specs=vmem_space,
        out_shape=jax.ShapeDtypeStruct((MB * SEGS, D), jnp.float32),
        compiler_params=params(48),
        name="contrast",
    )(flag, everyone, cls_positives, cls_ids)


def down_back_kernel(
    me_ref,
    token_grad,
    grad_cls,
    table3_ref,
    normed_ref,
    inverse_ref,
    vec,
    active_ref,
    residual_ref,
    low_ref,
    sums_ref,
    keep,
    send,
    low,
    staged,
    sem,
):
    step = pl.program_id(0)

    @pl.when(step == 0)
    def _():
        grads = grad_cls[...]
        upper = grads.astype(low_type)
        rest = grads - upper.astype(jnp.float32)
        middle = rest.astype(low_type)
        lower = (rest - middle.astype(jnp.float32)).astype(low_type)
        stacked = jnp.concatenate([upper, middle, lower], axis=0)
        gains = jnp.zeros((1, D), jnp.float32)
        shifts = jnp.zeros((1, D), jnp.float32)
        biases = jnp.zeros((1, D), jnp.float32)
        for first in range(0, ROWS, 256):
            part = slice(first, first + 256)
            upstream = token_grad[part, :] + contract_rows(table3_ref[:, part], stacked)
            n = normed_ref[part, :]
            gains = gains + column_sum(upstream * n)
            shifts = shifts + column_sum(upstream)
            grad = norm_back(upstream, n, inverse_ref[part, :], vec[10:11, :])
            residual_ref[part, :] = grad
            rounded = grad.astype(low_type)
            biases = biases + column_sum(rounded)
            low[part, :] = rounded
        low_ref[...] = low[...]
        sums_ref[...] = jnp.concatenate([biases, gains, shifts, jnp.zeros((5, D), jnp.float32)])

    at = pl.multiple_of(step * D, D)
    for first in range(0, D, 256):
        staged[pl.ds(at + first, 256), :] = contract_rows(
            active_ref[:, first : first + 256], low[...]
        ).astype(low_type)

    @pl.when(step == 3)
    def _():
        start_owners(me_ref[0], staged, 4 * PIECE_ROWS, keep, send, 0, sem)
        wait_bytes(staged, sem)


def down_back(me, token_grad, grad_cls, table3, normed, inverse, vec, active):
    half = jax.ShapeDtypeStruct((8, 4 * PIECE_ROWS, D), low_type)
    return pl.pallas_call(
        down_back_kernel,
        grid=(4,),
        in_specs=[scalar_space]
        + [vmem_space] * 6
        + [pl.BlockSpec((ROWS, D), lambda s: (0, s))],
        out_specs=[vmem_space] * 3 + [any_space] * 2,
        out_shape=[
            jax.ShapeDtypeStruct((ROWS, D), jnp.float32),
            jax.ShapeDtypeStruct((ROWS, D), low_type),
            jax.ShapeDtypeStruct((8, D), jnp.float32),
            half,
            half,
        ],
        scratch_shapes=[
            pltpu.VMEM((ROWS, D), low_type),
            pltpu.VMEM((FF, D), low_type),
            pltpu.SemaphoreType.DMA,
        ],
        compiler_params=params(48),
        cost_estimate=cost(2 * ROWS * D * FF, 25e6),
        name="down_back",
    )(me, token_grad, grad_cls, table3, normed, inverse, vec, active)


def up_back_kernel(
    me_ref,
    near_up,
    far_up,
    near_down,
    far_down,
    low_ref,
    slope_ref,
    hidden_ref,
    residual_hbm,
    normed_hbm,
    inverse_ref,
    ctx_hbm,
    vec,
    grad_one_ref,
    grad_ctx_ref,
    sums_ref,
    keep,
    send,
    keep_out,
    send_out,
    out_w,
    up_w,
    down_w,
    residual,
    normed,
    ctx,
    total,
    staged,
    bias_sums,
    sems,
):
    step = pl.program_id(0)
    me = me_ref[0]
    residual_in = pltpu.make_async_copy(residual_hbm, residual, sems.at[6])
    normed_in = pltpu.make_async_copy(normed_hbm, normed, sems.at[7])
    ctx_in = pltpu.make_async_copy(ctx_hbm, ctx, sems.at[8])

    @pl.when(step == 0)
    def _():
        start_pieces(me, near_down, far_down, 0, 4 * PIECE_ROWS, down_w, sems.at[5])
        for block in range(4):
            start_pieces(
                me,
                near_up,
                far_up,
                (1 + block) * PIECE_ROWS,
                PIECE_ROWS,
                up_w.at[block],
                sems.at[block],
            )
        start_pieces(me, near_up, far_up, 0, PIECE_ROWS, out_w, sems.at[4])
        residual_in.start()
        normed_in.start()
        ctx_in.start()
        wait_bytes(down_w, sems.at[5])

    for block in range(4):

        @pl.when(step == block)
        def _():
            wait_bytes(up_w.at[block], sems.at[block])

    at = pl.multiple_of(step * D, D)
    grads = []
    biases = jnp.zeros((1, D), jnp.float32)
    for first in range(0, ROWS, 256):
        part = slice(first, first + 256)
        active_grad = contract_cols(low_ref[part, :], down_w[pl.ds(at, D), :])
        grad = (active_grad * slope_ref[part, :].astype(jnp.float32)).astype(low_type)
        biases = biases + column_sum(grad)
        grads.append(grad)
        back = contract_cols(grad, up_w[step])

        @pl.when(step == 0)
        def _():
            total[part, :] = back

        @pl.when(step > 0)
        def _():
            total[part, :] += back

    grad = jnp.concatenate(grads, axis=0)
    for first in range(0, D, 256):
        staged[step, first : first + 256, :] = contract_rows(
            hidden_ref[:, first : first + 256], grad
        ).astype(low_type)
    bias_sums[step] = biases
    for block in range(4):

        @pl.when(step == block)
        def _():
            start_owners(
                me,
                staged.at[block],
                PIECE_ROWS,
                keep,
                send,
                block * PIECE_ROWS,
                sems.at[9 + block],
            )

    @pl.when(step == 3)
    def _():
        residual_in.wait()
        normed_in.wait()
        ctx_in.wait()
        wait_bytes(out_w, sems.at[4])
        gains = jnp.zeros((1, D), jnp.float32)
        shifts = jnp.zeros((1, D), jnp.float32)
        out_biases = jnp.zeros((1, D), jnp.float32)
        lows = []
        for first in range(0, ROWS, 256):
            part = slice(first, first + 256)
            upstream = residual[part, :] + total[part, :]
            n = normed[part, :]
            gains = gains + column_sum(upstream * n)
            shifts = shifts + column_sum(upstream)
            grad_one = norm_back(upstream, n, inverse_ref[part, :], vec[3:4, :])
            grad_one_ref[part, :] = grad_one
            rounded = grad_one.astype(low_type)
            out_biases = out_biases + column_sum(rounded)
            grad_ctx_ref[part, :] = contract_cols(rounded, out_w[...]).astype(low_type)
            lows.append(rounded)
        sums_ref[...] = jnp.concatenate(
            [bias_sums[block] for block in range(4)]
            + [out_biases, gains, shifts, jnp.zeros((1, D), jnp.float32)]
        )
        rounded = jnp.concatenate(lows, axis=0)
        for first in range(0, D, 256):
            staged[4, first : first + 256, :] = contract_rows(
                ctx[:, first : first + 256], rounded
            ).astype(low_type)
        start_owners(me, staged.at[4], PIECE_ROWS, keep_out, send_out, 0, sems.at[13])
        for block in range(5):
            wait_bytes(staged.at[block], sems.at[9 + block])


def up_back(
    me, near_up, far_up, near_down, far_down, low, slope, hidden, residual, normed, inverse, ctx, vec
):
    half = jax.ShapeDtypeStruct((8, 4 * PIECE_ROWS, D), low_type)
    half_out = jax.ShapeDtypeStruct((8, PIECE_ROWS, D), low_type)
    return pl.pallas_call(
        up_back_kernel,
        grid=(4,),
        in_specs=[scalar_space]
        + [any_space] * 4
        + [
            vmem_space,
            pl.BlockSpec((ROWS, D), lambda s: (0, s)),
            vmem_space,
            any_space,
            any_space,
            vmem_space,
            any_space,
            vmem_space,
        ],
        out_specs=[vmem_space] * 3 + [any_space] * 4,
        out_shape=[
            jax.ShapeDtypeStruct((ROWS, D), jnp.float32),
            jax.ShapeDtypeStruct((ROWS, D), low_type),
            jax.ShapeDtypeStruct((8, D), jnp.float32),
            half,
            half,
            half_out,
            half_out,
        ],
        scratch_shapes=[
            pltpu.VMEM((D, D), low_type),
            pltpu.VMEM((4, D, D), low_type),
            pltpu.VMEM((FF, D), low_type),
            pltpu.VMEM((ROWS, D), jnp.float32),
            pltpu.VMEM((ROWS, D), jnp.float32),
            pltpu.VMEM((ROWS, D), low_type),
            pltpu.VMEM((ROWS, D), jnp.float32),
            pltpu.VMEM((5, D, D), low_type),
            pltpu.VMEM((4, 1, D), jnp.float32),
            pltpu.SemaphoreType.DMA((14,)),
        ],
        compiler_params=params(56),
        cost_estimate=cost(2 * ROWS * D * (3 * FF + 2 * D), 40e6),
        name="up_back",
    )(
        me,
        near_up,
        far_up,
        near_down,
        far_down,
        low,
        slope,
        hidden,
        residual,
        normed,
        inverse,
        ctx,
        vec,
    )


def attention_back_kernel(
    group,
    me_ref,
    near,
    far,
    x_ref,
    seg_col,
    seg_row,
    mixed_ref,
    lse_ref,
    grad_ctx_ref,
    earlier_hbm,
    input_hbm,
    sums_ref,
    keep,
    send,
    w,
    total,
    weight_grad,
    staged,
    sems,
):
    mb = pl.program_id(0)
    me = me_ref[0]
    earlier_in = pltpu.make_async_copy(earlier_hbm, total, sems.at[1])

    @pl.when(mb == 0)
    def _():
        start_pieces(me, near, far, group * PIECE_ROWS, PIECE_ROWS, w, sems.at[0])
        earlier_in.start()

    mask = jnp.where(seg_col[...] == seg_row[...].reshape(1, L), 0.0, masked_score)
    mixed = mixed_ref[...].reshape(L, D)
    lse = lse_ref[...].reshape(L, HEADS)
    grad_q, grad_k, grad_v = [], [], []
    for head in range(HEADS):
        q = mixed[:, head * HD : (head + 1) * HD]
        k = mixed[:, QCOLS + head * HD : QCOLS + (head + 1) * HD]
        v = mixed[:, 2 * QCOLS + head * HD : 2 * QCOLS + (head + 1) * HD]
        grad_o = grad_ctx_ref[:, head * HD : (head + 1) * HD]
        dq, dk, dv = [], None, None
        for first in range(0, L, 256):
            part = slice(first, first + 256)
            scores = contract_cols(q[part], k) * (attention_scale * log2e) + mask[part]
            probs = jnp.exp2(scores - lse[part, head : head + 1])
            grad_probs = contract_cols(grad_o[part], v)
            inner = jnp.sum(probs * grad_probs, axis=-1, keepdims=True)
            grad_scores = (probs * (grad_probs - inner)).astype(low_type)
            dv_part = contract_rows(probs.astype(low_type), grad_o[part])
            dk_part = contract_rows(grad_scores, q[part])
            dq.append(rows_dot(grad_scores, k) * attention_scale)
            dk = dk_part if dk is None else dk + dk_part
            dv = dv_part if dv is None else dv + dv_part
        grad_q.append(jnp.concatenate(dq, axis=0))
        grad_k.append(dk * attention_scale)
        grad_v.append(dv)
    grad_mixed = jnp.concatenate(grad_q + grad_k + grad_v, axis=1).astype(low_type)

    @pl.when(mb == 0)
    def _():
        wait_bytes(w, sems.at[0])
        earlier_in.wait()

    rows = pl.ds(pl.multiple_of(mb * L, L), L)
    total[rows, :] += contract_cols(grad_mixed, w[...])
    bias = column_sum(grad_mixed)
    terms = contract_rows(x_ref[...], grad_mixed)

    @pl.when(mb == 0)
    def _():
        weight_grad[...] = terms
        sums_ref[0:1, :] = bias

    @pl.when(mb == 1)
    def _():
        out = pltpu.make_async_copy(total, input_hbm, sems.at[1])
        out.start()
        sums_ref[0:1, :] += bias
        staged[...] = (weight_grad[...] + terms).astype(low_type)
        start_owners(me, staged, PIECE_ROWS, keep, send, 0, sems.at[2])
        wait_bytes(staged, sems.at[2])
        out.wait()


def attention_back(
    me, near, far, x_low, seg_col, seg_row, mixed, lse, grad_ctx, earlier, group
):
    half = jax.ShapeDtypeStruct((8, PIECE_ROWS, D), low_type)
    return pl.pallas_call(
        partial(attention_back_kernel, group),
        grid=(MB,),
        in_specs=[
            scalar_space,
            any_space,
            any_space,
            pl.BlockSpec((L, D), lambda m: (m, 0)),
            pl.BlockSpec((L, 1), lambda m: (m, 0)),
            pl.BlockSpec((1, 1, L), lambda m: (m, 0, 0)),
            pl.BlockSpec((1, L, D), lambda m: (group, m, 0)),
            pl.BlockSpec((1, L, HEADS), lambda m: (group * MB + m, 0, 0)),
            pl.BlockSpec((L, QCOLS), lambda m: (m, group)),
            any_space,
        ],
        out_specs=[any_space, vmem_space, any_space, any_space],
        out_shape=[
            jax.ShapeDtypeStruct((ROWS, D), jnp.float32),
            jax.ShapeDtypeStruct((8, D), jnp.float32),
            half,
            half,
        ],
        scratch_shapes=[
            pltpu.VMEM((D, D), low_type),
            pltpu.VMEM((ROWS, D), jnp.float32),
            pltpu.VMEM((D, D), jnp.float32),
            pltpu.VMEM((D, D), low_type),
            pltpu.SemaphoreType.DMA((3,)),
        ],
        compiler_params=params(40),
        cost_estimate=cost(
            4 * ROWS * D * D + 20 * MB * HEADS * L * L * HD, 12e6, MB * HEADS * L * L
        ),
        name=f"attention_back_{group}",
    )(me, near, far, x_low, seg_col, seg_row, mixed, lse, grad_ctx, earlier)


def by_heads(matrix):
    shaped = matrix.reshape(matrix.shape[0], 3, HG, D // HG)
    return jnp.transpose(shaped, (2, 0, 1, 3)).reshape(HG, matrix.shape[0], D)


def from_heads(blocks):
    rows = blocks.shape[1]
    shaped = blocks.reshape(HG, rows, 3, D // HG)
    return jnp.transpose(shaped, (1, 2, 0, 3)).reshape(rows, 3 * D)


def by_columns(matrix):
    return jnp.transpose(matrix.reshape(matrix.shape[0], 4, D), (1, 0, 2))


def from_columns(blocks):
    return jnp.transpose(blocks, (1, 0, 2)).reshape(blocks.shape[1], 4 * D)


def adam_update(master, grad_share, first, second, rate, factor):
    clipped = grad_share * factor
    first_new = beta_first * first + (1.0 - beta_first) * clipped
    second_new = beta_second * second + (1.0 - beta_second) * clipped * clipped
    first_hat = first_new / (1.0 - beta_first**STEP)
    second_hat = second_new / (1.0 - beta_second**STEP)
    master_new = master - rate * (
        first_hat / (jnp.sqrt(second_hat) + adam_eps) + weight_decay * master
    )
    return (master_new[None], first_new[None], second_new[None])


def halves(matrix_rows):
    k = matrix_rows.shape[0]
    shaped = matrix_rows.reshape(k, 2, 2, 2, 2, -1, D)
    pieces = jnp.transpose(shaped, (4, 3, 2, 1, 0, 5, 6)).reshape(PIECES, -1, D)
    return (pieces[:8], pieces[8:])


def whole_rows(keep, send, k):
    shaped = jnp.concatenate([keep, send]).reshape(2, 2, 2, 2, k, -1, D)
    return jnp.transpose(shaped, (4, 3, 2, 1, 0, 5, 6)).reshape(k, -1, D)


def beside(sends, *work):
    received = [swapped(value, mask) for value, mask in sends]
    done = lax.optimization_barrier((received, work))
    return (done[0], *done[1])


def joined(pieces, received):
    return jnp.concatenate([pieces, received])


def parted(keep, received):
    half = keep.shape[0] // 2
    return (
        added(keep[:half], received[:half]).astype(low_type),
        added(keep[half:], received[half:]).astype(low_type),
    )


def body(
    tokens,
    segments,
    positives,
    token_grad,
    mix_weight,
    out_weight,
    up_weight,
    down_weight,
    vectors,
    first_mix,
    first_out,
    first_up,
    first_down,
    first_vectors,
    second_mix,
    second_out,
    second_up,
    second_down,
    second_vectors,
):
    owners = lax.axis_size("dp")
    fast = owners == PIECES
    index = lax.axis_index("dp")
    flag = lax.axis_index("tower").astype(jnp.int32).reshape(1)
    masters = (mix_weight[0], out_weight[0], up_weight[0], down_weight[0], vectors[0])
    low_mix, low_out, low_up, low_down, low_vec = (m.astype(low_type) for m in masters)
    share = low_vec.shape[1]
    queries_all = owners * SEGS

    if fast:
        me = index.astype(jnp.int32).reshape(1)
        extra = jnp.zeros((16, D), low_type)
        extra = extra.at[12:14, :SEGS].set(positives.astype(low_type))
        extra = lax.dynamic_update_slice(extra, low_vec, (0, index * share))
        pack_mix = jnp.concatenate([by_heads(low_mix).reshape(-1, D), extra])
        pack_up = jnp.concatenate([low_out, by_columns(low_up).reshape(-1, D)])
        mix, up, down = pack_mix[None], pack_up[None], low_down[None]
        ((got_mix,),) = beside([(mix, 8)])
        mix = joined(mix, got_mix)
        ((got_mix, got_up),) = beside([(mix, 4), (up, 8)])
        mix, up = joined(mix, got_mix), joined(up, got_up)
        ((got_mix, got_up, got_down),) = beside([(mix, 2), (up, 4), (down, 8)])
        mix_near, up, down = joined(mix, got_mix), joined(up, got_up), joined(down, got_down)
        mix_far = swapped(mix_near, 1)
        extras = jnp.concatenate([mix_near[:, 144:], mix_far[:, 144:]])
        vec_f = jnp.sum(extras[:, :12].astype(jnp.float32), axis=0)
        cls_positives = jnp.transpose(extras[:, 12:14, :SEGS].astype(jnp.int32), (1, 0, 2))
        cls_positives = cls_positives.reshape(MB, queries_all, 1)
        relative = relative_of(jnp.arange(PIECES, dtype=jnp.int32))
        cls_ids = ((relative ^ index)[:, None] * SEGS + jnp.arange(SEGS)[None, :]).reshape(1, -1)
    else:
        me = jnp.zeros((1,), jnp.int32)
        mix_near, mix_far = halves(by_heads(lax.all_gather(low_mix, "dp", axis=0, tiled=True)))
        out_near, out_far = halves(lax.all_gather(low_out, "dp", axis=0, tiled=True)[None])
        up_near, up_far = halves(by_columns(lax.all_gather(low_up, "dp", axis=0, tiled=True)))
        up_near = jnp.concatenate([out_near, up_near], axis=1)
        up_far = jnp.concatenate([out_far, up_far], axis=1)
        down_near, down_far = halves(lax.all_gather(low_down, "dp", axis=0, tiled=True)[None])
        vec_f = lax.all_gather(low_vec, "dp", axis=1, tiled=True).astype(jnp.float32)
        cls_positives = lax.all_gather(positives, "dp", axis=1, tiled=True)
        cls_positives = jnp.roll(cls_positives, -index * SEGS, axis=1)[:, :, None]
        cls_ids = jnp.roll(jnp.arange(queries_all, dtype=jnp.int32), -index * SEGS)[None]

    x_low = tokens[0].reshape(ROWS, D)
    seg_rows = segments[0].reshape(MB, L)
    seg_col, seg_row = seg_rows.reshape(ROWS, 1), seg_rows.reshape(MB, 1, L)
    before = jnp.concatenate([jnp.full((MB, 1), -1, jnp.int32), seg_rows[:, :-1]], axis=1)
    numbers = jnp.where(seg_rows != before, seg_rows, -1)
    numbers = jnp.where(numbers >= 0, numbers + SEGS * jnp.arange(MB)[:, None], -1).reshape(1, ROWS)
    table = (jnp.arange(MB * SEGS)[:, None] == numbers).astype(low_type)
    mixed_bias = jnp.concatenate([vec_f[0], jnp.zeros_like(vec_f[0]), vec_f[1]])
    mixed_bias = jnp.transpose(mixed_bias.reshape(3, HG, QCOLS), (1, 0, 2)).reshape(HG, 1, D)
    mixed, context, lse = attention_forward(
        me, mix_near, mix_far, x_low, seg_col, seg_row, mixed_bias
    )
    if fast:
        (got_up, got_down), mixed, context, lse = beside(
            [(up, 2), (down, 4)], mixed, context, lse
        )
        up_near, down = joined(up, got_up), joined(down, got_down)
        up_far = swapped(up_near, 1)
    normed_one, inverse_one, hidden, active, slope = up_forward(
        me, up_near, up_far, context, x_low, vec_f
    )
    if fast:
        (got_down,), normed_one, hidden, active, slope = beside(
            [(down, 2)], normed_one, hidden, active, slope
        )
        down_near = joined(down, got_down)
        down_far = swapped(down_near, 1)
    normed_two, inverse_two, output, cls_low = down_forward(
        me, down_near, down_far, active, normed_one, vec_f, table
    )

    both = jnp.concatenate([cls_low, tower_swapped(cls_low)])
    if fast:
        everyone = gather_pieces(both)
    else:
        everyone = jnp.roll(lax.all_gather(both, "dp", axis=0, tiled=False), -index, axis=0)
    everyone = jnp.transpose(everyone.reshape(owners, 2, MB, SEGS, D), (1, 2, 0, 3, 4))
    everyone = everyone.reshape(2, MB, queries_all, D)
    grad_cls = contrast_back(flag, everyone, cls_positives, cls_ids)

    residual, grad_ffn, sums_two, keep_down, send_down = down_back(
        me,
        token_grad[0].reshape(ROWS, D),
        grad_cls,
        jnp.concatenate([table] * 3),
        normed_two,
        inverse_two,
        vec_f,
        active,
    )
    if fast:
        (got_down,), residual, grad_ffn = beside([(send_down, 1)], residual, grad_ffn)
        keep_down, send_down = parted(keep_down, got_down)
    (grad_one, grad_ctx, sums_one, keep_up, send_up, keep_out, send_out) = up_back(
        me,
        up_near,
        up_far,
        down_near,
        down_far,
        grad_ffn,
        slope,
        hidden,
        residual,
        normed_one,
        inverse_one,
        context,
        vec_f,
    )
    if fast:
        (got_down,), grad_one, grad_ctx, send_up, send_out = beside(
            [(send_down, 2)], grad_one, grad_ctx, send_up, send_out
        )
        keep_down, send_down = parted(keep_down, got_down)
    back = partial(
        attention_back, me, mix_near, mix_far, x_low, seg_col, seg_row, mixed, lse, grad_ctx
    )
    grad_first, sums_a, keep_a, send_a = back(grad_one, 0)
    if fast:
        (got_down, got_up), grad_first, send_a = beside(
            [(send_down, 4), (send_up, 1)], grad_first, send_a
        )
        keep_down, send_down = parted(keep_down, got_down)
        keep_up, send_up = parted(keep_up, got_up)
        keep_a = jnp.concatenate([keep_out, keep_a], axis=1)
        send_a = jnp.concatenate([send_out, send_a], axis=1)
    grad_second, sums_b, keep_b, send_b = back(grad_first, 1)
    if fast:
        (got_down, got_up, got_a), grad_second, send_b = beside(
            [(send_down, 8), (send_up, 2), (send_a, 1)], grad_second, send_b
        )
        share_down = added(keep_down[0], got_down[0])
        keep_up, send_up = parted(keep_up, got_up)
        keep_a, send_a = parted(keep_a, got_a)
    input_grad, sums_c, keep_c, send_c = back(grad_second, 2)
    bias_mixed = jnp.concatenate([sums_a[:1], sums_b[:1], sums_c[:1]]).reshape(HG, 3, QCOLS)
    grad_vec = jnp.concatenate(
        [
            bias_mixed[:, 0].reshape(1, D),
            bias_mixed[:, 2].reshape(1, D),
            sums_one[4:7],
            sums_one[0:4],
            sums_two[0:3],
        ],
        axis=0,
    )
    if fast:
        vec_rows = jnp.broadcast_to(
            jnp.pad(grad_vec, ((0, 4), (0, 0))).astype(low_type)[None], (8, 16, D)
        )
        (got_up, got_a, got_b), input_grad, send_c = beside(
            [(send_up, 4), (send_a, 2), (send_b, 1)], input_grad, send_c
        )
        keep_up, send_up = parted(keep_up, got_up)
        keep_a, send_a = parted(keep_a, got_a)
        keep_b, send_b = parted(keep_b, got_b)
        keep_c = jnp.concatenate([keep_c, vec_rows], axis=1)
        send_c = jnp.concatenate([send_c, vec_rows], axis=1)
        ((got_up, got_a, got_b, got_c),) = beside(
            [(send_up, 8), (send_a, 4), (send_b, 2), (send_c, 1)]
        )
        share_up = added(keep_up[0], got_up[0])
        keep_a, send_a = parted(keep_a, got_a)
        keep_b, send_b = parted(keep_b, got_b)
        keep_c, send_c = parted(keep_c, got_c)
        ((got_a, got_b, got_c),) = beside([(send_a, 8), (send_b, 4), (send_c, 2)])
        share_a = added(keep_a[0], got_a[0])
        keep_b, send_b = parted(keep_b, got_b)
        keep_c, send_c = parted(keep_c, got_c)
        ((got_b, got_c),) = beside([(send_b, 8), (send_c, 4)])
        share_b = added(keep_b[0], got_b[0])
        keep_c, send_c = parted(keep_c, got_c)
        share_c = added(keep_c[0], swapped(send_c, 8)[0])
        share_out = share_a[:48]
        share_mix = from_heads(jnp.stack([share_a[48:], share_b, share_c[:48]]))
        share_vec = lax.dynamic_slice(share_c[48:60], (0, index * share), (12, share))
        share_up = from_columns(share_up.reshape(4, PIECE_ROWS, D))
    else:

        def scattered(matrix):
            return lax.psum_scatter(
                matrix.astype(jnp.float32), "dp", scatter_dimension=0, tiled=True
            )

        mix_blocks = jnp.concatenate(
            [whole_rows(*half, 1) for half in ((keep_a, send_a), (keep_b, send_b), (keep_c, send_c))]
        )
        share_mix = scattered(from_heads(mix_blocks))
        share_out = scattered(whole_rows(keep_out, send_out, 1)[0])
        share_up = scattered(from_columns(whole_rows(keep_up, send_up, 4)))
        share_down = scattered(whole_rows(keep_down, send_down, 1)[0])
        share_vec = lax.psum_scatter(grad_vec, "dp", scatter_dimension=1, tiled=True)

    shares = (share_mix, share_out, share_up, share_down, share_vec)
    local_square = sum(jnp.sum(s * s) for s in shares)
    if fast:
        grad_square = jnp.broadcast_to(local_square, (8, 128))
        for mask in (1, 2, 4, 8):
            grad_square = grad_square + swapped(grad_square, mask)
        grad_square = grad_square + tower_swapped(grad_square)
        grad_square = grad_square[0, 0]
    else:
        grad_square = lax.psum(local_square, ("tower", "dp"))
    factor = jnp.minimum(1.0, clip_norm / (jnp.sqrt(grad_square) + 1e-06))
    firsts = (first_mix[0], first_out[0], first_up[0], first_down[0], first_vectors[0])
    seconds = (second_mix[0], second_out[0], second_up[0], second_down[0], second_vectors[0])
    rates = (matrix_rate, matrix_rate, matrix_rate, matrix_rate, vector_rate)
    results = [
        adam_update(masters[i], shares[i], firsts[i], seconds[i], rates[i], factor)
        for i in range(5)
    ]
    return (
        output.reshape(1, MB, 1, L, D),
        input_grad.reshape(1, MB, 1, L, D),
        *(r[0] for r in results),
        *(r[1] for r in results),
        *(r[2] for r in results),
        grad_square,
    )


def solution(mesh):
    rows = P("tower", None, "dp", None, None)
    shards = (P("tower", "dp", None),) * 4 + (P("tower", None, "dp"),)
    in_specs = (rows, P("tower", None, "dp", None), P(None, "dp"), rows) + shards * 3
    out_specs = (rows, rows) + shards * 3 + (P(),)
    return jax.shard_map(body, mesh=mesh, in_specs=in_specs, out_specs=out_specs, check_vma=False)
```

```python
from functools import partial

import jax
import jax.numpy as jnp
from jax import lax
from jax.experimental import pallas as pl
from jax.experimental.pallas import tpu as pltpu
from jax.sharding import PartitionSpec as P

D = 768
FF = 3072
H = 12
HD = 64
L = 512
SEGS = 8
MB = 2
STEP = 5
HG = 3
PIECES = 16
PIECE_ROWS = D // PIECES

norm_eps = 1e-05
attention_scale = 0.125
score_scale = 0.0625
contrast_weight = 16.0
clip_norm = 1.0
beta_first = 0.9
beta_second = 0.999
adam_eps = 1e-08
weight_decay = 0.01
matrix_rate = 0.05
vector_rate = 0.5
masked_score = -1e30

low_type = jnp.bfloat16
highest = lax.Precision.HIGHEST


def swapped(value, mask):
    pairs = [(i, i ^ mask) for i in range(lax.axis_size("dp"))]
    return lax.ppermute(value, "dp", pairs)


def tower_swapped(value):
    return lax.ppermute(value, "tower", [(0, 1), (1, 0)])


def relative_of(place):
    return ((place & 1) << 3) | ((place & 2) << 1) | ((place & 4) >> 1) | (place >> 3)


def gather_pieces(own):
    pieces = own[None]
    for mask in (8, 4, 2, 1):
        pieces = jnp.concatenate([pieces, swapped(pieces, mask)])
    return pieces


def added(first, second):
    return first.astype(jnp.float32) + second.astype(jnp.float32)


def rows_dot(first_op, second_op):
    return jnp.dot(first_op, second_op, preferred_element_type=jnp.float32)


def contract_rows(first_op, second_op):
    return lax.dot_general(
        first_op, second_op, (((0,), (0,)), ((), ())), preferred_element_type=jnp.float32
    )


def contract_cols(first_op, second_op):
    return lax.dot_general(
        first_op, second_op, (((1,), (1,)), ((), ())), preferred_element_type=jnp.float32
    )


def layer_stats(values):
    centred = values - jnp.mean(values, axis=-1, keepdims=True)
    inverse = lax.rsqrt(jnp.mean(centred * centred, axis=-1, keepdims=True) + norm_eps)
    return (centred * inverse, inverse)


def norm_back(upstream, normed, inverse, gain_row):
    gained = upstream * gain_row
    return inverse * (
        gained
        - jnp.mean(gained, axis=-1, keepdims=True)
        - normed * jnp.mean(gained * normed, axis=-1, keepdims=True)
    )


def column_sum(values):
    return jnp.sum(values.astype(jnp.float32), axis=0, keepdims=True)


def gelu_parts(pre):
    below = 1.0 + (0.3275911 * 0.7071067811865476) * jnp.abs(pre)
    inner = pl.reciprocal(below, approx=True)
    inner = inner * (2.0 - below * inner)
    series = (0.5 * 1.061405429) * inner - (0.5 * 1.453152027)
    series = series * inner + (0.5 * 1.421413741)
    series = series * inner - (0.5 * 0.284496736)
    series = (series * inner + (0.5 * 0.254829592)) * inner
    bell = jnp.exp2(pre * pre * (-0.5 * log2e))
    half_tail = series * bell
    cumulative = jnp.where(pre >= 0.0, 1.0 - half_tail, half_tail)
    return (pre * cumulative, cumulative + pre * (bell * 0.3989422804014327))


log2e = 1.4426950408889634
ROWS = MB * L
QCOLS = D // HG
HEADS = H // HG
any_space = pl.BlockSpec(memory_space=pltpu.HBM)
scalar_space = pl.BlockSpec(memory_space=pltpu.SMEM)
vmem_space = pl.BlockSpec(memory_space=pltpu.VMEM)


def params(megabytes):
    return pltpu.CompilerParams(vmem_limit_bytes=megabytes * 1024 * 1024)


def cost(flops, moved, exps=0):
    return pl.CostEstimate(flops=int(flops), bytes_accessed=int(moved), transcendentals=int(exps))


def start_pieces(me, quads, row, target, sem):
    count = target.shape[1]
    for place in range(PIECES):
        pltpu.make_async_copy(
            quads[place // 4].at[place % 4, pl.ds(row, count), :],
            target.at[me ^ relative_of(place)],
            sem,
        ).start()


def start_owners(me, source, keep, send, sem):
    for place in range(PIECES):
        held = keep if place < 8 else send
        pltpu.make_async_copy(
            source.at[me ^ relative_of(place)], held.at[place % 8], sem
        ).start()


def block_of(pieces, index):
    at = pl.multiple_of(index * PIECE_ROWS, 16)
    return pieces[:, pl.ds(at, PIECE_ROWS), :].reshape(D, D)


def segment_mask(seg_row):
    numbers = seg_row[...].reshape(1, L)
    columns = jnp.transpose(jnp.broadcast_to(numbers, (8, L)))[:, :1]
    return jnp.where(columns == numbers, 0.0, masked_score)


def wait_bytes(whole, sem):
    pltpu.make_async_copy(whole, whole, sem).wait()


def attention_kernel(
    me_ref, *refs
):
    quads = refs[:4]
    x_ref, seg_row, mixed_ref, ctx_ref, lse_ref, vec_ref, w, mask, bias, sems = refs[4:]
    hg, mb = pl.program_id(0), pl.program_id(1)
    me = me_ref[0]

    @pl.when((hg == 0) & (mb == 0))
    def _():
        start_pieces(me, quads, 0, w, sems.at[0])

    @pl.when(hg == 0)
    def _():
        mask[mb] = segment_mask(seg_row)

    @pl.when((hg == 0) & (mb == 0))
    def _():
        wait_bytes(w, sems.at[0])
        vec = w[0, HG * PIECE_ROWS :, :].astype(jnp.float32)
        for place in range(1, PIECES):
            vec = vec + w[place, HG * PIECE_ROWS :, :].astype(jnp.float32)
        vec_ref[...] = vec
        for group in range(HG):
            columns = slice(group * QCOLS, (group + 1) * QCOLS)
            none = jnp.zeros((1, QCOLS), jnp.float32)
            bias[group] = jnp.concatenate([vec[0:1, columns], none, vec[1:2, columns]], axis=1)

    mixed = (rows_dot(x_ref[...], block_of(w, hg)) + bias[hg]).astype(low_type)
    mixed_ref[...] = mixed.reshape(mixed_ref.shape)
    v_t = jnp.transpose(mixed[:, 2 * QCOLS :])
    outs, totals = [], []

    def scores_of(head):
        here = slice(head * HD, (head + 1) * HD)
        q, k = mixed[:, here], mixed[:, QCOLS + head * HD : QCOLS + (head + 1) * HD]
        return contract_cols(k, q)

    ahead = scores_of(0)
    for head in range(HEADS):
        here = slice(head * HD, (head + 1) * HD)
        scores = ahead * (attention_scale * log2e) + mask[mb]
        if head + 1 < HEADS:
            ahead = scores_of(head + 1)
        largest = jnp.max(scores, axis=0, keepdims=True)
        expo = jnp.exp2(scores - largest)
        summed = jnp.sum(expo, axis=0, keepdims=True)
        probs = expo.astype(low_type)
        outs.append((rows_dot(v_t[here], probs) * (1.0 / summed)).astype(low_type))
        totals.append(largest + jnp.log(summed) * log2e)
    ctx_ref[...] = jnp.transpose(jnp.concatenate(outs, axis=0))
    lse_ref[...] = jnp.concatenate(totals, axis=0).reshape(lse_ref.shape)


def attention_forward(me, quads, x_low, seg_row):
    return pl.pallas_call(
        attention_kernel,
        grid=(HG, MB),
        in_specs=[
            scalar_space,
            *[any_space] * 4,
            pl.BlockSpec((L, D), lambda g, m: (m, 0)),
            pl.BlockSpec((1, 1, L), lambda g, m: (m, 0, 0)),
        ],
        out_specs=[
            pl.BlockSpec((1, L, D), lambda g, m: (g, m, 0)),
            pl.BlockSpec((L, QCOLS), lambda g, m: (m, g)),
            pl.BlockSpec((1, HEADS, L), lambda g, m: (g * MB + m, 0, 0)),
            pl.BlockSpec((16, D), lambda g, m: (0, 0)),
        ],
        out_shape=[
            jax.ShapeDtypeStruct((HG, ROWS, D), low_type),
            jax.ShapeDtypeStruct((ROWS, D), low_type),
            jax.ShapeDtypeStruct((HG * MB, HEADS, L), jnp.float32),
            jax.ShapeDtypeStruct((16, D), jnp.float32),
        ],
        scratch_shapes=[
            pltpu.VMEM((PIECES, HG * PIECE_ROWS + 16, D), low_type),
            pltpu.VMEM((MB, L, L), jnp.float32),
            pltpu.VMEM((HG, 1, D), jnp.float32),
            pltpu.SemaphoreType.DMA((1,)),
        ],
        compiler_params=params(40),
        cost_estimate=cost(2 * ROWS * D * 3 * D + 8 * MB * H * L * L * HD, 12e6, MB * H * L * L),
        name="mixed_attention",
    )(me, *quads, x_low, seg_row)


def up_kernel(
    me_ref,
    quad_0,
    quad_1,
    quad_2,
    quad_3,
    ctx_hbm,
    x_hbm,
    vec,
    normed_hbm,
    inverse_ref,
    hidden_hbm,
    active_ref,
    slope_ref,
    w,
    ctx,
    x,
    normed,
    hidden,
    sems,
):
    step = pl.program_id(0)
    me = me_ref[0]
    quads = (quad_0, quad_1, quad_2, quad_3)
    ctx_in = pltpu.make_async_copy(ctx_hbm, ctx, sems.at[1])
    x_in = pltpu.make_async_copy(x_hbm, x, sems.at[2])
    normed_out = pltpu.make_async_copy(normed, normed_hbm, sems.at[3])
    hidden_out = pltpu.make_async_copy(hidden, hidden_hbm, sems.at[4])

    @pl.when(step == 0)
    def _():
        start_pieces(me, quads, 0, w, sems.at[0])
        ctx_in.start()
        x_in.start()
        wait_bytes(w, sems.at[0])
        ctx_in.wait()
        x_in.wait()
        for first in range(0, ROWS, 256):
            part = slice(first, first + 256)
            branch = rows_dot(ctx[part, :], block_of(w, 4)) + vec[2:3, :]
            n, inv = layer_stats(x[part, :].astype(jnp.float32) + branch)
            normed[part, :] = n
            inverse_ref[part, :] = inv
            hidden[part, :] = (n * vec[3:4, :] + vec[4:5, :]).astype(low_type)
        normed_out.start()
        hidden_out.start()

    bias = vec[pl.ds(5 + step, 1), :]
    for first in range(0, ROWS, 256):
        part = slice(first, first + 256)
        pre = rows_dot(hidden[part, :], block_of(w, step)) + bias
        active, slope = gelu_parts(pre)
        active_ref[part, :] = active.astype(low_type)
        slope_ref[part, :] = slope.astype(low_type)

    @pl.when(step == 3)
    def _():
        normed_out.wait()
        hidden_out.wait()


def up_forward(me, quads, context, x_low, vec):
    return pl.pallas_call(
        up_kernel,
        grid=(4,),
        in_specs=[scalar_space, *[any_space] * 6, vmem_space],
        out_specs=[
            any_space,
            pl.BlockSpec((ROWS, 1), lambda s: (0, 0)),
            any_space,
            pl.BlockSpec((ROWS, D), lambda s: (0, s)),
            pl.BlockSpec((ROWS, D), lambda s: (0, s)),
        ],
        out_shape=[
            jax.ShapeDtypeStruct((ROWS, D), jnp.float32),
            jax.ShapeDtypeStruct((ROWS, 1), jnp.float32),
            jax.ShapeDtypeStruct((ROWS, D), low_type),
            jax.ShapeDtypeStruct((ROWS, FF), low_type),
            jax.ShapeDtypeStruct((ROWS, FF), low_type),
        ],
        scratch_shapes=[
            pltpu.VMEM((PIECES, 5 * PIECE_ROWS, D), low_type),
            pltpu.VMEM((ROWS, D), low_type),
            pltpu.VMEM((ROWS, D), low_type),
            pltpu.VMEM((ROWS, D), jnp.float32),
            pltpu.VMEM((ROWS, D), low_type),
            pltpu.SemaphoreType.DMA((5,)),
        ],
        compiler_params=params(44),
        cost_estimate=cost(2 * ROWS * D * (FF + D), 24e6, 2 * ROWS * FF),
        name="out_up",
    )(me, *quads, context, x_low, vec)


def down_kernel(
    me_ref,
    quad_0,
    quad_1,
    quad_2,
    quad_3,
    active_hbm,
    normed_one_hbm,
    vec,
    table_ref,
    normed_ref,
    inverse_ref,
    output_ref,
    cls_ref,
    w,
    active,
    normed_one_ref,
    sems,
):
    me = me_ref[0]
    start_pieces(me, (quad_0, quad_1, quad_2, quad_3), 0, w, sems.at[0])
    copies = []
    for index in range(4):
        part = pl.ds(index * 256, 256)
        copies.append(
            pltpu.make_async_copy(active_hbm.at[part, :], active.at[part, :], sems.at[1 + index])
        )
        copies[-1].start()
    normed_one_in = pltpu.make_async_copy(normed_one_hbm, normed_one_ref, sems.at[5])
    normed_one_in.start()
    wait_bytes(w, sems.at[0])
    for index in range(4):
        copies[index].wait()
        part = slice(index * 256, (index + 1) * 256)
        if index == 0:
            normed_one_in.wait()
        ffn = rows_dot(active[part, :], w[...].reshape(FF, D)) + vec[9:10, :]
        residual = normed_one_ref[part, :] * vec[3:4, :] + vec[4:5, :]
        n, inv = layer_stats(residual + ffn)
        normed_ref[part, :] = n
        inverse_ref[part, :] = inv
        output_ref[part, :] = (n * vec[10:11, :] + vec[11:12, :]).astype(low_type)
    cls_ref[...] = rows_dot(table_ref[...], output_ref[...]).astype(low_type)


def down_forward(me, quads, active, normed_one, vec, table):
    return pl.pallas_call(
        down_kernel,
        in_specs=[scalar_space, *[any_space] * 6, vmem_space, vmem_space],
        out_specs=[vmem_space] * 4,
        out_shape=[
            jax.ShapeDtypeStruct((ROWS, D), jnp.float32),
            jax.ShapeDtypeStruct((ROWS, 1), jnp.float32),
            jax.ShapeDtypeStruct((ROWS, D), low_type),
            jax.ShapeDtypeStruct((MB * SEGS, D), low_type),
        ],
        scratch_shapes=[
            pltpu.VMEM((PIECES, 4 * PIECE_ROWS, D), low_type),
            pltpu.VMEM((ROWS, FF), low_type),
            pltpu.VMEM((ROWS, D), jnp.float32),
            pltpu.SemaphoreType.DMA((6,)),
        ],
        compiler_params=params(40),
        cost_estimate=cost(2 * ROWS * D * FF, 19e6),
        name="down",
    )(me, *quads, active, normed_one, vec, table)


def contrast_kernel(flag_ref, all_ref, positive_ref, ids_ref, grad_ref):
    passage_here = flag_ref[0] == 1
    for batch in range(MB):
        mine, theirs = all_ref[0, batch], all_ref[1, batch]
        queries = jnp.where(passage_here, theirs, mine)
        passages = jnp.where(passage_here, mine, theirs)
        contrast = contract_cols(queries, passages) * score_scale
        top = jnp.max(contrast, axis=-1, keepdims=True)
        expo = jnp.exp(contrast - top)
        probs = expo / jnp.sum(expo, axis=-1, keepdims=True)
        chosen = (positive_ref[batch] == ids_ref[...]).astype(jnp.float32)
        grad = (contrast_weight * (probs - chosen)).astype(low_type)
        for_query = rows_dot(grad[:16], passages) * score_scale
        for_query = for_query.astype(low_type).astype(jnp.float32)
        for_passage = contract_rows(grad, queries)[:16] * score_scale
        taken = jnp.where(passage_here, for_passage, for_query)
        grad_ref[batch * SEGS : (batch + 1) * SEGS, :] = taken[:SEGS]


def contrast_back(flag, everyone, cls_positives, cls_ids):
    return pl.pallas_call(
        contrast_kernel,
        in_specs=[scalar_space, vmem_space, vmem_space, vmem_space],
        out_specs=vmem_space,
        out_shape=jax.ShapeDtypeStruct((MB * SEGS, D), jnp.float32),
        compiler_params=params(48),
        name="contrast",
    )(flag, everyone, cls_positives, cls_ids)


def down_back_kernel(
    me_ref,
    token_grad,
    grad_cls,
    table3_ref,
    normed_ref,
    inverse_ref,
    vec,
    active_ref,
    residual_ref,
    low_ref,
    sums_ref,
    keep,
    send,
    low,
    staged,
    sem,
):
    step = pl.program_id(0)

    @pl.when(step == 0)
    def _():
        grads = grad_cls[...]
        upper = grads.astype(low_type)
        rest = grads - upper.astype(jnp.float32)
        middle = rest.astype(low_type)
        lower = (rest - middle.astype(jnp.float32)).astype(low_type)
        stacked = jnp.concatenate([upper, middle, lower], axis=0)
        gains = jnp.zeros((1, D), jnp.float32)
        shifts = jnp.zeros((1, D), jnp.float32)
        biases = jnp.zeros((1, D), jnp.float32)
        for first in range(0, ROWS, 256):
            part = slice(first, first + 256)
            upstream = token_grad[part, :] + contract_rows(table3_ref[:, part], stacked)
            n = normed_ref[part, :]
            gains = gains + column_sum(upstream * n)
            shifts = shifts + column_sum(upstream)
            grad = norm_back(upstream, n, inverse_ref[part, :], vec[10:11, :])
            residual_ref[part, :] = grad
            rounded = grad.astype(low_type)
            biases = biases + column_sum(rounded)
            low[part, :] = rounded
        low_ref[...] = low[...]
        sums_ref[...] = jnp.concatenate([biases, gains, shifts, jnp.zeros((5, D), jnp.float32)])

    for first in range(4):
        at = first * 4 * PIECE_ROWS
        staged[4 * step + first] = contract_rows(
            active_ref[:, at : at + 4 * PIECE_ROWS], low[...]
        ).astype(low_type)

    @pl.when(step == 3)
    def _():
        start_owners(me_ref[0], staged, keep, send, sem)
        wait_bytes(staged, sem)


def down_back(me, token_grad, grad_cls, table3, normed, inverse, vec, active):
    half = jax.ShapeDtypeStruct((8, 4 * PIECE_ROWS, D), low_type)
    return pl.pallas_call(
        down_back_kernel,
        grid=(4,),
        in_specs=[scalar_space]
        + [vmem_space] * 6
        + [pl.BlockSpec((ROWS, D), lambda s: (0, s))],
        out_specs=[vmem_space] * 3 + [any_space] * 2,
        out_shape=[
            jax.ShapeDtypeStruct((ROWS, D), jnp.float32),
            jax.ShapeDtypeStruct((ROWS, D), low_type),
            jax.ShapeDtypeStruct((8, D), jnp.float32),
            half,
            half,
        ],
        scratch_shapes=[
            pltpu.VMEM((ROWS, D), low_type),
            pltpu.VMEM((PIECES, 4 * PIECE_ROWS, D), low_type),
            pltpu.SemaphoreType.DMA,
        ],
        compiler_params=params(48),
        cost_estimate=cost(2 * ROWS * D * FF, 25e6),
        name="down_back",
    )(me, token_grad, grad_cls, table3, normed, inverse, vec, active)


def up_back_kernel(
    me_ref,
    up_0,
    up_1,
    up_2,
    up_3,
    down_0,
    down_1,
    down_2,
    down_3,
    low_ref,
    slope_ref,
    hidden_ref,
    residual_hbm,
    normed_hbm,
    inverse_ref,
    ctx_hbm,
    vec,
    grad_one_ref,
    grad_ctx_ref,
    sums_ref,
    keep,
    send,
    keep_out,
    send_out,
    up_w,
    down_w,
    normed,
    ctx,
    total,
    staged,
    staged_out,
    bias_sums,
    sems,
):
    step = pl.program_id(0)
    me = me_ref[0]
    residual_in = pltpu.make_async_copy(residual_hbm, total, sems.at[2])
    normed_in = pltpu.make_async_copy(normed_hbm, normed, sems.at[3])
    ctx_in = pltpu.make_async_copy(ctx_hbm, ctx, sems.at[4])

    @pl.when(step == 0)
    def _():
        start_pieces(me, (down_0, down_1, down_2, down_3), 0, down_w, sems.at[0])
        start_pieces(me, (up_0, up_1, up_2, up_3), 0, up_w, sems.at[1])
        residual_in.start()
        normed_in.start()
        ctx_in.start()
        wait_bytes(down_w, sems.at[0])
        wait_bytes(up_w, sems.at[1])
        residual_in.wait()

    down_block = down_w[pl.ds(4 * step, 4)].reshape(D, D)
    up_block = block_of(up_w, step)
    grads = []
    biases = jnp.zeros((1, D), jnp.float32)
    for first in range(0, ROWS, 256):
        part = slice(first, first + 256)
        active_grad = contract_cols(low_ref[part, :], down_block)
        grad = (active_grad * slope_ref[part, :].astype(jnp.float32)).astype(low_type)
        biases = biases + column_sum(grad)
        grads.append(grad)
        total[part, :] += contract_cols(grad, up_block)

    grad = jnp.concatenate(grads, axis=0)
    at = pl.multiple_of(step * PIECE_ROWS, 16)
    for first in range(0, PIECES, 4):
        columns = slice(first * PIECE_ROWS, (first + 4) * PIECE_ROWS)
        terms = contract_rows(hidden_ref[:, columns], grad).astype(low_type)
        staged[first : first + 4, pl.ds(at, PIECE_ROWS), :] = terms.reshape(4, PIECE_ROWS, D)
    bias_sums[step] = biases

    @pl.when(step == 3)
    def _():
        start_owners(me, staged, keep, send, sems.at[5])
        normed_in.wait()
        ctx_in.wait()
        gains = jnp.zeros((1, D), jnp.float32)
        shifts = jnp.zeros((1, D), jnp.float32)
        out_biases = jnp.zeros((1, D), jnp.float32)
        lows = []
        for first in range(0, ROWS, 256):
            part = slice(first, first + 256)
            upstream = total[part, :]
            n = normed[part, :]
            gains = gains + column_sum(upstream * n)
            shifts = shifts + column_sum(upstream)
            grad_one = norm_back(upstream, n, inverse_ref[part, :], vec[3:4, :])
            grad_one_ref[part, :] = grad_one
            rounded = grad_one.astype(low_type)
            out_biases = out_biases + column_sum(rounded)
            grad_ctx_ref[part, :] = contract_cols(rounded, block_of(up_w, 4)).astype(low_type)
            lows.append(rounded)
        sums_ref[...] = jnp.concatenate(
            [bias_sums[block] for block in range(4)]
            + [out_biases, gains, shifts, jnp.zeros((1, D), jnp.float32)]
        )
        rounded = jnp.concatenate(lows, axis=0)
        for first in range(0, PIECES, 4):
            columns = slice(first * PIECE_ROWS, (first + 4) * PIECE_ROWS)
            terms = contract_rows(ctx[:, columns], rounded).astype(low_type)
            staged_out[first : first + 4] = terms.reshape(4, PIECE_ROWS, D)
        start_owners(me, staged_out, keep_out, send_out, sems.at[6])
        wait_bytes(staged, sems.at[5])
        wait_bytes(staged_out, sems.at[6])


def up_back(
    me, up_quads, down_quads, low, slope, hidden, residual, normed, inverse, ctx, vec
):
    half = jax.ShapeDtypeStruct((8, 4 * PIECE_ROWS, D), low_type)
    half_out = jax.ShapeDtypeStruct((8, PIECE_ROWS, D), low_type)
    return pl.pallas_call(
        up_back_kernel,
        grid=(4,),
        in_specs=[scalar_space]
        + [any_space] * 8
        + [
            vmem_space,
            pl.BlockSpec((ROWS, D), lambda s: (0, s)),
            vmem_space,
            any_space,
            any_space,
            vmem_space,
            any_space,
            vmem_space,
        ],
        out_specs=[vmem_space] * 3 + [any_space] * 4,
        out_shape=[
            jax.ShapeDtypeStruct((ROWS, D), jnp.float32),
            jax.ShapeDtypeStruct((ROWS, D), low_type),
            jax.ShapeDtypeStruct((8, D), jnp.float32),
            half,
            half,
            half_out,
            half_out,
        ],
        scratch_shapes=[
            pltpu.VMEM((PIECES, 5 * PIECE_ROWS, D), low_type),
            pltpu.VMEM((PIECES, 4 * PIECE_ROWS, D), low_type),
            pltpu.VMEM((ROWS, D), jnp.float32),
            pltpu.VMEM((ROWS, D), low_type),
            pltpu.VMEM((ROWS, D), jnp.float32),
            pltpu.VMEM((PIECES, 4 * PIECE_ROWS, D), low_type),
            pltpu.VMEM((PIECES, PIECE_ROWS, D), low_type),
            pltpu.VMEM((4, 1, D), jnp.float32),
            pltpu.SemaphoreType.DMA((7,)),
        ],
        compiler_params=params(56),
        cost_estimate=cost(2 * ROWS * D * (3 * FF + 2 * D), 40e6),
        name="up_back",
    )(
        me,
        *up_quads,
        *down_quads,
        low,
        slope,
        hidden,
        residual,
        normed,
        inverse,
        ctx,
        vec,
    )


def attention_back_kernel(
    me_ref,
    x_ref,
    seg_row,
    mixed_ref,
    lse_ref,
    grad_ctx_ref,
    *refs,
):
    others, (grad_mixed_ref, sums_ref, keep, send, weight_grad, staged, sem) = refs[:-7], refs[-7:]
    mb = pl.program_id(0)
    me = me_ref[0]
    mask = segment_mask(seg_row)
    mixed = mixed_ref[...].reshape(L, D)
    lse = lse_ref[...].reshape(HEADS, L)
    k_t = jnp.transpose(mixed[:, QCOLS : 2 * QCOLS])
    grad_q, grad_k, grad_v = [], [], []

    def products_of(head):
        here = slice(head * HD, (head + 1) * HD)
        q, k = mixed[:, here], mixed[:, QCOLS + head * HD : QCOLS + (head + 1) * HD]
        v = mixed[:, 2 * QCOLS + head * HD : 2 * QCOLS + (head + 1) * HD]
        return (contract_cols(k, q), contract_cols(v, grad_ctx_ref[:, here]))

    ahead = products_of(0)
    for head in range(HEADS):
        here = slice(head * HD, (head + 1) * HD)
        scores, grad_probs = ahead
        if head + 1 < HEADS:
            ahead = products_of(head + 1)
        scores = scores * (attention_scale * log2e) + mask
        probs = jnp.exp2(scores - lse[head : head + 1])
        inner = jnp.sum(probs * grad_probs, axis=0, keepdims=True)
        grad_scores = (probs * (grad_probs - inner)).astype(low_type)
        grad_v.append(rows_dot(probs.astype(low_type), grad_ctx_ref[:, here]).astype(low_type))
        grad_q.append((rows_dot(k_t[here], grad_scores) * attention_scale).astype(low_type))
        grad_k.append((rows_dot(grad_scores, mixed[:, here]) * attention_scale).astype(low_type))
    grad_mixed = jnp.concatenate(
        [jnp.transpose(jnp.concatenate(grad_q, axis=0))] + grad_k + grad_v, axis=1
    )

    grad_mixed_ref[...] = grad_mixed
    bias = column_sum(grad_mixed)
    terms = contract_rows(x_ref[...], grad_mixed)

    @pl.when(mb == 0)
    def _():
        weight_grad[...] = terms
        sums_ref[0:1, :] = bias

    @pl.when(mb == 1)
    def _():
        sums_ref[0:1, :] += bias
        grads = (weight_grad[...] + terms).astype(low_type)
        staged[:, :PIECE_ROWS, :] = grads.reshape(PIECES, PIECE_ROWS, D)
        if others:
            mixed_a, mixed_b, up, down = (other[...] for other in others)
            mixed_sums = (mixed_a[0:1], mixed_b[0:1], sums_ref[0:1, :])
            vectors = jnp.concatenate(
                [
                    jnp.concatenate([s[:, :QCOLS] for s in mixed_sums], axis=1),
                    jnp.concatenate([s[:, 2 * QCOLS :] for s in mixed_sums], axis=1),
                    up[4:7],
                    up[0:4],
                    down[0:3],
                    jnp.zeros((4, D), jnp.float32),
                ],
                axis=0,
            )
            for place in range(PIECES):
                staged[place, PIECE_ROWS:, :] = vectors.astype(low_type)
        start_owners(me, staged, keep, send, sem)
        wait_bytes(staged, sem)


def attention_back(me, x_low, seg_row, mixed, lse, grad_ctx, group, *others):
    rows = PIECE_ROWS + (16 if others else 0)
    half = jax.ShapeDtypeStruct((8, rows, D), low_type)
    return pl.pallas_call(
        attention_back_kernel,
        grid=(MB,),
        in_specs=[
            scalar_space,
            pl.BlockSpec((L, D), lambda m: (m, 0)),
            pl.BlockSpec((1, 1, L), lambda m: (m, 0, 0)),
            pl.BlockSpec((1, L, D), lambda m: (group, m, 0)),
            pl.BlockSpec((1, HEADS, L), lambda m: (group * MB + m, 0, 0)),
            pl.BlockSpec((L, QCOLS), lambda m: (m, group)),
            *[vmem_space] * len(others),
        ],
        out_specs=[pl.BlockSpec((L, D), lambda m: (m, 0)), vmem_space, any_space, any_space],
        out_shape=[
            jax.ShapeDtypeStruct((ROWS, D), low_type),
            jax.ShapeDtypeStruct((8, D), jnp.float32),
            half,
            half,
        ],
        scratch_shapes=[
            pltpu.VMEM((D, D), jnp.float32),
            pltpu.VMEM((PIECES, rows, D), low_type),
            pltpu.SemaphoreType.DMA,
        ],
        compiler_params=params(40),
        cost_estimate=cost(
            2 * ROWS * D * D + 20 * MB * HEADS * L * L * HD, 12e6, MB * HEADS * L * L
        ),
        name=f"attention_back_{group}",
    )(me, x_low, seg_row, mixed, lse, grad_ctx, *others)


def input_back_kernel(
    me_ref, quad_0, quad_1, quad_2, quad_3, one_ref, grad_0, grad_1, grad_2, input_ref, w, sem
):
    @pl.when(pl.program_id(0) == 0)
    def _():
        start_pieces(me_ref[0], (quad_0, quad_1, quad_2, quad_3), 0, w, sem)
        wait_bytes(w, sem)

    total = one_ref[...]
    for block, grad in enumerate((grad_0, grad_1, grad_2)):
        total = total + contract_cols(grad[...], block_of(w, block))
    input_ref[...] = total


def input_back(me, quads, grad_one, grads):
    rows = pl.BlockSpec((256, D), lambda s: (s, 0))
    return pl.pallas_call(
        input_back_kernel,
        grid=(ROWS // 256,),
        in_specs=[scalar_space] + [any_space] * 4 + [rows] * 4,
        out_specs=rows,
        out_shape=jax.ShapeDtypeStruct((ROWS, D), jnp.float32),
        scratch_shapes=[
            pltpu.VMEM((PIECES, HG * PIECE_ROWS, D), low_type),
            pltpu.SemaphoreType.DMA,
        ],
        compiler_params=params(24),
        cost_estimate=cost(6 * ROWS * D * D, 14e6),
        name="input_back",
    )(me, *quads, grad_one, *grads)


def adam_kernel(norm_ref, down_ref, up_ref, out_ref, mix_ab, mix_c, vec_ref, *refs):
    ins, outs, held, sems = refs[:15], refs[15:30], refs[30:45], refs[45]
    arrivals = [
        pltpu.make_async_copy(ins[i], held[i], sems.at[i]) for i in range(15)
    ]
    departures = [
        pltpu.make_async_copy(held[i], outs[i], sems.at[i]) for i in range(15)
    ]
    order = (3, 2, 0, 1, 4)
    for index in order:
        for i in (index, 5 + index, 10 + index):
            arrivals[i].start()
    factor = jnp.minimum(1.0, clip_norm / (jnp.sqrt(norm_ref[0:1, 0:1]) + 1e-06))

    def update(index, columns, grad, rate):
        master, first, second = held[index], held[5 + index], held[10 + index]
        clipped = grad * factor
        first_new = beta_first * first[:, columns] + (1.0 - beta_first) * clipped
        second_new = beta_second * second[:, columns] + (1.0 - beta_second) * clipped * clipped
        root = jnp.sqrt(second_new / (1.0 - beta_second**STEP)) + adam_eps
        step = first_new / (1.0 - beta_first**STEP) / root
        old = master[:, columns]
        master[:, columns] = old - rate * (step + weight_decay * old)
        first[:, columns] = first_new
        second[:, columns] = second_new

    for index in order:
        for i in (index, 5 + index, 10 + index):
            arrivals[i].wait()
        if index == 0:
            parts = (mix_ab[:PIECE_ROWS, :], mix_ab[PIECE_ROWS:, :], mix_c[:PIECE_ROWS, :])
            for group, share in enumerate(parts):
                for third in range(3):
                    at = third * D + group * QCOLS
                    grad = share[:, third * QCOLS : (third + 1) * QCOLS]
                    update(0, slice(at, at + QCOLS), grad, matrix_rate)
        elif index == 1:
            update(1, slice(0, D), out_ref[...], matrix_rate)
        elif index == 2:
            for block in range(4):
                grad = up_ref[block * PIECE_ROWS : (block + 1) * PIECE_ROWS, :]
                update(2, slice(block * D, (block + 1) * D), grad, matrix_rate)
        elif index == 3:
            update(3, slice(0, D), down_ref[...], matrix_rate)
        else:
            update(4, slice(0, PIECE_ROWS), vec_ref[...], vector_rate)
        for i in (index, 5 + index, 10 + index):
            departures[i].start()
    for departure in departures:
        departure.wait()


def adam_all(norm, shares, arrays):
    return pl.pallas_call(
        adam_kernel,
        in_specs=[vmem_space] * 7 + [any_space] * 15,
        out_specs=[any_space] * 15,
        out_shape=[jax.ShapeDtypeStruct(a.shape, jnp.float32) for a in arrays],
        scratch_shapes=[pltpu.VMEM(a.shape, jnp.float32) for a in arrays]
        + [pltpu.SemaphoreType.DMA((15,))],
        compiler_params=params(40),
        cost_estimate=cost(40e6, 25e6),
        name="adam",
    )(norm, *shares, *arrays)


def by_heads(matrix):
    shaped = matrix.reshape(matrix.shape[0], 3, HG, D // HG)
    return jnp.transpose(shaped, (2, 0, 1, 3)).reshape(HG, matrix.shape[0], D)


def from_heads(blocks):
    rows = blocks.shape[1]
    shaped = blocks.reshape(HG, rows, 3, D // HG)
    return jnp.transpose(shaped, (1, 2, 0, 3)).reshape(rows, 3 * D)


def by_columns(matrix):
    return jnp.transpose(matrix.reshape(matrix.shape[0], 4, D), (1, 0, 2))


def from_columns(blocks):
    return jnp.transpose(blocks, (1, 0, 2)).reshape(blocks.shape[1], 4 * D)


def adam_update(master, grad_share, first, second, rate, factor):
    clipped = grad_share * factor
    first_new = beta_first * first + (1.0 - beta_first) * clipped
    second_new = beta_second * second + (1.0 - beta_second) * clipped * clipped
    first_hat = first_new / (1.0 - beta_first**STEP)
    second_hat = second_new / (1.0 - beta_second**STEP)
    master_new = master - rate * (
        first_hat / (jnp.sqrt(second_hat) + adam_eps) + weight_decay * master
    )
    return (master_new[None], first_new[None], second_new[None])


def quads_of(matrix_rows):
    k = matrix_rows.shape[0]
    shaped = matrix_rows.reshape(k, 2, 2, 2, 2, -1, D)
    pieces = jnp.transpose(shaped, (4, 3, 2, 1, 0, 5, 6)).reshape(4, 4, -1, D)
    return tuple(pieces[i] for i in range(4))


def whole_rows(keep, send, k):
    shaped = jnp.concatenate([keep, send]).reshape(2, 2, 2, 2, k, -1, D)
    return jnp.transpose(shaped, (4, 3, 2, 1, 0, 5, 6)).reshape(k, -1, D)


def beside(sends, *work):
    received = [swapped(value, mask) for value, mask in sends]
    done = lax.optimization_barrier((received, work))
    return (done[0], *done[1])


def across(value, tower_mask, dp_mask):
    owners = lax.axis_size("dp")
    flip = tower_mask * owners + dp_mask
    pairs = [(i, i ^ flip) for i in range(2 * owners)]
    return lax.ppermute(value, ("tower", "dp"), pairs)


def joined(pieces, received):
    return jnp.concatenate([pieces, received])


def parted(keep, received):
    half = keep.shape[0] // 2
    return (
        added(keep[:half], received[:half]).astype(low_type),
        added(keep[half:], received[half:]).astype(low_type),
    )


def body(
    tokens,
    segments,
    positives,
    token_grad,
    mix_weight,
    out_weight,
    up_weight,
    down_weight,
    vectors,
    first_mix,
    first_out,
    first_up,
    first_down,
    first_vectors,
    second_mix,
    second_out,
    second_up,
    second_down,
    second_vectors,
):
    owners = lax.axis_size("dp")
    fast = owners == PIECES
    index = lax.axis_index("dp")
    flag = lax.axis_index("tower").astype(jnp.int32).reshape(1)
    masters = (mix_weight[0], out_weight[0], up_weight[0], down_weight[0], vectors[0])
    low_mix, low_out, low_up, low_down, low_vec = (m.astype(low_type) for m in masters)
    share = low_vec.shape[1]
    queries_all = owners * SEGS

    if fast:
        me = index.astype(jnp.int32).reshape(1)
        extra = jnp.zeros((16, D), low_type)
        extra = extra.at[12:14, :SEGS].set(positives.astype(low_type))
        extra = lax.dynamic_update_slice(extra, low_vec, (0, index * share))
        pack_mix = jnp.concatenate([by_heads(low_mix).reshape(-1, D), extra])
        pack_up = jnp.concatenate([by_columns(low_up).reshape(-1, D), low_out])
        mix, up, down = pack_mix[None], pack_up[None], low_down[None]
        ((got_mix,),) = beside([(mix, 8)])
        mix = joined(mix, got_mix)
        ((got_mix, got_up),) = beside([(mix, 4), (up, 8)])
        mix, up = joined(mix, got_mix), joined(up, got_up)
        ((mix_y, mix_core, got_up, got_down),) = beside([(mix, 2), (mix, 1), (up, 4), (down, 8)])
        up, down = joined(up, got_up), joined(down, got_down)
        mix_quads = (mix, mix_y, mix_core, swapped(mix_y, 1))
        extras = jnp.concatenate([quad[:, 156:158, :SEGS] for quad in mix_quads])
        cls_positives = jnp.transpose(extras.astype(jnp.int32), (1, 0, 2))
        cls_positives = cls_positives.reshape(MB, queries_all, 1)
        relative = relative_of(jnp.arange(PIECES, dtype=jnp.int32))
        cls_ids = ((relative ^ index)[:, None] * SEGS + jnp.arange(SEGS)[None, :]).reshape(1, -1)
    else:
        me = jnp.zeros((1,), jnp.int32)
        mix_quads = quads_of(by_heads(lax.all_gather(low_mix, "dp", axis=0, tiled=True)))
        out_quads = quads_of(lax.all_gather(low_out, "dp", axis=0, tiled=True)[None])
        up_quads = quads_of(by_columns(lax.all_gather(low_up, "dp", axis=0, tiled=True)))
        up_quads = tuple(
            jnp.concatenate(pair, axis=1) for pair in zip(up_quads, out_quads, strict=True)
        )
        down_quads = quads_of(lax.all_gather(low_down, "dp", axis=0, tiled=True)[None])
        vec_low = lax.all_gather(low_vec, "dp", axis=1, tiled=True)
        extra = jnp.zeros((PIECES, 16, D), low_type).at[0, :12].set(vec_low)
        mix_quads = tuple(
            jnp.concatenate([quad, extra[4 * i : 4 * i + 4]], axis=1)
            for i, quad in enumerate(mix_quads)
        )
        cls_positives = lax.all_gather(positives, "dp", axis=1, tiled=True)
        cls_positives = jnp.roll(cls_positives, -index * SEGS, axis=1)[:, :, None]
        cls_ids = jnp.roll(jnp.arange(queries_all, dtype=jnp.int32), -index * SEGS)[None]

    x_low = tokens[0].reshape(ROWS, D)
    seg_rows = segments[0].reshape(MB, L)
    seg_row = seg_rows.reshape(MB, 1, L)
    before = jnp.concatenate([jnp.full((MB, 1), -1, jnp.int32), seg_rows[:, :-1]], axis=1)
    numbers = jnp.where(seg_rows != before, seg_rows, -1)
    numbers = jnp.where(numbers >= 0, numbers + SEGS * jnp.arange(MB)[:, None], -1).reshape(1, ROWS)
    table = (jnp.arange(MB * SEGS)[:, None] == numbers).astype(low_type)
    mixed, context, lse, vec_f = attention_forward(me, mix_quads, x_low, seg_row)
    if fast:
        (up_y, up_core, got_down), mixed, context, lse, vec_f = beside(
            [(up, 2), (up, 1), (down, 4)], mixed, context, lse, vec_f
        )
        down = joined(down, got_down)
        up_quads = (up, up_y, up_core, swapped(up_y, 1))
    normed_one, inverse_one, hidden, active, slope = up_forward(
        me, up_quads, context, x_low, vec_f
    )
    if fast:
        (down_y, down_core), normed_one, hidden, active, slope = beside(
            [(down, 2), (down, 1)], normed_one, hidden, active, slope
        )
        down_quads = (down, down_y, down_core, swapped(down_y, 1))
    normed_two, inverse_two, output, cls_low = down_forward(
        me, down_quads, active, normed_one, vec_f, table
    )

    if fast:
        first = [cls_low] + [across(cls_low, t, m) for t, m in ((0, 8), (1, 0), (1, 8))]
        four = jnp.stack(first).reshape(2, 2, MB, SEGS, D)
        second = [four] + [across(four, 0, m) for m in (4, 2, 6)]
        eight = jnp.stack(second)
        everyone = jnp.stack([eight, across(eight, 0, 1)])
        everyone = jnp.transpose(everyone, (2, 4, 0, 1, 3, 5, 6))
    else:
        both = jnp.concatenate([cls_low, tower_swapped(cls_low)])
        everyone = jnp.roll(lax.all_gather(both, "dp", axis=0, tiled=False), -index, axis=0)
        everyone = jnp.transpose(everyone.reshape(owners, 2, MB, SEGS, D), (1, 2, 0, 3, 4))
    everyone = everyone.reshape(2, MB, queries_all, D)
    grad_cls = contrast_back(flag, everyone, cls_positives, cls_ids)

    residual, grad_ffn, sums_two, keep_down, send_down = down_back(
        me,
        token_grad[0].reshape(ROWS, D),
        grad_cls,
        jnp.concatenate([table] * 3),
        normed_two,
        inverse_two,
        vec_f,
        active,
    )
    if fast:
        (got_down,), residual, grad_ffn = beside([(send_down, 1)], residual, grad_ffn)
        keep_down, send_down = parted(keep_down, got_down)
    grad_one, grad_ctx, sums_one, keep_up, send_up, keep_out, send_out = up_back(
        me,
        up_quads,
        down_quads,
        grad_ffn,
        slope,
        hidden,
        residual,
        normed_one,
        inverse_one,
        context,
        vec_f,
    )
    if fast:
        (got_down,), grad_one, grad_ctx, send_up, send_out = beside(
            [(send_down, 2)], grad_one, grad_ctx, send_up, send_out
        )
        keep_down, send_down = parted(keep_down, got_down)
    if fast:
        (got_up, got_out), grad_ctx = beside([(send_up, 1), (send_out, 1)], grad_ctx)
        keep_up, send_up = parted(keep_up, got_up)
        keep_out, send_out = parted(keep_out, got_out)
    back = partial(attention_back, me, x_low, seg_row, mixed, lse)
    grad_a, sums_a, keep_a, send_a = back(grad_ctx, 0)
    grad_b, sums_b, keep_b, send_b = back(grad_ctx, 1)
    if fast:
        (got_down, got_up), grad_ctx, send_a, send_b = beside(
            [(send_down, 4), (send_up, 2)], grad_ctx, send_a, send_b
        )
        keep_down, send_down = parted(keep_down, got_down)
        keep_up, send_up = parted(keep_up, got_up)
    grad_c, sums_c, keep_c, send_c = back(grad_ctx, 2, sums_a, sums_b, sums_one, sums_two)
    if fast:
        (got_down, got_up, got_out, got_a, got_b), grad_c, send_c = beside(
            [(send_down, 8), (send_up, 4), (send_out, 2), (send_a, 1), (send_b, 1)],
            grad_c,
            send_c,
        )
        share_down = added(keep_down[0], got_down[0])
        keep_up, send_up = parted(keep_up, got_up)
        keep_out, send_out = parted(keep_out, got_out)
        two_a, two_b = parted(keep_a, got_a), parted(keep_b, got_b)
        keep_ab = jnp.concatenate([two_a[0], two_b[0]], axis=1)
        send_ab = jnp.concatenate([two_a[1], two_b[1]], axis=1)
    input_grad = input_back(me, mix_quads, grad_one, (grad_a, grad_b, grad_c))
    if fast:
        (got_up, got_out, got_ab, got_c), input_grad = beside(
            [(send_up, 8), (send_out, 4), (send_ab, 2), (send_c, 1)], input_grad
        )
        share_up = added(keep_up[0], got_up[0])
        keep_out, send_out = parted(keep_out, got_out)
        keep_ab, send_ab = parted(keep_ab, got_ab)
        keep_c, send_c = parted(keep_c, got_c)
        ((got_out, got_ab, got_c),) = beside([(send_out, 8), (send_ab, 4), (send_c, 2)])
        share_out = added(keep_out[0], got_out[0])
        keep_ab, send_ab = parted(keep_ab, got_ab)
        keep_c, send_c = parted(keep_c, got_c)
        ((got_ab, got_c),) = beside([(send_ab, 8), (send_c, 4)])
        share_ab = added(keep_ab[0], got_ab[0])
        keep_c, send_c = parted(keep_c, got_c)
        share_c = added(keep_c[0], swapped(send_c, 8)[0])
        share_vec = lax.dynamic_slice(share_c[48:60], (0, index * share), (12, share))
        shares = (share_down, share_up, share_out, share_ab, share_c, share_vec)
        norm_shares = shares[:4] + (share_c[:48], share_vec)
    else:

        def scattered(matrix):
            return lax.psum_scatter(
                matrix.astype(jnp.float32), "dp", scatter_dimension=0, tiled=True
            )

        mix_blocks = jnp.concatenate(
            [
                whole_rows(keep[:, :48], send[:, :48], 1)
                for keep, send in ((keep_a, send_a), (keep_b, send_b), (keep_c, send_c))
            ]
        )
        bias_mixed = jnp.concatenate([sums_a[:1], sums_b[:1], sums_c[:1]]).reshape(HG, 3, QCOLS)
        grad_vec = jnp.concatenate(
            [
                bias_mixed[:, 0].reshape(1, D),
                bias_mixed[:, 2].reshape(1, D),
                sums_one[4:7],
                sums_one[0:4],
                sums_two[0:3],
            ],
            axis=0,
        )
        shares = (
            scattered(from_heads(mix_blocks)),
            scattered(whole_rows(keep_out, send_out, 1)[0]),
            scattered(from_columns(whole_rows(keep_up, send_up, 4))),
            scattered(whole_rows(keep_down, send_down, 1)[0]),
            lax.psum_scatter(grad_vec, "dp", scatter_dimension=1, tiled=True),
        )
        norm_shares = shares

    local_square = sum(jnp.sum(s * s) for s in norm_shares)
    firsts = (first_mix[0], first_out[0], first_up[0], first_down[0], first_vectors[0])
    seconds = (second_mix[0], second_out[0], second_up[0], second_down[0], second_vectors[0])
    if fast:
        norm = jnp.broadcast_to(local_square, (8, 128))
        norm = (norm + across(norm, 0, 8)) + (across(norm, 1, 0) + across(norm, 1, 8))
        norm = (norm + across(norm, 0, 4)) + (across(norm, 0, 2) + across(norm, 0, 6))
        norm = norm + across(norm, 0, 1)
        grad_square = norm[0, 0]
        arrays = [
            pltpu.with_memory_space_constraint(a, pltpu.HBM) for a in masters + firsts + seconds
        ]
        updated = adam_all(norm, shares, arrays)
        updated = tuple(u[None] for u in updated)
    else:
        grad_square = lax.psum(local_square, ("tower", "dp"))
        factor = jnp.minimum(1.0, clip_norm / (jnp.sqrt(grad_square) + 1e-06))
        rates = (matrix_rate, matrix_rate, matrix_rate, matrix_rate, vector_rate)
        results = [
            adam_update(masters[i], shares[i], firsts[i], seconds[i], rates[i], factor)
            for i in range(5)
        ]
        updated = tuple(r[i] for i in range(3) for r in results)
    return (
        output.reshape(1, MB, 1, L, D),
        input_grad.reshape(1, MB, 1, L, D),
        *updated,
        grad_square,
    )


def solution(mesh):
    rows = P("tower", None, "dp", None, None)
    shards = (P("tower", "dp", None),) * 4 + (P("tower", None, "dp"),)
    in_specs = (rows, P("tower", None, "dp", None), P(None, "dp"), rows) + shards * 3
    out_specs = (rows, rows) + shards * 3 + (P(),)
    return jax.shard_map(body, mesh=mesh, in_specs=in_specs, out_specs=out_specs, check_vma=False)
```

```python
from functools import partial

import jax
import jax.numpy as jnp
from jax import lax
from jax.experimental import pallas as pl
from jax.experimental.pallas import tpu as pltpu
from jax.sharding import PartitionSpec as P

D = 768
FF = 3072
H = 12
HD = 64
L = 512
SEGS = 8
MB = 2
STEP = 5
HG = 3
PIECES = 16
PIECE_ROWS = D // PIECES

norm_eps = 1e-05
attention_scale = 0.125
score_scale = 0.0625
contrast_weight = 16.0
clip_norm = 1.0
beta_first = 0.9
beta_second = 0.999
adam_eps = 1e-08
weight_decay = 0.01
matrix_rate = 0.05
vector_rate = 0.5
masked_score = -1e30

low_type = jnp.bfloat16
highest = lax.Precision.HIGHEST


def swapped(value, mask):
    pairs = [(i, i ^ mask) for i in range(lax.axis_size("dp"))]
    return lax.ppermute(value, "dp", pairs)


def tower_swapped(value):
    return lax.ppermute(value, "tower", [(0, 1), (1, 0)])


def relative_of(place):
    return ((place & 1) << 3) | ((place & 2) << 1) | ((place & 4) >> 1) | (place >> 3)


def relative_y_first(place):
    return ((place & 1) << 1) | ((place & 2) << 2) | (place & 4) | (place >> 3)


def gather_pieces(own):
    pieces = own[None]
    for mask in (8, 4, 2, 1):
        pieces = jnp.concatenate([pieces, swapped(pieces, mask)])
    return pieces


def added(first, second):
    return first.astype(jnp.float32) + second.astype(jnp.float32)


def rows_dot(first_op, second_op):
    return jnp.dot(first_op, second_op, preferred_element_type=jnp.float32)


def contract_rows(first_op, second_op):
    return lax.dot_general(
        first_op, second_op, (((0,), (0,)), ((), ())), preferred_element_type=jnp.float32
    )


def contract_cols(first_op, second_op):
    return lax.dot_general(
        first_op, second_op, (((1,), (1,)), ((), ())), preferred_element_type=jnp.float32
    )


def layer_stats(values):
    centred = values - jnp.mean(values, axis=-1, keepdims=True)
    inverse = lax.rsqrt(jnp.mean(centred * centred, axis=-1, keepdims=True) + norm_eps)
    return (centred * inverse, inverse)


def norm_back(upstream, normed, inverse, gain_row):
    gained = upstream * gain_row
    return inverse * (
        gained
        - jnp.mean(gained, axis=-1, keepdims=True)
        - normed * jnp.mean(gained * normed, axis=-1, keepdims=True)
    )


def column_sum(values):
    return jnp.sum(values.astype(jnp.float32), axis=0, keepdims=True)


def gelu_parts(pre):
    below = 1.0 + (0.3275911 * 0.7071067811865476) * jnp.abs(pre)
    inner = pl.reciprocal(below, approx=True)
    inner = inner * (2.0 - below * inner)
    series = (0.5 * 1.061405429) * inner - (0.5 * 1.453152027)
    series = series * inner + (0.5 * 1.421413741)
    series = series * inner - (0.5 * 0.284496736)
    series = (series * inner + (0.5 * 0.254829592)) * inner
    bell = jnp.exp2(pre * pre * (-0.5 * log2e))
    half_tail = series * bell
    cumulative = jnp.where(pre >= 0.0, 1.0 - half_tail, half_tail)
    return (pre * cumulative, cumulative + pre * (bell * 0.3989422804014327))


log2e = 1.4426950408889634
ROWS = MB * L
QCOLS = D // HG
HEADS = H // HG
any_space = pl.BlockSpec(memory_space=pltpu.HBM)
scalar_space = pl.BlockSpec(memory_space=pltpu.SMEM)
vmem_space = pl.BlockSpec(memory_space=pltpu.VMEM)


def kept_in_hbm(array):
    return pltpu.with_memory_space_constraint(array, pltpu.HBM)


def params(megabytes):
    return pltpu.CompilerParams(vmem_limit_bytes=megabytes * 1024 * 1024)


def cost(flops, moved, exps=0):
    return pl.CostEstimate(flops=int(flops), bytes_accessed=int(moved), transcendentals=int(exps))


def start_pieces(me, quads, target, sem, order=relative_of, at=0):
    count = quads[0].shape[1]
    for place in range(PIECES):
        pltpu.make_async_copy(
            quads[place // 4].at[place % 4],
            target.at[me ^ order(place), pl.ds(at, count), :],
            sem,
        ).start()


def start_up(me, quads, quads_last, target, sem):
    start_pieces(me, quads, target, sem)
    start_pieces(me, quads_last, target, sem, relative_y_first, 4 * PIECE_ROWS)


def up_block_of(pieces, step):
    return block_of(pieces, step + step // 3)


def start_owners(me, source, keep, send, sem):
    for place in range(PIECES):
        held = keep if place < 8 else send
        pltpu.make_async_copy(
            source.at[me ^ relative_of(place)], held.at[place % 8], sem
        ).start()


def block_of(pieces, index):
    at = pl.multiple_of(index * PIECE_ROWS, 16)
    return pieces[:, pl.ds(at, PIECE_ROWS), :].reshape(D, D)


def segment_mask(seg_row):
    numbers = seg_row[...].reshape(1, L)
    columns = jnp.transpose(jnp.broadcast_to(numbers, (8, L)))[:, :1]
    return jnp.where(columns == numbers, 0.0, masked_score)


def wait_bytes(whole, sem):
    pltpu.make_async_copy(whole, whole, sem).wait()


def attention_kernel(
    me_ref, *refs
):
    quads = refs[:4]
    x_ref, seg_row, mixed_ref, ctx_ref, lse_ref, vec_ref, w, mask, bias, sems = refs[4:]
    hg, mb = pl.program_id(0), pl.program_id(1)
    me = me_ref[0]

    @pl.when((hg == 0) & (mb == 0))
    def _():
        start_pieces(me, quads, w, sems.at[0])

    @pl.when(hg == 0)
    def _():
        mask[mb] = segment_mask(seg_row)

    @pl.when((hg == 0) & (mb == 0))
    def _():
        wait_bytes(w, sems.at[0])
        vec = w[0, HG * PIECE_ROWS :, :].astype(jnp.float32)
        for place in range(1, PIECES):
            vec = vec + w[place, HG * PIECE_ROWS :, :].astype(jnp.float32)
        vec_ref[...] = vec
        for group in range(HG):
            columns = slice(group * QCOLS, (group + 1) * QCOLS)
            none = jnp.zeros((1, QCOLS), jnp.float32)
            bias[group] = jnp.concatenate([vec[0:1, columns], none, vec[1:2, columns]], axis=1)

    mixed = (rows_dot(x_ref[...], block_of(w, hg)) + bias[hg]).astype(low_type)
    mixed_ref[...] = mixed.reshape(mixed_ref.shape)
    v_t = jnp.transpose(mixed[:, 2 * QCOLS :])
    outs, totals = [], []

    def scores_of(head):
        here = slice(head * HD, (head + 1) * HD)
        q, k = mixed[:, here], mixed[:, QCOLS + head * HD : QCOLS + (head + 1) * HD]
        return contract_cols(k, q)

    ahead = scores_of(0)
    for head in range(HEADS):
        here = slice(head * HD, (head + 1) * HD)
        scores = ahead * (attention_scale * log2e) + mask[mb]
        if head + 1 < HEADS:
            ahead = scores_of(head + 1)
        largest = jnp.max(scores, axis=0, keepdims=True)
        expo = jnp.exp2(scores - largest)
        summed = jnp.sum(expo, axis=0, keepdims=True)
        probs = expo.astype(low_type)
        outs.append((rows_dot(v_t[here], probs) * (1.0 / summed)).astype(low_type))
        totals.append(largest + jnp.log(summed) * log2e)
    ctx_ref[...] = jnp.transpose(jnp.concatenate(outs, axis=0))
    lse_ref[...] = jnp.concatenate(totals, axis=0).reshape(lse_ref.shape)


def attention_forward(me, quads, x_low, seg_row):
    return pl.pallas_call(
        attention_kernel,
        grid=(HG, MB),
        in_specs=[
            scalar_space,
            *[any_space] * 4,
            pl.BlockSpec((L, D), lambda g, m: (m, 0)),
            pl.BlockSpec((1, 1, L), lambda g, m: (m, 0, 0)),
        ],
        out_specs=[
            pl.BlockSpec((1, L, D), lambda g, m: (g, m, 0)),
            pl.BlockSpec((L, QCOLS), lambda g, m: (m, g)),
            pl.BlockSpec((1, HEADS, L), lambda g, m: (g * MB + m, 0, 0)),
            pl.BlockSpec((16, D), lambda g, m: (0, 0)),
        ],
        out_shape=[
            jax.ShapeDtypeStruct((HG, ROWS, D), low_type),
            jax.ShapeDtypeStruct((ROWS, D), low_type),
            jax.ShapeDtypeStruct((HG * MB, HEADS, L), jnp.float32),
            jax.ShapeDtypeStruct((16, D), jnp.float32),
        ],
        scratch_shapes=[
            pltpu.VMEM((PIECES, HG * PIECE_ROWS + 16, D), low_type),
            pltpu.VMEM((MB, L, L), jnp.float32),
            pltpu.VMEM((HG, 1, D), jnp.float32),
            pltpu.SemaphoreType.DMA((1,)),
        ],
        compiler_params=params(40),
        cost_estimate=cost(2 * ROWS * D * 3 * D + 8 * MB * H * L * L * HD, 12e6, MB * H * L * L),
        name="mixed_attention",
    )(me, *quads, x_low, seg_row)


def up_kernel(
    me_ref,
    quad_0,
    quad_1,
    quad_2,
    quad_3,
    last_0,
    last_1,
    last_2,
    last_3,
    ctx_hbm,
    x_hbm,
    vec,
    normed_hbm,
    inverse_ref,
    hidden_hbm,
    active_ref,
    slope_ref,
    w,
    ctx,
    x,
    normed,
    hidden,
    sems,
):
    step = pl.program_id(0)
    me = me_ref[0]
    quads, quads_last = (quad_0, quad_1, quad_2, quad_3), (last_0, last_1, last_2, last_3)
    ctx_in = pltpu.make_async_copy(ctx_hbm, ctx, sems.at[1])
    x_in = pltpu.make_async_copy(x_hbm, x, sems.at[2])
    normed_out = pltpu.make_async_copy(normed, normed_hbm, sems.at[3])
    hidden_out = pltpu.make_async_copy(hidden, hidden_hbm, sems.at[4])

    @pl.when(step == 0)
    def _():
        start_up(me, quads, quads_last, w, sems.at[0])
        ctx_in.start()
        x_in.start()
        wait_bytes(w, sems.at[0])
        ctx_in.wait()
        x_in.wait()
        for first in range(0, ROWS, 256):
            part = slice(first, first + 256)
            branch = rows_dot(ctx[part, :], block_of(w, 3)) + vec[2:3, :]
            n, inv = layer_stats(x[part, :].astype(jnp.float32) + branch)
            normed[part, :] = n
            inverse_ref[part, :] = inv
            hidden[part, :] = (n * vec[3:4, :] + vec[4:5, :]).astype(low_type)
        normed_out.start()
        hidden_out.start()

    bias = vec[pl.ds(5 + step, 1), :]
    for first in range(0, ROWS, 256):
        part = slice(first, first + 256)
        pre = rows_dot(hidden[part, :], up_block_of(w, step)) + bias
        active, slope = gelu_parts(pre)
        active_ref[part, :] = active.astype(low_type)
        slope_ref[part, :] = slope.astype(low_type)

    @pl.when(step == 3)
    def _():
        normed_out.wait()
        hidden_out.wait()


def up_forward(me, quads, quads_last, context, x_low, vec):
    return pl.pallas_call(
        up_kernel,
        grid=(4,),
        in_specs=[scalar_space, *[any_space] * 10, vmem_space],
        out_specs=[
            any_space,
            pl.BlockSpec((ROWS, 1), lambda s: (0, 0)),
            any_space,
            pl.BlockSpec((ROWS, D), lambda s: (0, s)),
            pl.BlockSpec((ROWS, D), lambda s: (0, s)),
        ],
        out_shape=[
            jax.ShapeDtypeStruct((ROWS, D), jnp.float32),
            jax.ShapeDtypeStruct((ROWS, 1), jnp.float32),
            jax.ShapeDtypeStruct((ROWS, D), low_type),
            jax.ShapeDtypeStruct((ROWS, FF), low_type),
            jax.ShapeDtypeStruct((ROWS, FF), low_type),
        ],
        scratch_shapes=[
            pltpu.VMEM((PIECES, 5 * PIECE_ROWS, D), low_type),
            pltpu.VMEM((ROWS, D), low_type),
            pltpu.VMEM((ROWS, D), low_type),
            pltpu.VMEM((ROWS, D), jnp.float32),
            pltpu.VMEM((ROWS, D), low_type),
            pltpu.SemaphoreType.DMA((5,)),
        ],
        compiler_params=params(44),
        cost_estimate=cost(2 * ROWS * D * (FF + D), 24e6, 2 * ROWS * FF),
        name="out_up",
    )(me, *quads, *quads_last, context, x_low, vec)


def down_kernel(
    me_ref,
    quad_0,
    quad_1,
    quad_2,
    quad_3,
    active_hbm,
    normed_one_hbm,
    vec,
    table_ref,
    normed_ref,
    inverse_ref,
    output_ref,
    cls_ref,
    w,
    active,
    normed_one_ref,
    sems,
):
    me = me_ref[0]
    start_pieces(me, (quad_0, quad_1, quad_2, quad_3), w, sems.at[0])
    copies = []
    for index in range(4):
        part = pl.ds(index * 256, 256)
        copies.append(
            pltpu.make_async_copy(active_hbm.at[part, :], active.at[part, :], sems.at[1 + index])
        )
        copies[-1].start()
    normed_one_in = pltpu.make_async_copy(normed_one_hbm, normed_one_ref, sems.at[5])
    normed_one_in.start()
    wait_bytes(w, sems.at[0])
    for index in range(4):
        copies[index].wait()
        part = slice(index * 256, (index + 1) * 256)
        if index == 0:
            normed_one_in.wait()
        ffn = rows_dot(active[part, :], w[...].reshape(FF, D)) + vec[9:10, :]
        residual = normed_one_ref[part, :] * vec[3:4, :] + vec[4:5, :]
        n, inv = layer_stats(residual + ffn)
        normed_ref[part, :] = n
        inverse_ref[part, :] = inv
        output_ref[part, :] = (n * vec[10:11, :] + vec[11:12, :]).astype(low_type)
    cls_ref[...] = rows_dot(table_ref[...], output_ref[...]).astype(low_type)


def down_forward(me, quads, active, normed_one, vec, table):
    return pl.pallas_call(
        down_kernel,
        in_specs=[scalar_space, *[any_space] * 6, vmem_space, vmem_space],
        out_specs=[vmem_space] * 4,
        out_shape=[
            jax.ShapeDtypeStruct((ROWS, D), jnp.float32),
            jax.ShapeDtypeStruct((ROWS, 1), jnp.float32),
            jax.ShapeDtypeStruct((ROWS, D), low_type),
            jax.ShapeDtypeStruct((MB * SEGS, D), low_type),
        ],
        scratch_shapes=[
            pltpu.VMEM((PIECES, 4 * PIECE_ROWS, D), low_type),
            pltpu.VMEM((ROWS, FF), low_type),
            pltpu.VMEM((ROWS, D), jnp.float32),
            pltpu.SemaphoreType.DMA((6,)),
        ],
        compiler_params=params(40),
        cost_estimate=cost(2 * ROWS * D * FF, 19e6),
        name="down",
    )(me, *quads, active, normed_one, vec, table)


def contrast_kernel(flag_ref, all_ref, positive_ref, ids_ref, grad_ref):
    passage_here = flag_ref[0] == 1
    for batch in range(MB):
        mine, theirs = all_ref[0, batch], all_ref[1, batch]
        queries = jnp.where(passage_here, theirs, mine)
        passages = jnp.where(passage_here, mine, theirs)
        contrast = contract_cols(queries, passages) * score_scale
        top = jnp.max(contrast, axis=-1, keepdims=True)
        expo = jnp.exp(contrast - top)
        probs = expo / jnp.sum(expo, axis=-1, keepdims=True)
        chosen = (positive_ref[batch] == ids_ref[...]).astype(jnp.float32)
        grad = (contrast_weight * (probs - chosen)).astype(low_type)
        for_query = rows_dot(grad[:16], passages) * score_scale
        for_query = for_query.astype(low_type).astype(jnp.float32)
        for_passage = contract_rows(grad, queries)[:16] * score_scale
        taken = jnp.where(passage_here, for_passage, for_query)
        grad_ref[batch * SEGS : (batch + 1) * SEGS, :] = taken[:SEGS]


def contrast_back(flag, everyone, cls_positives, cls_ids):
    return pl.pallas_call(
        contrast_kernel,
        in_specs=[scalar_space, vmem_space, vmem_space, vmem_space],
        out_specs=vmem_space,
        out_shape=jax.ShapeDtypeStruct((MB * SEGS, D), jnp.float32),
        compiler_params=params(48),
        name="contrast",
    )(flag, everyone, cls_positives, cls_ids)


def down_back_kernel(
    me_ref,
    token_grad,
    grad_cls,
    table3_ref,
    normed_ref,
    inverse_ref,
    vec,
    active_ref,
    residual_ref,
    low_ref,
    sums_ref,
    keep,
    send,
    low,
    staged,
    sem,
):
    step = pl.program_id(0)

    @pl.when(step == 0)
    def _():
        grads = grad_cls[...]
        upper = grads.astype(low_type)
        rest = grads - upper.astype(jnp.float32)
        middle = rest.astype(low_type)
        lower = (rest - middle.astype(jnp.float32)).astype(low_type)
        stacked = jnp.concatenate([upper, middle, lower], axis=0)
        gains = jnp.zeros((1, D), jnp.float32)
        shifts = jnp.zeros((1, D), jnp.float32)
        biases = jnp.zeros((1, D), jnp.float32)
        for first in range(0, ROWS, 256):
            part = slice(first, first + 256)
            upstream = token_grad[part, :] + contract_rows(table3_ref[:, part], stacked)
            n = normed_ref[part, :]
            gains = gains + column_sum(upstream * n)
            shifts = shifts + column_sum(upstream)
            grad = norm_back(upstream, n, inverse_ref[part, :], vec[10:11, :])
            residual_ref[part, :] = grad
            rounded = grad.astype(low_type)
            biases = biases + column_sum(rounded)
            low[part, :] = rounded
        low_ref[...] = low[...]
        sums_ref[...] = jnp.concatenate([biases, gains, shifts, jnp.zeros((5, D), jnp.float32)])

    for first in range(4):
        at = first * 4 * PIECE_ROWS
        staged[4 * step + first] = contract_rows(
            active_ref[:, at : at + 4 * PIECE_ROWS], low[...]
        ).astype(low_type)

    @pl.when(step == 3)
    def _():
        start_owners(me_ref[0], staged, keep, send, sem)
        wait_bytes(staged, sem)


def down_back(me, token_grad, grad_cls, table3, normed, inverse, vec, active):
    half = jax.ShapeDtypeStruct((8, 4 * PIECE_ROWS, D), low_type)
    return pl.pallas_call(
        down_back_kernel,
        grid=(4,),
        in_specs=[scalar_space]
        + [vmem_space] * 6
        + [pl.BlockSpec((ROWS, D), lambda s: (0, s))],
        out_specs=[vmem_space] * 3 + [any_space] * 2,
        out_shape=[
            jax.ShapeDtypeStruct((ROWS, D), jnp.float32),
            jax.ShapeDtypeStruct((ROWS, D), low_type),
            jax.ShapeDtypeStruct((8, D), jnp.float32),
            half,
            half,
        ],
        scratch_shapes=[
            pltpu.VMEM((ROWS, D), low_type),
            pltpu.VMEM((PIECES, 4 * PIECE_ROWS, D), low_type),
            pltpu.SemaphoreType.DMA,
        ],
        compiler_params=params(48),
        cost_estimate=cost(2 * ROWS * D * FF, 25e6),
        name="down_back",
    )(me, token_grad, grad_cls, table3, normed, inverse, vec, active)


def up_back_kernel(
    me_ref,
    up_0,
    up_1,
    up_2,
    up_3,
    last_0,
    last_1,
    last_2,
    last_3,
    down_0,
    down_1,
    down_2,
    down_3,
    low_ref,
    slope_ref,
    hidden_ref,
    residual_hbm,
    normed_hbm,
    inverse_ref,
    ctx_hbm,
    vec,
    grad_one_ref,
    grad_ctx_ref,
    sums_ref,
    keep,
    send,
    keep_out,
    send_out,
    up_w,
    down_w,
    normed,
    ctx,
    total,
    staged,
    staged_out,
    bias_sums,
    sems,
):
    step = pl.program_id(0)
    me = me_ref[0]
    residual_in = pltpu.make_async_copy(residual_hbm, total, sems.at[2])
    normed_in = pltpu.make_async_copy(normed_hbm, normed, sems.at[3])
    ctx_in = pltpu.make_async_copy(ctx_hbm, ctx, sems.at[4])

    @pl.when(step == 0)
    def _():
        start_pieces(me, (down_0, down_1, down_2, down_3), down_w, sems.at[0])
        last = (last_0, last_1, last_2, last_3)
        start_up(me, (up_0, up_1, up_2, up_3), last, up_w, sems.at[1])
        residual_in.start()
        normed_in.start()
        ctx_in.start()
        wait_bytes(down_w, sems.at[0])
        wait_bytes(up_w, sems.at[1])
        residual_in.wait()

    down_block = down_w[pl.ds(4 * step, 4)].reshape(D, D)
    up_block = up_block_of(up_w, step)
    grads = []
    biases = jnp.zeros((1, D), jnp.float32)
    for first in range(0, ROWS, 256):
        part = slice(first, first + 256)
        active_grad = contract_cols(low_ref[part, :], down_block)
        grad = (active_grad * slope_ref[part, :].astype(jnp.float32)).astype(low_type)
        biases = biases + column_sum(grad)
        grads.append(grad)
        total[part, :] += contract_cols(grad, up_block)

    grad = jnp.concatenate(grads, axis=0)
    at = pl.multiple_of(step * PIECE_ROWS, 16)
    for first in range(0, PIECES, 4):
        columns = slice(first * PIECE_ROWS, (first + 4) * PIECE_ROWS)
        terms = contract_rows(hidden_ref[:, columns], grad).astype(low_type)
        staged[first : first + 4, pl.ds(at, PIECE_ROWS), :] = terms.reshape(4, PIECE_ROWS, D)
    bias_sums[step] = biases

    @pl.when(step == 3)
    def _():
        start_owners(me, staged, keep, send, sems.at[5])
        normed_in.wait()
        ctx_in.wait()
        gains = jnp.zeros((1, D), jnp.float32)
        shifts = jnp.zeros((1, D), jnp.float32)
        out_biases = jnp.zeros((1, D), jnp.float32)
        lows = []
        for first in range(0, ROWS, 256):
            part = slice(first, first + 256)
            upstream = total[part, :]
            n = normed[part, :]
            gains = gains + column_sum(upstream * n)
            shifts = shifts + column_sum(upstream)
            grad_one = norm_back(upstream, n, inverse_ref[part, :], vec[3:4, :])
            grad_one_ref[part, :] = grad_one
            rounded = grad_one.astype(low_type)
            out_biases = out_biases + column_sum(rounded)
            grad_ctx_ref[part, :] = contract_cols(rounded, block_of(up_w, 3)).astype(low_type)
            lows.append(rounded)
        sums_ref[...] = jnp.concatenate(
            [bias_sums[block] for block in range(4)]
            + [out_biases, gains, shifts, jnp.zeros((1, D), jnp.float32)]
        )
        rounded = jnp.concatenate(lows, axis=0)
        for first in range(0, PIECES, 4):
            columns = slice(first * PIECE_ROWS, (first + 4) * PIECE_ROWS)
            terms = contract_rows(ctx[:, columns], rounded).astype(low_type)
            staged_out[first : first + 4] = terms.reshape(4, PIECE_ROWS, D)
        start_owners(me, staged_out, keep_out, send_out, sems.at[6])
        wait_bytes(staged, sems.at[5])
        wait_bytes(staged_out, sems.at[6])


def up_back(
    me, up_quads, up_last, down_quads, low, slope, hidden, residual, normed, inverse, ctx, vec
):
    half = jax.ShapeDtypeStruct((8, 4 * PIECE_ROWS, D), low_type)
    half_out = jax.ShapeDtypeStruct((8, PIECE_ROWS, D), low_type)
    return pl.pallas_call(
        up_back_kernel,
        grid=(4,),
        in_specs=[scalar_space]
        + [any_space] * 12
        + [
            vmem_space,
            pl.BlockSpec((ROWS, D), lambda s: (0, s)),
            vmem_space,
            any_space,
            any_space,
            vmem_space,
            any_space,
            vmem_space,
        ],
        out_specs=[vmem_space] * 3 + [any_space] * 4,
        out_shape=[
            jax.ShapeDtypeStruct((ROWS, D), jnp.float32),
            jax.ShapeDtypeStruct((ROWS, D), low_type),
            jax.ShapeDtypeStruct((8, D), jnp.float32),
            half,
            half,
            half_out,
            half_out,
        ],
        scratch_shapes=[
            pltpu.VMEM((PIECES, 5 * PIECE_ROWS, D), low_type),
            pltpu.VMEM((PIECES, 4 * PIECE_ROWS, D), low_type),
            pltpu.VMEM((ROWS, D), jnp.float32),
            pltpu.VMEM((ROWS, D), low_type),
            pltpu.VMEM((ROWS, D), jnp.float32),
            pltpu.VMEM((PIECES, 4 * PIECE_ROWS, D), low_type),
            pltpu.VMEM((PIECES, PIECE_ROWS, D), low_type),
            pltpu.VMEM((4, 1, D), jnp.float32),
            pltpu.SemaphoreType.DMA((7,)),
        ],
        compiler_params=params(56),
        cost_estimate=cost(2 * ROWS * D * (3 * FF + 2 * D), 40e6),
        name="up_back",
    )(
        me,
        *up_quads,
        *up_last,
        *down_quads,
        low,
        slope,
        hidden,
        residual,
        normed,
        inverse,
        ctx,
        vec,
    )


def attention_back_kernel(
    me_ref,
    x_ref,
    seg_row,
    mixed_ref,
    lse_ref,
    grad_ctx_ref,
    *refs,
):
    others, (grad_mixed_ref, sums_ref, keep, send, weight_grad, staged, sem) = refs[:-7], refs[-7:]
    mb = pl.program_id(0)
    me = me_ref[0]
    mask = segment_mask(seg_row)
    mixed = mixed_ref[...].reshape(L, D)
    lse = lse_ref[...].reshape(HEADS, L)
    k_t = jnp.transpose(mixed[:, QCOLS : 2 * QCOLS])
    grad_q, grad_k, grad_v = [], [], []

    def products_of(head):
        here = slice(head * HD, (head + 1) * HD)
        q, k = mixed[:, here], mixed[:, QCOLS + head * HD : QCOLS + (head + 1) * HD]
        v = mixed[:, 2 * QCOLS + head * HD : 2 * QCOLS + (head + 1) * HD]
        return (contract_cols(k, q), contract_cols(v, grad_ctx_ref[:, here]))

    ahead = products_of(0)
    for head in range(HEADS):
        here = slice(head * HD, (head + 1) * HD)
        scores, grad_probs = ahead
        if head + 1 < HEADS:
            ahead = products_of(head + 1)
        scores = scores * (attention_scale * log2e) + mask
        probs = jnp.exp2(scores - lse[head : head + 1])
        inner = jnp.sum(probs * grad_probs, axis=0, keepdims=True)
        grad_scores = (probs * (grad_probs - inner)).astype(low_type)
        grad_v.append(rows_dot(probs.astype(low_type), grad_ctx_ref[:, here]).astype(low_type))
        grad_q.append((rows_dot(k_t[here], grad_scores) * attention_scale).astype(low_type))
        grad_k.append((rows_dot(grad_scores, mixed[:, here]) * attention_scale).astype(low_type))
    grad_mixed = jnp.concatenate(
        [jnp.transpose(jnp.concatenate(grad_q, axis=0))] + grad_k + grad_v, axis=1
    )

    grad_mixed_ref[...] = grad_mixed
    bias = column_sum(grad_mixed)
    terms = contract_rows(x_ref[...], grad_mixed)

    @pl.when(mb == 0)
    def _():
        weight_grad[...] = terms
        sums_ref[0:1, :] = bias

    @pl.when(mb == 1)
    def _():
        sums_ref[0:1, :] += bias
        grads = (weight_grad[...] + terms).astype(low_type)
        staged[:, :PIECE_ROWS, :] = grads.reshape(PIECES, PIECE_ROWS, D)
        if others:
            mixed_a, mixed_b, up, down = (other[...] for other in others)
            mixed_sums = (mixed_a[0:1], mixed_b[0:1], sums_ref[0:1, :])
            vectors = jnp.concatenate(
                [
                    jnp.concatenate([s[:, :QCOLS] for s in mixed_sums], axis=1),
                    jnp.concatenate([s[:, 2 * QCOLS :] for s in mixed_sums], axis=1),
                    up[4:7],
                    up[0:4],
                    down[0:3],
                    jnp.zeros((4, D), jnp.float32),
                ],
                axis=0,
            )
            for place in range(PIECES):
                staged[place, PIECE_ROWS:, :] = vectors.astype(low_type)
        start_owners(me, staged, keep, send, sem)
        wait_bytes(staged, sem)


def attention_back(me, x_low, seg_row, mixed, lse, grad_ctx, group, *others):
    rows = PIECE_ROWS + (16 if others else 0)
    half = jax.ShapeDtypeStruct((8, rows, D), low_type)
    return pl.pallas_call(
        attention_back_kernel,
        grid=(MB,),
        in_specs=[
            scalar_space,
            pl.BlockSpec((L, D), lambda m: (m, 0)),
            pl.BlockSpec((1, 1, L), lambda m: (m, 0, 0)),
            pl.BlockSpec((1, L, D), lambda m: (group, m, 0)),
            pl.BlockSpec((1, HEADS, L), lambda m: (group * MB + m, 0, 0)),
            pl.BlockSpec((L, QCOLS), lambda m: (m, group)),
            *[vmem_space] * len(others),
        ],
        out_specs=[pl.BlockSpec((L, D), lambda m: (m, 0)), vmem_space, any_space, any_space],
        out_shape=[
            jax.ShapeDtypeStruct((ROWS, D), low_type),
            jax.ShapeDtypeStruct((8, D), jnp.float32),
            half,
            half,
        ],
        scratch_shapes=[
            pltpu.VMEM((D, D), jnp.float32),
            pltpu.VMEM((PIECES, rows, D), low_type),
            pltpu.SemaphoreType.DMA,
        ],
        compiler_params=params(40),
        cost_estimate=cost(
            2 * ROWS * D * D + 20 * MB * HEADS * L * L * HD, 12e6, MB * HEADS * L * L
        ),
        name=f"attention_back_{group}",
    )(me, x_low, seg_row, kept_in_hbm(mixed), lse, grad_ctx, *others)


def input_back_kernel(
    me_ref, quad_0, quad_1, quad_2, quad_3, one_ref, grad_0, grad_1, grad_2, input_ref, w, sem
):
    @pl.when(pl.program_id(0) == 0)
    def _():
        start_pieces(me_ref[0], (quad_0, quad_1, quad_2, quad_3), w, sem)
        wait_bytes(w, sem)

    total = one_ref[...]
    for block, grad in enumerate((grad_0, grad_1, grad_2)):
        total = total + contract_cols(grad[...], block_of(w, block))
    input_ref[...] = total


def input_back(me, quads, grad_one, grads):
    rows = pl.BlockSpec((256, D), lambda s: (s, 0))
    return pl.pallas_call(
        input_back_kernel,
        grid=(ROWS // 256,),
        in_specs=[scalar_space] + [any_space] * 4 + [rows] * 4,
        out_specs=rows,
        out_shape=jax.ShapeDtypeStruct((ROWS, D), jnp.float32),
        scratch_shapes=[
            pltpu.VMEM((PIECES, HG * PIECE_ROWS + 16, D), low_type),
            pltpu.SemaphoreType.DMA,
        ],
        compiler_params=params(24),
        cost_estimate=cost(6 * ROWS * D * D, 14e6),
        name="input_back",
    )(me, *quads, grad_one, *grads)


def adam_kernel(norm_ref, down_ref, up_ref, out_mix, mix_bc, vec_ref, *refs):
    ins, outs, held, sems = refs[:15], refs[15:30], refs[30:45], refs[45]
    arrivals = [
        pltpu.make_async_copy(ins[i], held[i], sems.at[i]) for i in range(15)
    ]
    departures = [
        pltpu.make_async_copy(held[i], outs[i], sems.at[i]) for i in range(15)
    ]
    order = (3, 2, 0, 1, 4)
    for index in order:
        for i in (index, 5 + index, 10 + index):
            arrivals[i].start()
    factor = jnp.minimum(1.0, clip_norm / (jnp.sqrt(norm_ref[0:1, 0:1]) + 1e-06))

    def update(index, columns, grad, rate):
        master, first, second = held[index], held[5 + index], held[10 + index]
        clipped = grad * factor
        first_new = beta_first * first[:, columns] + (1.0 - beta_first) * clipped
        second_new = beta_second * second[:, columns] + (1.0 - beta_second) * clipped * clipped
        root = jnp.sqrt(second_new / (1.0 - beta_second**STEP)) + adam_eps
        step = first_new / (1.0 - beta_first**STEP) / root
        old = master[:, columns]
        master[:, columns] = old - rate * (step + weight_decay * old)
        first[:, columns] = first_new
        second[:, columns] = second_new

    for index in order:
        for i in (index, 5 + index, 10 + index):
            arrivals[i].wait()
        if index == 0:
            one, two = PIECE_ROWS, 2 * PIECE_ROWS
            parts = (out_mix[one:two, :], mix_bc[:one, :], mix_bc[one:two, :])
            for group, share in enumerate(parts):
                for third in range(3):
                    at = third * D + group * QCOLS
                    grad = share[:, third * QCOLS : (third + 1) * QCOLS]
                    update(0, slice(at, at + QCOLS), grad, matrix_rate)
        elif index == 1:
            update(1, slice(0, D), out_mix[:PIECE_ROWS, :], matrix_rate)
        elif index == 2:
            for block in range(4):
                grad = up_ref[block * PIECE_ROWS : (block + 1) * PIECE_ROWS, :]
                update(2, slice(block * D, (block + 1) * D), grad, matrix_rate)
        elif index == 3:
            update(3, slice(0, D), down_ref[...], matrix_rate)
        else:
            update(4, slice(0, PIECE_ROWS), vec_ref[...], vector_rate)
        for i in (index, 5 + index, 10 + index):
            departures[i].start()
    for departure in departures:
        departure.wait()


def adam_all(norm, shares, arrays):
    return pl.pallas_call(
        adam_kernel,
        in_specs=[vmem_space] * 6 + [any_space] * 15,
        out_specs=[any_space] * 15,
        out_shape=[jax.ShapeDtypeStruct(a.shape, jnp.float32) for a in arrays],
        scratch_shapes=[pltpu.VMEM(a.shape, jnp.float32) for a in arrays]
        + [pltpu.SemaphoreType.DMA((15,))],
        compiler_params=params(40),
        cost_estimate=cost(40e6, 25e6),
        name="adam",
    )(norm, *shares, *arrays)


def by_heads(matrix):
    shaped = matrix.reshape(matrix.shape[0], 3, HG, D // HG)
    return jnp.transpose(shaped, (2, 0, 1, 3)).reshape(HG, matrix.shape[0], D)


def from_heads(blocks):
    rows = blocks.shape[1]
    shaped = blocks.reshape(HG, rows, 3, D // HG)
    return jnp.transpose(shaped, (1, 2, 0, 3)).reshape(rows, 3 * D)


def by_columns(matrix):
    return jnp.transpose(matrix.reshape(matrix.shape[0], 4, D), (1, 0, 2))


def from_columns(blocks):
    return jnp.transpose(blocks, (1, 0, 2)).reshape(blocks.shape[1], 4 * D)


def adam_update(master, grad_share, first, second, rate, factor):
    clipped = grad_share * factor
    first_new = beta_first * first + (1.0 - beta_first) * clipped
    second_new = beta_second * second + (1.0 - beta_second) * clipped * clipped
    first_hat = first_new / (1.0 - beta_first**STEP)
    second_hat = second_new / (1.0 - beta_second**STEP)
    master_new = master - rate * (
        first_hat / (jnp.sqrt(second_hat) + adam_eps) + weight_decay * master
    )
    return (master_new[None], first_new[None], second_new[None])


def quads_of(matrix_rows):
    k = matrix_rows.shape[0]
    shaped = matrix_rows.reshape(k, 2, 2, 2, 2, -1, D)
    pieces = jnp.transpose(shaped, (4, 3, 2, 1, 0, 5, 6)).reshape(4, 4, -1, D)
    return tuple(pieces[i] for i in range(4))


def whole_rows(keep, send, k):
    shaped = jnp.concatenate([keep, send]).reshape(2, 2, 2, 2, k, -1, D)
    return jnp.transpose(shaped, (4, 3, 2, 1, 0, 5, 6)).reshape(k, -1, D)


def beside(sends, *work):
    received = [swapped(value, mask) for value, mask in sends]
    done = lax.optimization_barrier((received, work))
    return (done[0], *done[1])


def across(value, tower_mask, dp_mask):
    owners = lax.axis_size("dp")
    flip = tower_mask * owners + dp_mask
    pairs = [(i, i ^ flip) for i in range(2 * owners)]
    return lax.ppermute(value, ("tower", "dp"), pairs)


def joined(pieces, received):
    return jnp.concatenate([pieces, received])


def parted(keep, received):
    half = keep.shape[0] // 2
    return (
        added(keep[:half], received[:half]).astype(low_type),
        added(keep[half:], received[half:]).astype(low_type),
    )


def body(
    tokens,
    segments,
    positives,
    token_grad,
    mix_weight,
    out_weight,
    up_weight,
    down_weight,
    vectors,
    first_mix,
    first_out,
    first_up,
    first_down,
    first_vectors,
    second_mix,
    second_out,
    second_up,
    second_down,
    second_vectors,
):
    owners = lax.axis_size("dp")
    fast = owners == PIECES
    index = lax.axis_index("dp")
    flag = lax.axis_index("tower").astype(jnp.int32).reshape(1)
    masters = (mix_weight[0], out_weight[0], up_weight[0], down_weight[0], vectors[0])
    low_mix, low_out, low_up, low_down, low_vec = (m.astype(low_type) for m in masters)
    share = low_vec.shape[1]
    queries_all = owners * SEGS

    if fast:
        me = index.astype(jnp.int32).reshape(1)
        extra = jnp.zeros((16, D), low_type)
        extra = extra.at[12:14, :SEGS].set(positives.astype(low_type))
        extra = lax.dynamic_update_slice(extra, low_vec, (0, index * share))
        pack_mix = jnp.concatenate([by_heads(low_mix).reshape(-1, D), extra])
        low_blocks = by_columns(low_up)
        pack_up = jnp.concatenate([low_blocks[:3].reshape(-1, D), low_out])
        mix, up, last, down = pack_mix[None], pack_up[None], low_blocks[3:], low_down[None]
        ((got_mix, got_last),) = beside([(mix, 8), (last, 2)])
        mix, last = joined(mix, got_mix), joined(last, got_last)
        ((got_mix, got_up),) = beside([(mix, 4), (up, 8)])
        mix, up = joined(mix, got_mix), joined(up, got_up)
        ((mix_y, mix_core, got_up, got_last, got_down),) = beside(
            [(mix, 2), (mix, 1), (up, 4), (last, 8), (down, 8)]
        )
        up, last, down = joined(up, got_up), joined(last, got_last), joined(down, got_down)
        mix_quads = (mix, mix_y, mix_core, swapped(mix_y, 1))
        extras = jnp.concatenate([quad[:, 156:158, :SEGS] for quad in mix_quads])
        cls_positives = jnp.transpose(extras.astype(jnp.int32), (1, 0, 2))
        cls_positives = cls_positives.reshape(MB, queries_all, 1)
        relative = relative_of(jnp.arange(PIECES, dtype=jnp.int32))
        cls_ids = ((relative ^ index)[:, None] * SEGS + jnp.arange(SEGS)[None, :]).reshape(1, -1)
    else:
        me = jnp.zeros((1,), jnp.int32)
        mix_quads = quads_of(by_heads(lax.all_gather(low_mix, "dp", axis=0, tiled=True)))
        up_blocks = by_columns(lax.all_gather(low_up, "dp", axis=0, tiled=True))
        out_block = lax.all_gather(low_out, "dp", axis=0, tiled=True)[None]
        up_quads = quads_of(jnp.concatenate([up_blocks[:3], out_block]))
        up_last = jnp.concatenate(quads_of(up_blocks[3:]))
        up_last = jnp.stack(
            [up_last[relative_of(relative_y_first(place))] for place in range(PIECES)]
        ).reshape(4, 4, PIECE_ROWS, D)
        up_last = tuple(up_last[i] for i in range(4))
        down_quads = quads_of(lax.all_gather(low_down, "dp", axis=0, tiled=True)[None])
        vec_low = lax.all_gather(low_vec, "dp", axis=1, tiled=True)
        extra = jnp.zeros((PIECES, 16, D), low_type).at[0, :12].set(vec_low)
        mix_quads = tuple(
            jnp.concatenate([quad, extra[4 * i : 4 * i + 4]], axis=1)
            for i, quad in enumerate(mix_quads)
        )
        cls_positives = lax.all_gather(positives, "dp", axis=1, tiled=True)
        cls_positives = jnp.roll(cls_positives, -index * SEGS, axis=1)[:, :, None]
        cls_ids = jnp.roll(jnp.arange(queries_all, dtype=jnp.int32), -index * SEGS)[None]

    x_low = tokens[0].reshape(ROWS, D)
    seg_rows = segments[0].reshape(MB, L)
    seg_row = seg_rows.reshape(MB, 1, L)
    before = jnp.concatenate([jnp.full((MB, 1), -1, jnp.int32), seg_rows[:, :-1]], axis=1)
    numbers = jnp.where(seg_rows != before, seg_rows, -1)
    numbers = jnp.where(numbers >= 0, numbers + SEGS * jnp.arange(MB)[:, None], -1).reshape(1, ROWS)
    table = (jnp.arange(MB * SEGS)[:, None] == numbers).astype(low_type)
    mixed, context, lse, vec_f = attention_forward(me, mix_quads, x_low, seg_row)
    if fast:
        (up_y, up_core, last_z, last_core, got_down), mixed, context, lse, vec_f = beside(
            [(up, 2), (up, 1), (last, 4), (last, 1), (down, 4)], mixed, context, lse, vec_f
        )
        down = joined(down, got_down)
        up_quads = (up, up_y, up_core, swapped(up_y, 1))
        up_last = (last, last_z, last_core, swapped(last_z, 1))
    normed_one, inverse_one, hidden, active, slope = up_forward(
        me, up_quads, up_last, context, x_low, vec_f
    )
    if fast:
        (down_y, down_core), normed_one, hidden, active, slope = beside(
            [(down, 2), (down, 1)], normed_one, hidden, active, slope
        )
        down_quads = (down, down_y, down_core, swapped(down_y, 1))
    normed_two, inverse_two, output, cls_low = down_forward(
        me, down_quads, active, normed_one, vec_f, table
    )

    if fast:
        first = [cls_low] + [across(cls_low, t, m) for t, m in ((0, 8), (1, 0), (1, 8))]
        four = jnp.stack(first).reshape(2, 2, MB, SEGS, D)
        second = [four] + [across(four, 0, m) for m in (4, 2, 6)]
        eight = jnp.stack(second)
        everyone = jnp.stack([eight, across(eight, 0, 1)])
        everyone = jnp.transpose(everyone, (2, 4, 0, 1, 3, 5, 6))
    else:
        both = jnp.concatenate([cls_low, tower_swapped(cls_low)])
        everyone = jnp.roll(lax.all_gather(both, "dp", axis=0, tiled=False), -index, axis=0)
        everyone = jnp.transpose(everyone.reshape(owners, 2, MB, SEGS, D), (1, 2, 0, 3, 4))
    everyone = everyone.reshape(2, MB, queries_all, D)
    grad_cls = contrast_back(flag, everyone, cls_positives, cls_ids)

    residual, grad_ffn, sums_two, keep_down, send_down = down_back(
        me,
        token_grad[0].reshape(ROWS, D),
        grad_cls,
        jnp.concatenate([table] * 3),
        normed_two,
        inverse_two,
        vec_f,
        active,
    )
    if fast:
        (got_down,), residual, grad_ffn = beside([(send_down, 1)], residual, grad_ffn)
        keep_down, send_down = parted(keep_down, got_down)
    grad_one, grad_ctx, sums_one, keep_up, send_up, keep_out, send_out = up_back(
        me,
        up_quads,
        up_last,
        down_quads,
        grad_ffn,
        slope,
        hidden,
        residual,
        normed_one,
        inverse_one,
        context,
        vec_f,
    )
    if fast:
        (got_down,), grad_one, grad_ctx, send_up, send_out = beside(
            [(send_down, 2)], grad_one, grad_ctx, send_up, send_out
        )
        keep_down, send_down = parted(keep_down, got_down)
    back = partial(attention_back, me, x_low, seg_row, mixed, lse)
    grad_a, sums_a, keep_a, send_a = back(grad_ctx, 0)
    if fast:
        (got_down, got_up, got_out), grad_ctx, send_a = beside(
            [(send_down, 4), (send_up, 1), (send_out, 1)], grad_ctx, send_a
        )
        keep_down, send_down = parted(keep_down, got_down)
        keep_up, send_up = parted(keep_up, got_up)
        keep_out, send_out = parted(keep_out, got_out)
    grad_b, sums_b, keep_b, send_b = back(grad_ctx, 1)
    grad_c, sums_c, keep_c, send_c = back(grad_ctx, 2, sums_a, sums_b, sums_one, sums_two)
    if fast:
        (got_down, got_up, got_a), grad_b, grad_c, send_b, send_c = beside(
            [(send_down, 8), (send_up, 2), (send_a, 1)], grad_b, grad_c, send_b, send_c
        )
        share_down = added(keep_down[0], got_down[0])
        keep_up, send_up = parted(keep_up, got_up)
        two_a = parted(keep_a, got_a)
        keep_oa = jnp.concatenate([keep_out, two_a[0]], axis=1)
        send_oa = jnp.concatenate([send_out, two_a[1]], axis=1)
    input_grad = input_back(me, mix_quads, grad_one, (grad_a, grad_b, grad_c))
    if fast:
        (got_up, got_oa, got_b, got_c), input_grad = beside(
            [(send_up, 4), (send_oa, 2), (send_b, 1), (send_c, 1)], input_grad
        )
        keep_up, send_up = parted(keep_up, got_up)
        keep_oa, send_oa = parted(keep_oa, got_oa)
        two_b, two_c = parted(keep_b, got_b), parted(keep_c, got_c)
        keep_bc = jnp.concatenate([two_b[0], two_c[0]], axis=1)
        send_bc = jnp.concatenate([two_b[1], two_c[1]], axis=1)
        ((got_up, got_oa, got_bc),) = beside([(send_up, 8), (send_oa, 4), (send_bc, 2)])
        share_up = added(keep_up[0], got_up[0])
        keep_oa, send_oa = parted(keep_oa, got_oa)
        keep_bc, send_bc = parted(keep_bc, got_bc)
        ((got_oa, got_bc),) = beside([(send_oa, 8), (send_bc, 4)])
        share_oa = added(keep_oa[0], got_oa[0])
        keep_bc, send_bc = parted(keep_bc, got_bc)
        share_bc = added(keep_bc[0], swapped(send_bc, 8)[0])
        share_vec = lax.dynamic_slice(share_bc[96:108], (0, index * share), (12, share))
        shares = (share_down, share_up, share_oa, share_bc, share_vec)
        norm_shares = shares[:3] + (share_bc[:96], share_vec)
    else:

        def scattered(matrix):
            return lax.psum_scatter(
                matrix.astype(jnp.float32), "dp", scatter_dimension=0, tiled=True
            )

        mix_blocks = jnp.concatenate(
            [
                whole_rows(keep[:, :48], send[:, :48], 1)
                for keep, send in ((keep_a, send_a), (keep_b, send_b), (keep_c, send_c))
            ]
        )
        bias_mixed = jnp.concatenate([sums_a[:1], sums_b[:1], sums_c[:1]]).reshape(HG, 3, QCOLS)
        grad_vec = jnp.concatenate(
            [
                bias_mixed[:, 0].reshape(1, D),
                bias_mixed[:, 2].reshape(1, D),
                sums_one[4:7],
                sums_one[0:4],
                sums_two[0:3],
            ],
            axis=0,
        )
        shares = (
            scattered(from_heads(mix_blocks)),
            scattered(whole_rows(keep_out, send_out, 1)[0]),
            scattered(from_columns(whole_rows(keep_up, send_up, 4))),
            scattered(whole_rows(keep_down, send_down, 1)[0]),
            lax.psum_scatter(grad_vec, "dp", scatter_dimension=1, tiled=True),
        )
        norm_shares = shares

    local_square = sum(jnp.sum(s * s) for s in norm_shares)
    firsts = (first_mix[0], first_out[0], first_up[0], first_down[0], first_vectors[0])
    seconds = (second_mix[0], second_out[0], second_up[0], second_down[0], second_vectors[0])
    if fast:
        norm = jnp.broadcast_to(local_square, (8, 128))
        norm = (norm + across(norm, 0, 8)) + (across(norm, 1, 0) + across(norm, 1, 8))
        norm = (norm + across(norm, 0, 4)) + (across(norm, 0, 2) + across(norm, 0, 6))
        norm = norm + across(norm, 0, 1)
        grad_square = norm[0, 0]
        arrays = [
            pltpu.with_memory_space_constraint(a, pltpu.HBM) for a in masters + firsts + seconds
        ]
        updated = adam_all(norm, shares, arrays)
        updated = tuple(u[None] for u in updated)
    else:
        grad_square = lax.psum(local_square, ("tower", "dp"))
        factor = jnp.minimum(1.0, clip_norm / (jnp.sqrt(grad_square) + 1e-06))
        rates = (matrix_rate, matrix_rate, matrix_rate, matrix_rate, vector_rate)
        results = [
            adam_update(masters[i], shares[i], firsts[i], seconds[i], rates[i], factor)
            for i in range(5)
        ]
        updated = tuple(r[i] for i in range(3) for r in results)
    return (
        output.reshape(1, MB, 1, L, D),
        input_grad.reshape(1, MB, 1, L, D),
        *updated,
        grad_square,
    )


def solution(mesh):
    rows = P("tower", None, "dp", None, None)
    shards = (P("tower", "dp", None),) * 4 + (P("tower", None, "dp"),)
    in_specs = (rows, P("tower", None, "dp", None), P(None, "dp"), rows) + shards * 3
    out_specs = (rows, rows) + shards * 3 + (P(),)
    return jax.shard_map(body, mesh=mesh, in_specs=in_specs, out_specs=out_specs, check_vma=False)
```

```python
from functools import partial

import jax
import jax.numpy as jnp
from jax import lax
from jax.experimental import pallas as pl
from jax.experimental.pallas import tpu as pltpu
from jax.sharding import PartitionSpec as P

D = 768
FF = 3072
H = 12
HD = 64
L = 512
SEGS = 8
MB = 2
STEP = 5
HG = 3
PIECES = 16
PIECE_ROWS = D // PIECES

norm_eps = 1e-05
attention_scale = 0.125
score_scale = 0.0625
contrast_weight = 16.0
clip_norm = 1.0
beta_first = 0.9
beta_second = 0.999
adam_eps = 1e-08
weight_decay = 0.01
matrix_rate = 0.05
vector_rate = 0.5
masked_score = -1e30

low_type = jnp.bfloat16
highest = lax.Precision.HIGHEST


def swapped(value, mask):
    pairs = [(i, i ^ mask) for i in range(lax.axis_size("dp"))]
    return lax.ppermute(value, "dp", pairs)


def tower_swapped(value):
    return lax.ppermute(value, "tower", [(0, 1), (1, 0)])


def relative_of(place):
    return ((place & 1) << 3) | ((place & 2) << 1) | ((place & 4) >> 1) | (place >> 3)


def relative_y_first(place):
    return ((place & 1) << 1) | ((place & 2) << 2) | (place & 4) | (place >> 3)


def gather_pieces(own):
    pieces = own[None]
    for mask in (8, 4, 2, 1):
        pieces = jnp.concatenate([pieces, swapped(pieces, mask)])
    return pieces


def added(first, second):
    return first.astype(jnp.float32) + second.astype(jnp.float32)


def rows_dot(first_op, second_op):
    return jnp.dot(first_op, second_op, preferred_element_type=jnp.float32)


def contract_rows(first_op, second_op):
    return lax.dot_general(
        first_op, second_op, (((0,), (0,)), ((), ())), preferred_element_type=jnp.float32
    )


def contract_cols(first_op, second_op):
    return lax.dot_general(
        first_op, second_op, (((1,), (1,)), ((), ())), preferred_element_type=jnp.float32
    )


def layer_stats(values):
    centred = values - jnp.mean(values, axis=-1, keepdims=True)
    inverse = lax.rsqrt(jnp.mean(centred * centred, axis=-1, keepdims=True) + norm_eps)
    return (centred * inverse, inverse)


def norm_back(upstream, normed, inverse, gain_row):
    gained = upstream * gain_row
    return inverse * (
        gained
        - jnp.mean(gained, axis=-1, keepdims=True)
        - normed * jnp.mean(gained * normed, axis=-1, keepdims=True)
    )


def column_sum(values):
    return jnp.sum(values.astype(jnp.float32), axis=0, keepdims=True)


def gelu_parts(pre):
    below = 1.0 + (0.3275911 * 0.7071067811865476) * jnp.abs(pre)
    inner = pl.reciprocal(below, approx=True)
    inner = inner * (2.0 - below * inner)
    series = (0.5 * 1.061405429) * inner - (0.5 * 1.453152027)
    series = series * inner + (0.5 * 1.421413741)
    series = series * inner - (0.5 * 0.284496736)
    series = (series * inner + (0.5 * 0.254829592)) * inner
    bell = jnp.exp2(pre * pre * (-0.5 * log2e))
    half_tail = series * bell
    cumulative = jnp.where(pre >= 0.0, 1.0 - half_tail, half_tail)
    return (pre * cumulative, cumulative + pre * (bell * 0.3989422804014327))


log2e = 1.4426950408889634
ROWS = MB * L
QCOLS = D // HG
HEADS = H // HG
any_space = pl.BlockSpec(memory_space=pltpu.HBM)
scalar_space = pl.BlockSpec(memory_space=pltpu.SMEM)
vmem_space = pl.BlockSpec(memory_space=pltpu.VMEM)


def kept_in_hbm(array):
    return pltpu.with_memory_space_constraint(array, pltpu.HBM)


def params(megabytes):
    return pltpu.CompilerParams(vmem_limit_bytes=megabytes * 1024 * 1024)


def cost(flops, moved, exps=0):
    return pl.CostEstimate(flops=int(flops), bytes_accessed=int(moved), transcendentals=int(exps))


def start_pieces(me, quads, target, sem, order=relative_of, at=0):
    count = quads[0].shape[1]
    for place in range(PIECES):
        pltpu.make_async_copy(
            quads[place // 4].at[place % 4],
            target.at[me ^ order(place), pl.ds(at, count), :],
            sem,
        ).start()


def start_up(me, quads, quads_last, target, sem):
    start_pieces(me, quads, target, sem)
    start_pieces(me, quads_last, target, sem, relative_y_first, 4 * PIECE_ROWS)


def up_block_of(pieces, step):
    return block_of(pieces, step + step // 3)


def start_owners(me, source, keep, send, sem):
    for place in range(PIECES):
        held = keep if place < 8 else send
        pltpu.make_async_copy(
            source.at[me ^ relative_of(place)], held.at[place % 8], sem
        ).start()


def block_of(pieces, index):
    at = pl.multiple_of(index * PIECE_ROWS, 16)
    return pieces[:, pl.ds(at, PIECE_ROWS), :].reshape(D, D)


def segment_mask(seg_row):
    numbers = seg_row[...].reshape(1, L)
    columns = jnp.transpose(jnp.broadcast_to(numbers, (8, L)))[:, :1]
    return jnp.where(columns == numbers, 0.0, masked_score)


def wait_bytes(whole, sem):
    pltpu.make_async_copy(whole, whole, sem).wait()


def attention_kernel(
    me_ref, *refs
):
    quads = refs[:4]
    x_ref, seg_row, mixed_ref, ctx_ref, lse_ref, vec_ref, w, mask, bias, sems = refs[4:]
    hg, mb = pl.program_id(0), pl.program_id(1)
    me = me_ref[0]

    @pl.when((hg == 0) & (mb == 0))
    def _():
        start_pieces(me, quads, w, sems.at[0])

    @pl.when(hg == 0)
    def _():
        mask[mb] = segment_mask(seg_row)

    @pl.when((hg == 0) & (mb == 0))
    def _():
        wait_bytes(w, sems.at[0])
        vec = w[0, HG * PIECE_ROWS :, :].astype(jnp.float32)
        for place in range(1, PIECES):
            vec = vec + w[place, HG * PIECE_ROWS :, :].astype(jnp.float32)
        vec_ref[...] = vec
        for group in range(HG):
            columns = slice(group * QCOLS, (group + 1) * QCOLS)
            none = jnp.zeros((1, QCOLS), jnp.float32)
            bias[group] = jnp.concatenate([vec[0:1, columns], none, vec[1:2, columns]], axis=1)

    mixed = (rows_dot(x_ref[...], block_of(w, hg)) + bias[hg]).astype(low_type)
    mixed_ref[...] = mixed.reshape(mixed_ref.shape)
    v_t = jnp.transpose(mixed[:, 2 * QCOLS :])
    outs, totals = [], []

    def scores_of(head):
        here = slice(head * HD, (head + 1) * HD)
        q, k = mixed[:, here], mixed[:, QCOLS + head * HD : QCOLS + (head + 1) * HD]
        return contract_cols(k, q)

    ahead = scores_of(0)
    for head in range(HEADS):
        here = slice(head * HD, (head + 1) * HD)
        scores = ahead * (attention_scale * log2e) + mask[mb]
        if head + 1 < HEADS:
            ahead = scores_of(head + 1)
        largest = jnp.max(scores, axis=0, keepdims=True)
        expo = jnp.exp2(scores - largest)
        summed = jnp.sum(expo, axis=0, keepdims=True)
        probs = expo.astype(low_type)
        outs.append((rows_dot(v_t[here], probs) * (1.0 / summed)).astype(low_type))
        totals.append(largest + jnp.log(summed) * log2e)
    ctx_ref[...] = jnp.transpose(jnp.concatenate(outs, axis=0))
    lse_ref[...] = jnp.concatenate(totals, axis=0).reshape(lse_ref.shape)


def attention_forward(me, quads, x_low, seg_row):
    return pl.pallas_call(
        attention_kernel,
        grid=(HG, MB),
        in_specs=[
            scalar_space,
            *[any_space] * 4,
            pl.BlockSpec((L, D), lambda g, m: (m, 0)),
            pl.BlockSpec((1, 1, L), lambda g, m: (m, 0, 0)),
        ],
        out_specs=[
            pl.BlockSpec((1, L, D), lambda g, m: (g, m, 0)),
            pl.BlockSpec((L, QCOLS), lambda g, m: (m, g)),
            pl.BlockSpec((1, HEADS, L), lambda g, m: (g * MB + m, 0, 0)),
            pl.BlockSpec((16, D), lambda g, m: (0, 0)),
        ],
        out_shape=[
            pltpu.HBM((HG, ROWS, D), low_type),
            pltpu.HBM((ROWS, D), low_type),
            jax.ShapeDtypeStruct((HG * MB, HEADS, L), jnp.float32),
            jax.ShapeDtypeStruct((16, D), jnp.float32),
        ],
        scratch_shapes=[
            pltpu.VMEM((PIECES, HG * PIECE_ROWS + 16, D), low_type),
            pltpu.VMEM((MB, L, L), jnp.float32),
            pltpu.VMEM((HG, 1, D), jnp.float32),
            pltpu.SemaphoreType.DMA((1,)),
        ],
        compiler_params=params(40),
        cost_estimate=cost(2 * ROWS * D * 3 * D + 8 * MB * H * L * L * HD, 12e6, MB * H * L * L),
        name="mixed_attention",
    )(me, *quads, x_low, seg_row)


def up_kernel(
    me_ref,
    quad_0,
    quad_1,
    quad_2,
    quad_3,
    last_0,
    last_1,
    last_2,
    last_3,
    ctx_hbm,
    x_hbm,
    vec,
    normed_hbm,
    inverse_ref,
    hidden_hbm,
    active_ref,
    slope_ref,
    w,
    ctx,
    x,
    normed,
    hidden,
    sems,
):
    step = pl.program_id(0)
    me = me_ref[0]
    quads, quads_last = (quad_0, quad_1, quad_2, quad_3), (last_0, last_1, last_2, last_3)
    ctx_in = pltpu.make_async_copy(ctx_hbm, ctx, sems.at[1])
    x_in = pltpu.make_async_copy(x_hbm, x, sems.at[2])
    normed_out = pltpu.make_async_copy(normed, normed_hbm, sems.at[3])
    hidden_out = pltpu.make_async_copy(hidden, hidden_hbm, sems.at[4])

    @pl.when(step == 0)
    def _():
        start_up(me, quads, quads_last, w, sems.at[0])
        ctx_in.start()
        x_in.start()
        wait_bytes(w, sems.at[0])
        ctx_in.wait()
        x_in.wait()
        for first in range(0, ROWS, 256):
            part = slice(first, first + 256)
            branch = rows_dot(ctx[part, :], block_of(w, 3)) + vec[2:3, :]
            n, inv = layer_stats(x[part, :].astype(jnp.float32) + branch)
            normed[part, :] = n
            inverse_ref[part, :] = inv
            hidden[part, :] = (n * vec[3:4, :] + vec[4:5, :]).astype(low_type)
        normed_out.start()
        hidden_out.start()

    bias = vec[pl.ds(5 + step, 1), :]
    for first in range(0, ROWS, 256):
        part = slice(first, first + 256)
        pre = rows_dot(hidden[part, :], up_block_of(w, step)) + bias
        active, slope = gelu_parts(pre)
        active_ref[part, :] = active.astype(low_type)
        slope_ref[part, :] = slope.astype(low_type)

    @pl.when(step == 3)
    def _():
        normed_out.wait()
        hidden_out.wait()


def up_forward(me, quads, quads_last, context, x_low, vec):
    return pl.pallas_call(
        up_kernel,
        grid=(4,),
        in_specs=[scalar_space, *[any_space] * 10, vmem_space],
        out_specs=[
            any_space,
            pl.BlockSpec((ROWS, 1), lambda s: (0, 0)),
            any_space,
            pl.BlockSpec((ROWS, D), lambda s: (0, s)),
            pl.BlockSpec((ROWS, D), lambda s: (0, s)),
        ],
        out_shape=[
            pltpu.HBM((ROWS, D), jnp.float32),
            jax.ShapeDtypeStruct((ROWS, 1), jnp.float32),
            pltpu.HBM((ROWS, D), low_type),
            pltpu.HBM((ROWS, FF), low_type),
            pltpu.HBM((ROWS, FF), low_type),
        ],
        scratch_shapes=[
            pltpu.VMEM((PIECES, 5 * PIECE_ROWS, D), low_type),
            pltpu.VMEM((ROWS, D), low_type),
            pltpu.VMEM((ROWS, D), low_type),
            pltpu.VMEM((ROWS, D), jnp.float32),
            pltpu.VMEM((ROWS, D), low_type),
            pltpu.SemaphoreType.DMA((5,)),
        ],
        compiler_params=params(44),
        cost_estimate=cost(2 * ROWS * D * (FF + D), 24e6, 2 * ROWS * FF),
        name="out_up",
    )(me, *quads, *quads_last, context, x_low, vec)


def down_kernel(
    me_ref,
    quad_0,
    quad_1,
    quad_2,
    quad_3,
    active_hbm,
    normed_one_hbm,
    vec,
    table_ref,
    normed_hbm,
    inverse_ref,
    output_hbm,
    cls_ref,
    w,
    active,
    normed_one,
    normed,
    output,
    sems,
):
    me = me_ref[0]
    start_pieces(me, (quad_0, quad_1, quad_2, quad_3), w, sems.at[0])
    arrivals, departures = [], []
    for index in range(4):
        part = pl.ds(index * 256, 256)
        arrivals.append(
            (
                pltpu.make_async_copy(
                    active_hbm.at[part, :], active.at[part, :], sems.at[1 + index]
                ),
                pltpu.make_async_copy(
                    normed_one_hbm.at[part, :], normed_one.at[part, :], sems.at[5 + index]
                ),
            )
        )
        departures.append(
            (
                pltpu.make_async_copy(
                    normed.at[part, :], normed_hbm.at[part, :], sems.at[9 + index]
                ),
                pltpu.make_async_copy(
                    output.at[part, :], output_hbm.at[part, :], sems.at[13 + index]
                ),
            )
        )
        for arrival in arrivals[index]:
            arrival.start()
    wait_bytes(w, sems.at[0])
    for index in range(4):
        for arrival in arrivals[index]:
            arrival.wait()
        part = slice(index * 256, (index + 1) * 256)
        ffn = rows_dot(active[part, :], w[...].reshape(FF, D)) + vec[9:10, :]
        residual = normed_one[part, :] * vec[3:4, :] + vec[4:5, :]
        n, inv = layer_stats(residual + ffn)
        normed[part, :] = n
        inverse_ref[part, :] = inv
        output[part, :] = (n * vec[10:11, :] + vec[11:12, :]).astype(low_type)
        for departure in departures[index]:
            departure.start()
    cls_ref[...] = rows_dot(table_ref[...], output[...]).astype(low_type)
    for pair in departures:
        for departure in pair:
            departure.wait()


def down_forward(me, quads, active, normed_one, vec, table):
    return pl.pallas_call(
        down_kernel,
        in_specs=[scalar_space, *[any_space] * 6, vmem_space, vmem_space],
        out_specs=[any_space, vmem_space, any_space, vmem_space],
        out_shape=[
            pltpu.HBM((ROWS, D), jnp.float32),
            jax.ShapeDtypeStruct((ROWS, 1), jnp.float32),
            pltpu.HBM((ROWS, D), low_type),
            jax.ShapeDtypeStruct((MB * SEGS, D), low_type),
        ],
        scratch_shapes=[
            pltpu.VMEM((PIECES, 4 * PIECE_ROWS, D), low_type),
            pltpu.VMEM((ROWS, FF), low_type),
            pltpu.VMEM((ROWS, D), jnp.float32),
            pltpu.VMEM((ROWS, D), jnp.float32),
            pltpu.VMEM((ROWS, D), low_type),
            pltpu.SemaphoreType.DMA((17,)),
        ],
        compiler_params=params(40),
        cost_estimate=cost(2 * ROWS * D * FF, 19e6),
        name="down",
    )(me, *quads, kept_in_hbm(active), kept_in_hbm(normed_one), vec, table)


def contrast_kernel(flag_ref, all_ref, positive_ref, ids_ref, grad_ref):
    passage_here = flag_ref[0] == 1
    for batch in range(MB):
        mine, theirs = all_ref[0, batch], all_ref[1, batch]
        queries = jnp.where(passage_here, theirs, mine)
        passages = jnp.where(passage_here, mine, theirs)
        contrast = contract_cols(queries, passages) * score_scale
        top = jnp.max(contrast, axis=-1, keepdims=True)
        expo = jnp.exp(contrast - top)
        probs = expo / jnp.sum(expo, axis=-1, keepdims=True)
        chosen = (positive_ref[batch] == ids_ref[...]).astype(jnp.float32)
        grad = (contrast_weight * (probs - chosen)).astype(low_type)
        for_query = rows_dot(grad[:16], passages) * score_scale
        for_query = for_query.astype(low_type).astype(jnp.float32)
        for_passage = contract_rows(grad, queries)[:16] * score_scale
        taken = jnp.where(passage_here, for_passage, for_query)
        grad_ref[batch * SEGS : (batch + 1) * SEGS, :] = taken[:SEGS]


def contrast_back(flag, everyone, cls_positives, cls_ids):
    return pl.pallas_call(
        contrast_kernel,
        in_specs=[scalar_space, vmem_space, vmem_space, vmem_space],
        out_specs=vmem_space,
        out_shape=jax.ShapeDtypeStruct((MB * SEGS, D), jnp.float32),
        compiler_params=params(48),
        name="contrast",
    )(flag, everyone, cls_positives, cls_ids)


def down_back_kernel(
    me_ref,
    token_grad_hbm,
    grad_cls,
    table3_ref,
    normed_hbm,
    inverse_ref,
    vec,
    active_ref,
    residual_hbm,
    low_ref,
    sums_ref,
    keep,
    send,
    low,
    token_grad,
    normed,
    residual,
    staged,
    sems,
):
    step = pl.program_id(0)
    me = me_ref[0]
    residual_out = pltpu.make_async_copy(residual, residual_hbm, sems.at[8])

    @pl.when(step == 0)
    def _():
        arrivals = []
        for index in range(4):
            part = pl.ds(index * 256, 256)
            arrivals.append(
                (
                    pltpu.make_async_copy(
                        token_grad_hbm.at[part, :], token_grad.at[part, :], sems.at[index]
                    ),
                    pltpu.make_async_copy(
                        normed_hbm.at[part, :], normed.at[part, :], sems.at[4 + index]
                    ),
                )
            )
            for arrival in arrivals[index]:
                arrival.start()
        grads = grad_cls[...]
        upper = grads.astype(low_type)
        rest = grads - upper.astype(jnp.float32)
        middle = rest.astype(low_type)
        lower = (rest - middle.astype(jnp.float32)).astype(low_type)
        stacked = jnp.concatenate([upper, middle, lower], axis=0)
        gains = jnp.zeros((1, D), jnp.float32)
        shifts = jnp.zeros((1, D), jnp.float32)
        biases = jnp.zeros((1, D), jnp.float32)
        for index in range(4):
            part = slice(index * 256, (index + 1) * 256)
            for arrival in arrivals[index]:
                arrival.wait()
            upstream = token_grad[part, :] + contract_rows(table3_ref[:, part], stacked)
            n = normed[part, :]
            gains = gains + column_sum(upstream * n)
            shifts = shifts + column_sum(upstream)
            grad = norm_back(upstream, n, inverse_ref[part, :], vec[10:11, :])
            residual[part, :] = grad
            rounded = grad.astype(low_type)
            biases = biases + column_sum(rounded)
            low[part, :] = rounded
        residual_out.start()
        low_ref[...] = low[...]
        sums_ref[...] = jnp.concatenate([biases, gains, shifts, jnp.zeros((5, D), jnp.float32)])

    for first in range(4):
        at = first * 4 * PIECE_ROWS
        staged[4 * step + first] = contract_rows(
            active_ref[:, at : at + 4 * PIECE_ROWS], low[...]
        ).astype(low_type)

    @pl.when(step == 3)
    def _():
        start_owners(me, staged, keep, send, sems.at[9])
        residual_out.wait()
        wait_bytes(staged, sems.at[9])


def down_back(me, token_grad, grad_cls, table3, normed, inverse, vec, active):
    half = jax.ShapeDtypeStruct((8, 4 * PIECE_ROWS, D), low_type)
    return pl.pallas_call(
        down_back_kernel,
        grid=(4,),
        in_specs=[
            scalar_space,
            any_space,
            vmem_space,
            vmem_space,
            any_space,
            vmem_space,
            vmem_space,
            pl.BlockSpec((ROWS, D), lambda s: (0, s)),
        ],
        out_specs=[any_space] + [vmem_space] * 2 + [any_space] * 2,
        out_shape=[
            pltpu.HBM((ROWS, D), jnp.float32),
            jax.ShapeDtypeStruct((ROWS, D), low_type),
            jax.ShapeDtypeStruct((8, D), jnp.float32),
            half,
            half,
        ],
        scratch_shapes=[
            pltpu.VMEM((ROWS, D), low_type),
            pltpu.VMEM((ROWS, D), jnp.float32),
            pltpu.VMEM((ROWS, D), jnp.float32),
            pltpu.VMEM((ROWS, D), jnp.float32),
            pltpu.VMEM((PIECES, 4 * PIECE_ROWS, D), low_type),
            pltpu.SemaphoreType.DMA((10,)),
        ],
        compiler_params=params(44),
        cost_estimate=cost(2 * ROWS * D * FF, 25e6),
        name="down_back",
    )(
        me,
        kept_in_hbm(token_grad),
        grad_cls,
        table3,
        kept_in_hbm(normed),
        inverse,
        vec,
        kept_in_hbm(active),
    )


def up_back_kernel(
    me_ref,
    up_0,
    up_1,
    up_2,
    up_3,
    last_0,
    last_1,
    last_2,
    last_3,
    down_0,
    down_1,
    down_2,
    down_3,
    low_ref,
    slope_ref,
    hidden_ref,
    residual_hbm,
    normed_hbm,
    inverse_ref,
    ctx_hbm,
    vec,
    grad_one_hbm,
    grad_ctx_ref,
    sums_ref,
    keep,
    send,
    keep_out,
    send_out,
    up_w,
    down_w,
    normed,
    ctx,
    total,
    staged,
    staged_out,
    bias_sums,
    sems,
):
    step = pl.program_id(0)
    me = me_ref[0]
    residual_in = pltpu.make_async_copy(residual_hbm, total, sems.at[2])
    normed_in = pltpu.make_async_copy(normed_hbm, normed, sems.at[3])
    ctx_in = pltpu.make_async_copy(ctx_hbm, ctx, sems.at[4])

    @pl.when(step == 0)
    def _():
        start_pieces(me, (down_0, down_1, down_2, down_3), down_w, sems.at[0])
        last = (last_0, last_1, last_2, last_3)
        start_up(me, (up_0, up_1, up_2, up_3), last, up_w, sems.at[1])
        residual_in.start()
        normed_in.start()
        ctx_in.start()
        wait_bytes(down_w, sems.at[0])

    down_block = down_w[pl.ds(4 * step, 4)].reshape(D, D)
    biases = jnp.zeros((1, D), jnp.float32)
    grads = []
    for first in range(0, ROWS, 256):
        part = slice(first, first + 256)
        active_grad = contract_cols(low_ref[part, :], down_block)
        grad = (active_grad * slope_ref[part, :].astype(jnp.float32)).astype(low_type)
        biases = biases + column_sum(grad)
        grads.append(grad)
    grad = jnp.concatenate(grads, axis=0)

    @pl.when(step == 0)
    def _():
        wait_bytes(up_w, sems.at[1])
        residual_in.wait()

    total[...] += contract_cols(grad, up_block_of(up_w, step))
    at = pl.multiple_of(step * PIECE_ROWS, 16)
    for first in range(0, PIECES, 4):
        columns = slice(first * PIECE_ROWS, (first + 4) * PIECE_ROWS)
        terms = contract_rows(hidden_ref[:, columns], grad).astype(low_type)
        staged[first : first + 4, pl.ds(at, PIECE_ROWS), :] = terms.reshape(4, PIECE_ROWS, D)
    bias_sums[step] = biases

    @pl.when(step == 3)
    def _():
        start_owners(me, staged, keep, send, sems.at[5])
        normed_in.wait()
        ctx_in.wait()
        gains = jnp.zeros((1, D), jnp.float32)
        shifts = jnp.zeros((1, D), jnp.float32)
        out_biases = jnp.zeros((1, D), jnp.float32)
        lows, departures = [], []
        for first in range(0, ROWS, 256):
            part = slice(first, first + 256)
            upstream = total[part, :]
            n = normed[part, :]
            gains = gains + column_sum(upstream * n)
            shifts = shifts + column_sum(upstream)
            grad_one = norm_back(upstream, n, inverse_ref[part, :], vec[3:4, :])
            total[part, :] = grad_one
            departures.append(
                pltpu.make_async_copy(
                    total.at[part, :], grad_one_hbm.at[part, :], sems.at[7 + first // 256]
                )
            )
            departures[-1].start()
            rounded = grad_one.astype(low_type)
            out_biases = out_biases + column_sum(rounded)
            grad_ctx_ref[part, :] = contract_cols(rounded, block_of(up_w, 3)).astype(low_type)
            lows.append(rounded)
        sums_ref[...] = jnp.concatenate(
            [bias_sums[block] for block in range(4)]
            + [out_biases, gains, shifts, jnp.zeros((1, D), jnp.float32)]
        )
        rounded = jnp.concatenate(lows, axis=0)
        for first in range(0, PIECES, 4):
            columns = slice(first * PIECE_ROWS, (first + 4) * PIECE_ROWS)
            terms = contract_rows(ctx[:, columns], rounded).astype(low_type)
            staged_out[first : first + 4] = terms.reshape(4, PIECE_ROWS, D)
        start_owners(me, staged_out, keep_out, send_out, sems.at[6])
        wait_bytes(staged, sems.at[5])
        wait_bytes(staged_out, sems.at[6])
        for departure in departures:
            departure.wait()


def up_back(
    me, up_quads, up_last, down_quads, low, slope, hidden, residual, normed, inverse, ctx, vec
):
    half = jax.ShapeDtypeStruct((8, 4 * PIECE_ROWS, D), low_type)
    half_out = jax.ShapeDtypeStruct((8, PIECE_ROWS, D), low_type)
    return pl.pallas_call(
        up_back_kernel,
        grid=(4,),
        in_specs=[scalar_space]
        + [any_space] * 12
        + [
            vmem_space,
            pl.BlockSpec((ROWS, D), lambda s: (0, s)),
            vmem_space,
            any_space,
            any_space,
            vmem_space,
            any_space,
            vmem_space,
        ],
        out_specs=[any_space] + [vmem_space] * 2 + [any_space] * 4,
        out_shape=[
            pltpu.HBM((ROWS, D), jnp.float32),
            jax.ShapeDtypeStruct((ROWS, D), low_type),
            jax.ShapeDtypeStruct((8, D), jnp.float32),
            half,
            half,
            half_out,
            half_out,
        ],
        scratch_shapes=[
            pltpu.VMEM((PIECES, 5 * PIECE_ROWS, D), low_type),
            pltpu.VMEM((PIECES, 4 * PIECE_ROWS, D), low_type),
            pltpu.VMEM((ROWS, D), jnp.float32),
            pltpu.VMEM((ROWS, D), low_type),
            pltpu.VMEM((ROWS, D), jnp.float32),
            pltpu.VMEM((PIECES, 4 * PIECE_ROWS, D), low_type),
            pltpu.VMEM((PIECES, PIECE_ROWS, D), low_type),
            pltpu.VMEM((4, 1, D), jnp.float32),
            pltpu.SemaphoreType.DMA((11,)),
        ],
        compiler_params=params(56),
        cost_estimate=cost(2 * ROWS * D * (3 * FF + 2 * D), 40e6),
        name="up_back",
    )(
        me,
        *up_quads,
        *up_last,
        *down_quads,
        low,
        slope,
        hidden,
        residual,
        normed,
        inverse,
        ctx,
        vec,
    )


def attention_back_kernel(
    me_ref,
    x_ref,
    seg_row,
    mixed_ref,
    lse_ref,
    grad_ctx_ref,
    *refs,
):
    others, (grad_mixed_ref, sums_ref, keep, send, weight_grad, staged, sem) = refs[:-7], refs[-7:]
    mb = pl.program_id(0)
    me = me_ref[0]
    mask = segment_mask(seg_row)
    mixed = mixed_ref[...].reshape(L, D)
    lse = lse_ref[...].reshape(HEADS, L)
    k_t = jnp.transpose(mixed[:, QCOLS : 2 * QCOLS])
    grad_q, grad_k, grad_v = [], [], []

    def products_of(head):
        here = slice(head * HD, (head + 1) * HD)
        q, k = mixed[:, here], mixed[:, QCOLS + head * HD : QCOLS + (head + 1) * HD]
        v = mixed[:, 2 * QCOLS + head * HD : 2 * QCOLS + (head + 1) * HD]
        return (contract_cols(k, q), contract_cols(v, grad_ctx_ref[:, here]))

    ahead = products_of(0)
    for head in range(HEADS):
        here = slice(head * HD, (head + 1) * HD)
        scores, grad_probs = ahead
        if head + 1 < HEADS:
            ahead = products_of(head + 1)
        scores = scores * (attention_scale * log2e) + mask
        probs = jnp.exp2(scores - lse[head : head + 1])
        inner = jnp.sum(probs * grad_probs, axis=0, keepdims=True)
        grad_scores = (probs * (grad_probs - inner)).astype(low_type)
        grad_v.append(rows_dot(probs.astype(low_type), grad_ctx_ref[:, here]).astype(low_type))
        grad_q.append((rows_dot(k_t[here], grad_scores) * attention_scale).astype(low_type))
        grad_k.append((rows_dot(grad_scores, mixed[:, here]) * attention_scale).astype(low_type))
    grad_mixed = jnp.concatenate(
        [jnp.transpose(jnp.concatenate(grad_q, axis=0))] + grad_k + grad_v, axis=1
    )

    grad_mixed_ref[...] = grad_mixed
    bias = column_sum(grad_mixed)
    terms = contract_rows(x_ref[...], grad_mixed)

    @pl.when(mb == 0)
    def _():
        weight_grad[...] = terms
        sums_ref[0:1, :] = bias

    @pl.when(mb == 1)
    def _():
        sums_ref[0:1, :] += bias
        grads = (weight_grad[...] + terms).astype(low_type)
        staged[:, :PIECE_ROWS, :] = grads.reshape(PIECES, PIECE_ROWS, D)
        if others:
            mixed_a, mixed_b, up, down = (other[...] for other in others)
            mixed_sums = (mixed_a[0:1], mixed_b[0:1], sums_ref[0:1, :])
            vectors = jnp.concatenate(
                [
                    jnp.concatenate([s[:, :QCOLS] for s in mixed_sums], axis=1),
                    jnp.concatenate([s[:, 2 * QCOLS :] for s in mixed_sums], axis=1),
                    up[4:7],
                    up[0:4],
                    down[0:3],
                    jnp.zeros((4, D), jnp.float32),
                ],
                axis=0,
            )
            for place in range(PIECES):
                staged[place, PIECE_ROWS:, :] = vectors.astype(low_type)
        start_owners(me, staged, keep, send, sem)
        wait_bytes(staged, sem)


def attention_back(me, x_low, seg_row, mixed, lse, grad_ctx, group, *others):
    rows = PIECE_ROWS + (16 if others else 0)
    half = jax.ShapeDtypeStruct((8, rows, D), low_type)
    return pl.pallas_call(
        attention_back_kernel,
        grid=(MB,),
        in_specs=[
            scalar_space,
            pl.BlockSpec((L, D), lambda m: (m, 0)),
            pl.BlockSpec((1, 1, L), lambda m: (m, 0, 0)),
            pl.BlockSpec((1, L, D), lambda m: (group, m, 0)),
            pl.BlockSpec((1, HEADS, L), lambda m: (group * MB + m, 0, 0)),
            pl.BlockSpec((L, QCOLS), lambda m: (m, group)),
            *[vmem_space] * len(others),
        ],
        out_specs=[pl.BlockSpec((L, D), lambda m: (m, 0)), vmem_space, any_space, any_space],
        out_shape=[
            jax.ShapeDtypeStruct((ROWS, D), low_type),
            jax.ShapeDtypeStruct((8, D), jnp.float32),
            half,
            half,
        ],
        scratch_shapes=[
            pltpu.VMEM((D, D), jnp.float32),
            pltpu.VMEM((PIECES, rows, D), low_type),
            pltpu.SemaphoreType.DMA,
        ],
        compiler_params=params(40),
        cost_estimate=cost(
            2 * ROWS * D * D + 20 * MB * HEADS * L * L * HD, 12e6, MB * HEADS * L * L
        ),
        name=f"attention_back_{group}",
    )(me, x_low, seg_row, kept_in_hbm(mixed), lse, grad_ctx, *others)


def input_back_kernel(
    me_ref, quad_0, quad_1, quad_2, quad_3, one_ref, grad_0, grad_1, grad_2, input_ref, w, sem
):
    @pl.when(pl.program_id(0) == 0)
    def _():
        start_pieces(me_ref[0], (quad_0, quad_1, quad_2, quad_3), w, sem)
        wait_bytes(w, sem)

    total = one_ref[...]
    for block, grad in enumerate((grad_0, grad_1, grad_2)):
        total = total + contract_cols(grad[...], block_of(w, block))
    input_ref[...] = total


def input_back(me, quads, grad_one, grads):
    rows = pl.BlockSpec((256, D), lambda s: (s, 0))
    return pl.pallas_call(
        input_back_kernel,
        grid=(ROWS // 256,),
        in_specs=[scalar_space] + [any_space] * 4 + [rows] * 4,
        out_specs=rows,
        out_shape=jax.ShapeDtypeStruct((ROWS, D), jnp.float32),
        scratch_shapes=[
            pltpu.VMEM((PIECES, HG * PIECE_ROWS + 16, D), low_type),
            pltpu.SemaphoreType.DMA,
        ],
        compiler_params=params(24),
        cost_estimate=cost(6 * ROWS * D * D, 14e6),
        name="input_back",
    )(me, *quads, grad_one, *grads)


def adam_kernel(norm_ref, down_ref, up_ref, out_mix, mix_bc, vec_ref, *refs):
    ins, outs, held, sems = refs[:15], refs[15:30], refs[30:45], refs[45]
    arrivals = [
        pltpu.make_async_copy(ins[i], held[i], sems.at[i]) for i in range(15)
    ]
    departures = [
        pltpu.make_async_copy(held[i], outs[i], sems.at[i]) for i in range(15)
    ]
    order = (3, 2, 0, 1, 4)
    for index in order:
        for i in (index, 5 + index, 10 + index):
            arrivals[i].start()
    factor = jnp.minimum(1.0, clip_norm / (jnp.sqrt(norm_ref[0:1, 0:1]) + 1e-06))

    def update(index, columns, grad, rate):
        master, first, second = held[index], held[5 + index], held[10 + index]
        clipped = grad * factor
        first_new = beta_first * first[:, columns] + (1.0 - beta_first) * clipped
        second_new = beta_second * second[:, columns] + (1.0 - beta_second) * clipped * clipped
        root = jnp.sqrt(second_new / (1.0 - beta_second**STEP)) + adam_eps
        step = first_new / (1.0 - beta_first**STEP) / root
        old = master[:, columns]
        master[:, columns] = old - rate * (step + weight_decay * old)
        first[:, columns] = first_new
        second[:, columns] = second_new

    for index in order:
        for i in (index, 5 + index, 10 + index):
            arrivals[i].wait()
        if index == 0:
            one, two = PIECE_ROWS, 2 * PIECE_ROWS
            parts = (out_mix[one:two, :], mix_bc[:one, :], mix_bc[one:two, :])
            for group, share in enumerate(parts):
                for third in range(3):
                    at = third * D + group * QCOLS
                    grad = share[:, third * QCOLS : (third + 1) * QCOLS]
                    update(0, slice(at, at + QCOLS), grad, matrix_rate)
        elif index == 1:
            update(1, slice(0, D), out_mix[:PIECE_ROWS, :], matrix_rate)
        elif index == 2:
            for block in range(4):
                grad = up_ref[block * PIECE_ROWS : (block + 1) * PIECE_ROWS, :]
                update(2, slice(block * D, (block + 1) * D), grad, matrix_rate)
        elif index == 3:
            update(3, slice(0, D), down_ref[...], matrix_rate)
        else:
            update(4, slice(0, PIECE_ROWS), vec_ref[...], vector_rate)
        for i in (index, 5 + index, 10 + index):
            departures[i].start()
    for departure in departures:
        departure.wait()


def adam_all(norm, shares, arrays):
    return pl.pallas_call(
        adam_kernel,
        in_specs=[vmem_space] * 6 + [any_space] * 15,
        out_specs=[any_space] * 15,
        out_shape=[jax.ShapeDtypeStruct(a.shape, jnp.float32) for a in arrays],
        scratch_shapes=[pltpu.VMEM(a.shape, jnp.float32) for a in arrays]
        + [pltpu.SemaphoreType.DMA((15,))],
        compiler_params=params(40),
        cost_estimate=cost(40e6, 25e6),
        name="adam",
    )(norm, *shares, *arrays)


def by_heads(matrix):
    shaped = matrix.reshape(matrix.shape[0], 3, HG, D // HG)
    return jnp.transpose(shaped, (2, 0, 1, 3)).reshape(HG, matrix.shape[0], D)


def from_heads(blocks):
    rows = blocks.shape[1]
    shaped = blocks.reshape(HG, rows, 3, D // HG)
    return jnp.transpose(shaped, (1, 2, 0, 3)).reshape(rows, 3 * D)


def by_columns(matrix):
    return jnp.transpose(matrix.reshape(matrix.shape[0], 4, D), (1, 0, 2))


def from_columns(blocks):
    return jnp.transpose(blocks, (1, 0, 2)).reshape(blocks.shape[1], 4 * D)


def adam_update(master, grad_share, first, second, rate, factor):
    clipped = grad_share * factor
    first_new = beta_first * first + (1.0 - beta_first) * clipped
    second_new = beta_second * second + (1.0 - beta_second) * clipped * clipped
    first_hat = first_new / (1.0 - beta_first**STEP)
    second_hat = second_new / (1.0 - beta_second**STEP)
    master_new = master - rate * (
        first_hat / (jnp.sqrt(second_hat) + adam_eps) + weight_decay * master
    )
    return (master_new[None], first_new[None], second_new[None])


def quads_of(matrix_rows):
    k = matrix_rows.shape[0]
    shaped = matrix_rows.reshape(k, 2, 2, 2, 2, -1, D)
    pieces = jnp.transpose(shaped, (4, 3, 2, 1, 0, 5, 6)).reshape(4, 4, -1, D)
    return tuple(pieces[i] for i in range(4))


def whole_rows(keep, send, k):
    shaped = jnp.concatenate([keep, send]).reshape(2, 2, 2, 2, k, -1, D)
    return jnp.transpose(shaped, (4, 3, 2, 1, 0, 5, 6)).reshape(k, -1, D)


def beside(sends, *work):
    received = [swapped(value, mask) for value, mask in sends]
    done = lax.optimization_barrier((received, work))
    return (done[0], *done[1])


def across(value, tower_mask, dp_mask):
    owners = lax.axis_size("dp")
    flip = tower_mask * owners + dp_mask
    pairs = [(i, i ^ flip) for i in range(2 * owners)]
    return lax.ppermute(value, ("tower", "dp"), pairs)


def joined(pieces, received):
    return jnp.concatenate([pieces, received])


def parted(keep, received):
    half = keep.shape[0] // 2
    return (
        added(keep[:half], received[:half]).astype(low_type),
        added(keep[half:], received[half:]).astype(low_type),
    )


def body(
    tokens,
    segments,
    positives,
    token_grad,
    mix_weight,
    out_weight,
    up_weight,
    down_weight,
    vectors,
    first_mix,
    first_out,
    first_up,
    first_down,
    first_vectors,
    second_mix,
    second_out,
    second_up,
    second_down,
    second_vectors,
):
    owners = lax.axis_size("dp")
    fast = owners == PIECES
    index = lax.axis_index("dp")
    flag = lax.axis_index("tower").astype(jnp.int32).reshape(1)
    masters = (mix_weight[0], out_weight[0], up_weight[0], down_weight[0], vectors[0])
    low_mix, low_out, low_up, low_down, low_vec = (m.astype(low_type) for m in masters)
    share = low_vec.shape[1]
    queries_all = owners * SEGS

    if fast:
        me = index.astype(jnp.int32).reshape(1)
        extra = jnp.zeros((16, D), low_type)
        extra = extra.at[12:14, :SEGS].set(positives.astype(low_type))
        extra = lax.dynamic_update_slice(extra, low_vec, (0, index * share))
        pack_mix = jnp.concatenate([by_heads(low_mix).reshape(-1, D), extra])
        low_blocks = by_columns(low_up)
        pack_up = jnp.concatenate([low_blocks[:3].reshape(-1, D), low_out])
        mix, up, last, down = pack_mix[None], pack_up[None], low_blocks[3:], low_down[None]
        ((got_mix, got_last),) = beside([(mix, 8), (last, 2)])
        mix, last = joined(mix, got_mix), joined(last, got_last)
        ((got_mix, got_up),) = beside([(mix, 4), (up, 8)])
        mix, up = joined(mix, got_mix), joined(up, got_up)
        ((mix_y, mix_core, got_up, got_last, got_down),) = beside(
            [(mix, 2), (mix, 1), (up, 4), (last, 8), (down, 8)]
        )
        up, last, down = joined(up, got_up), joined(last, got_last), joined(down, got_down)
        mix_quads = (mix, mix_y, mix_core, swapped(mix_y, 1))
        extras = jnp.concatenate([quad[:, 156:158, :SEGS] for quad in mix_quads])
        cls_positives = jnp.transpose(extras.astype(jnp.int32), (1, 0, 2))
        cls_positives = cls_positives.reshape(MB, queries_all, 1)
        relative = relative_of(jnp.arange(PIECES, dtype=jnp.int32))
        cls_ids = ((relative ^ index)[:, None] * SEGS + jnp.arange(SEGS)[None, :]).reshape(1, -1)
    else:
        me = jnp.zeros((1,), jnp.int32)
        mix_quads = quads_of(by_heads(lax.all_gather(low_mix, "dp", axis=0, tiled=True)))
        up_blocks = by_columns(lax.all_gather(low_up, "dp", axis=0, tiled=True))
        out_block = lax.all_gather(low_out, "dp", axis=0, tiled=True)[None]
        up_quads = quads_of(jnp.concatenate([up_blocks[:3], out_block]))
        up_last = jnp.concatenate(quads_of(up_blocks[3:]))
        up_last = jnp.stack(
            [up_last[relative_of(relative_y_first(place))] for place in range(PIECES)]
        ).reshape(4, 4, PIECE_ROWS, D)
        up_last = tuple(up_last[i] for i in range(4))
        down_quads = quads_of(lax.all_gather(low_down, "dp", axis=0, tiled=True)[None])
        vec_low = lax.all_gather(low_vec, "dp", axis=1, tiled=True)
        extra = jnp.zeros((PIECES, 16, D), low_type).at[0, :12].set(vec_low)
        mix_quads = tuple(
            jnp.concatenate([quad, extra[4 * i : 4 * i + 4]], axis=1)
            for i, quad in enumerate(mix_quads)
        )
        cls_positives = lax.all_gather(positives, "dp", axis=1, tiled=True)
        cls_positives = jnp.roll(cls_positives, -index * SEGS, axis=1)[:, :, None]
        cls_ids = jnp.roll(jnp.arange(queries_all, dtype=jnp.int32), -index * SEGS)[None]

    x_low = tokens[0].reshape(ROWS, D)
    seg_rows = segments[0].reshape(MB, L)
    seg_row = seg_rows.reshape(MB, 1, L)
    before = jnp.concatenate([jnp.full((MB, 1), -1, jnp.int32), seg_rows[:, :-1]], axis=1)
    numbers = jnp.where(seg_rows != before, seg_rows, -1)
    numbers = jnp.where(numbers >= 0, numbers + SEGS * jnp.arange(MB)[:, None], -1).reshape(1, ROWS)
    table = (jnp.arange(MB * SEGS)[:, None] == numbers).astype(low_type)
    mixed, context, lse, vec_f = attention_forward(me, mix_quads, x_low, seg_row)
    if fast:
        (up_y, up_core, last_z, last_core, got_down), mixed, context, lse, vec_f = beside(
            [(up, 2), (up, 1), (last, 4), (last, 1), (down, 4)], mixed, context, lse, vec_f
        )
        down = joined(down, got_down)
        up_quads = (up, up_y, up_core, swapped(up_y, 1))
        up_last = (last, last_z, last_core, swapped(last_z, 1))
    normed_one, inverse_one, hidden, active, slope = up_forward(
        me, up_quads, up_last, context, x_low, vec_f
    )
    if fast:
        (down_y, down_core), normed_one, hidden, active, slope = beside(
            [(down, 2), (down, 1)], normed_one, hidden, active, slope
        )
        down_quads = (down, down_y, down_core, swapped(down_y, 1))
    normed_two, inverse_two, output, cls_low = down_forward(
        me, down_quads, active, normed_one, vec_f, table
    )

    if fast:
        first = [cls_low] + [across(cls_low, t, m) for t, m in ((0, 8), (1, 0), (1, 8))]
        four = jnp.stack(first).reshape(2, 2, MB, SEGS, D)
        second = [four] + [across(four, 0, m) for m in (4, 2, 6)]
        eight = jnp.stack(second)
        everyone = jnp.stack([eight, across(eight, 0, 1)])
        everyone = jnp.transpose(everyone, (2, 4, 0, 1, 3, 5, 6))
    else:
        both = jnp.concatenate([cls_low, tower_swapped(cls_low)])
        everyone = jnp.roll(lax.all_gather(both, "dp", axis=0, tiled=False), -index, axis=0)
        everyone = jnp.transpose(everyone.reshape(owners, 2, MB, SEGS, D), (1, 2, 0, 3, 4))
    everyone = everyone.reshape(2, MB, queries_all, D)
    grad_cls = contrast_back(flag, everyone, cls_positives, cls_ids)

    residual, grad_ffn, sums_two, keep_down, send_down = down_back(
        me,
        token_grad[0].reshape(ROWS, D),
        grad_cls,
        jnp.concatenate([table] * 3),
        normed_two,
        inverse_two,
        vec_f,
        active,
    )
    if fast:
        (got_down,), residual, grad_ffn = beside([(send_down, 1)], residual, grad_ffn)
        keep_down, send_down = parted(keep_down, got_down)
    grad_one, grad_ctx, sums_one, keep_up, send_up, keep_out, send_out = up_back(
        me,
        up_quads,
        up_last,
        down_quads,
        grad_ffn,
        slope,
        hidden,
        residual,
        normed_one,
        inverse_one,
        context,
        vec_f,
    )
    if fast:
        (got_down,), grad_one, grad_ctx, send_up, send_out = beside(
            [(send_down, 2)], grad_one, grad_ctx, send_up, send_out
        )
        keep_down, send_down = parted(keep_down, got_down)
    back = partial(attention_back, me, x_low, seg_row, mixed, lse)
    grad_a, sums_a, keep_a, send_a = back(grad_ctx, 0)
    if fast:
        (got_down, got_up, got_out), grad_ctx, send_a = beside(
            [(send_down, 4), (send_up, 1), (send_out, 1)], grad_ctx, send_a
        )
        keep_down, send_down = parted(keep_down, got_down)
        keep_up, send_up = parted(keep_up, got_up)
        keep_out, send_out = parted(keep_out, got_out)
    grad_b, sums_b, keep_b, send_b = back(grad_ctx, 1)
    grad_c, sums_c, keep_c, send_c = back(grad_ctx, 2, sums_a, sums_b, sums_one, sums_two)
    if fast:
        (got_down, got_up, got_a), grad_b, grad_c, send_b, send_c = beside(
            [(send_down, 8), (send_up, 2), (send_a, 1)], grad_b, grad_c, send_b, send_c
        )
        share_down = added(keep_down[0], got_down[0])
        keep_up, send_up = parted(keep_up, got_up)
        two_a = parted(keep_a, got_a)
        keep_oa = jnp.concatenate([keep_out, two_a[0]], axis=1)
        send_oa = jnp.concatenate([send_out, two_a[1]], axis=1)
    input_grad = input_back(me, mix_quads, grad_one, (grad_a, grad_b, grad_c))
    if fast:
        (got_up, got_oa, got_b, got_c), input_grad = beside(
            [(send_up, 4), (send_oa, 2), (send_b, 1), (send_c, 1)], input_grad
        )
        keep_up, send_up = parted(keep_up, got_up)
        keep_oa, send_oa = parted(keep_oa, got_oa)
        two_b, two_c = parted(keep_b, got_b), parted(keep_c, got_c)
        keep_bc = jnp.concatenate([two_b[0], two_c[0]], axis=1)
        send_bc = jnp.concatenate([two_b[1], two_c[1]], axis=1)
        ((got_up, got_oa, got_bc),) = beside([(send_up, 8), (send_oa, 4), (send_bc, 2)])
        share_up = added(keep_up[0], got_up[0])
        keep_oa, send_oa = parted(keep_oa, got_oa)
        keep_bc, send_bc = parted(keep_bc, got_bc)
        ((got_oa, got_bc),) = beside([(send_oa, 8), (send_bc, 4)])
        share_oa = added(keep_oa[0], got_oa[0])
        keep_bc, send_bc = parted(keep_bc, got_bc)
        share_bc = added(keep_bc[0], swapped(send_bc, 8)[0])
        share_vec = lax.dynamic_slice(share_bc[96:108], (0, index * share), (12, share))
        shares = (share_down, share_up, share_oa, share_bc, share_vec)
        norm_shares = shares[:3] + (share_bc[:96], share_vec)
    else:

        def scattered(matrix):
            return lax.psum_scatter(
                matrix.astype(jnp.float32), "dp", scatter_dimension=0, tiled=True
            )

        mix_blocks = jnp.concatenate(
            [
                whole_rows(keep[:, :48], send[:, :48], 1)
                for keep, send in ((keep_a, send_a), (keep_b, send_b), (keep_c, send_c))
            ]
        )
        bias_mixed = jnp.concatenate([sums_a[:1], sums_b[:1], sums_c[:1]]).reshape(HG, 3, QCOLS)
        grad_vec = jnp.concatenate(
            [
                bias_mixed[:, 0].reshape(1, D),
                bias_mixed[:, 2].reshape(1, D),
                sums_one[4:7],
                sums_one[0:4],
                sums_two[0:3],
            ],
            axis=0,
        )
        shares = (
            scattered(from_heads(mix_blocks)),
            scattered(whole_rows(keep_out, send_out, 1)[0]),
            scattered(from_columns(whole_rows(keep_up, send_up, 4))),
            scattered(whole_rows(keep_down, send_down, 1)[0]),
            lax.psum_scatter(grad_vec, "dp", scatter_dimension=1, tiled=True),
        )
        norm_shares = shares

    local_square = sum(jnp.sum(s * s) for s in norm_shares)
    firsts = (first_mix[0], first_out[0], first_up[0], first_down[0], first_vectors[0])
    seconds = (second_mix[0], second_out[0], second_up[0], second_down[0], second_vectors[0])
    if fast:
        norm = jnp.broadcast_to(local_square, (8, 128))
        norm = (norm + across(norm, 0, 8)) + (across(norm, 1, 0) + across(norm, 1, 8))
        norm = (norm + across(norm, 0, 4)) + (across(norm, 0, 2) + across(norm, 0, 6))
        norm = norm + across(norm, 0, 1)
        grad_square = norm[0, 0]
        arrays = [
            pltpu.with_memory_space_constraint(a, pltpu.HBM) for a in masters + firsts + seconds
        ]
        updated = adam_all(norm, shares, arrays)
        updated = tuple(u[None] for u in updated)
    else:
        grad_square = lax.psum(local_square, ("tower", "dp"))
        factor = jnp.minimum(1.0, clip_norm / (jnp.sqrt(grad_square) + 1e-06))
        rates = (matrix_rate, matrix_rate, matrix_rate, matrix_rate, vector_rate)
        results = [
            adam_update(masters[i], shares[i], firsts[i], seconds[i], rates[i], factor)
            for i in range(5)
        ]
        updated = tuple(r[i] for i in range(3) for r in results)
    return (
        output.reshape(1, MB, 1, L, D),
        input_grad.reshape(1, MB, 1, L, D),
        *updated,
        grad_square,
    )


def solution(mesh):
    rows = P("tower", None, "dp", None, None)
    shards = (P("tower", "dp", None),) * 4 + (P("tower", None, "dp"),)
    in_specs = (rows, P("tower", None, "dp", None), P(None, "dp"), rows) + shards * 3
    out_specs = (rows, rows) + shards * 3 + (P(),)
    return jax.shard_map(body, mesh=mesh, in_specs=in_specs, out_specs=out_specs, check_vma=False)
```

```python
from functools import partial

import jax
import jax.numpy as jnp
from jax import lax
from jax.experimental import pallas as pl
from jax.experimental.pallas import tpu as pltpu
from jax.sharding import PartitionSpec as P

D = 768
FF = 3072
H = 12
HD = 64
L = 512
SEGS = 8
MB = 2
STEP = 5
HG = 3
PIECES = 16
PIECE_ROWS = D // PIECES

norm_eps = 1e-05
attention_scale = 0.125
score_scale = 0.0625
contrast_weight = 16.0
clip_norm = 1.0
beta_first = 0.9
beta_second = 0.999
adam_eps = 1e-08
weight_decay = 0.01
matrix_rate = 0.05
vector_rate = 0.5
masked_score = -1e30

low_type = jnp.bfloat16
highest = lax.Precision.HIGHEST


def swapped(value, mask):
    pairs = [(i, i ^ mask) for i in range(lax.axis_size("dp"))]
    return lax.ppermute(value, "dp", pairs)


def tower_swapped(value):
    return lax.ppermute(value, "tower", [(0, 1), (1, 0)])


def relative_of(place):
    return ((place & 1) << 3) | ((place & 2) << 1) | ((place & 4) >> 1) | (place >> 3)


def relative_y_first(place):
    return ((place & 1) << 1) | ((place & 2) << 2) | (place & 4) | (place >> 3)


def gather_pieces(own):
    pieces = own[None]
    for mask in (8, 4, 2, 1):
        pieces = jnp.concatenate([pieces, swapped(pieces, mask)])
    return pieces


def added(first, second):
    return first.astype(jnp.float32) + second.astype(jnp.float32)


def rows_dot(first_op, second_op):
    return jnp.dot(first_op, second_op, preferred_element_type=jnp.float32)


def contract_rows(first_op, second_op):
    return lax.dot_general(
        first_op, second_op, (((0,), (0,)), ((), ())), preferred_element_type=jnp.float32
    )


def contract_cols(first_op, second_op):
    return lax.dot_general(
        first_op, second_op, (((1,), (1,)), ((), ())), preferred_element_type=jnp.float32
    )


def layer_stats(values):
    centred = values - jnp.mean(values, axis=-1, keepdims=True)
    inverse = lax.rsqrt(jnp.mean(centred * centred, axis=-1, keepdims=True) + norm_eps)
    return (centred * inverse, inverse)


def norm_back(upstream, normed, inverse, gain_row):
    gained = upstream * gain_row
    return inverse * (
        gained
        - jnp.mean(gained, axis=-1, keepdims=True)
        - normed * jnp.mean(gained * normed, axis=-1, keepdims=True)
    )


def column_sum(values):
    return jnp.sum(values.astype(jnp.float32), axis=0, keepdims=True)


def gelu_parts(pre):
    below = 1.0 + (0.3275911 * 0.7071067811865476) * jnp.abs(pre)
    inner = pl.reciprocal(below, approx=True)
    inner = inner * (2.0 - below * inner)
    series = (0.5 * 1.061405429) * inner - (0.5 * 1.453152027)
    series = series * inner + (0.5 * 1.421413741)
    series = series * inner - (0.5 * 0.284496736)
    series = (series * inner + (0.5 * 0.254829592)) * inner
    bell = jnp.exp2(pre * pre * (-0.5 * log2e))
    half_tail = series * bell
    cumulative = jnp.where(pre >= 0.0, 1.0 - half_tail, half_tail)
    return (pre * cumulative, cumulative + pre * (bell * 0.3989422804014327))


log2e = 1.4426950408889634
ROWS = MB * L
QCOLS = D // HG
HEADS = H // HG
any_space = pl.BlockSpec(memory_space=pltpu.HBM)
scalar_space = pl.BlockSpec(memory_space=pltpu.SMEM)
vmem_space = pl.BlockSpec(memory_space=pltpu.VMEM)


def kept_in_hbm(array):
    return pltpu.with_memory_space_constraint(array, pltpu.HBM)


def params(megabytes):
    return pltpu.CompilerParams(vmem_limit_bytes=megabytes * 1024 * 1024)


def cost(flops, moved, exps=0):
    return pl.CostEstimate(flops=int(flops), bytes_accessed=int(moved), transcendentals=int(exps))


def start_pieces(me, quads, target, sem, order=relative_of, at=0):
    count = quads[0].shape[1]
    for place in range(PIECES):
        pltpu.make_async_copy(
            quads[place // 4].at[place % 4],
            target.at[me ^ order(place), pl.ds(at, count), :],
            sem,
        ).start()


def start_up(me, quads, quads_last, target, sem):
    start_pieces(me, quads, target, sem)
    start_pieces(me, quads_last, target, sem, relative_y_first, 4 * PIECE_ROWS)


def up_block_of(pieces, step):
    return block_of(pieces, step + step // 3)


def start_owners(me, source, keep, send, sem):
    for place in range(PIECES):
        held = keep if place < 8 else send
        pltpu.make_async_copy(
            source.at[me ^ relative_of(place)], held.at[place % 8], sem
        ).start()


def block_of(pieces, index):
    at = pl.multiple_of(index * PIECE_ROWS, 16)
    return pieces[:, pl.ds(at, PIECE_ROWS), :].reshape(D, D)


def segment_mask(seg_row):
    numbers = seg_row[...].reshape(1, L)
    columns = jnp.transpose(jnp.broadcast_to(numbers, (8, L)))[:, :1]
    return jnp.where(columns == numbers, 0.0, masked_score)


def wait_bytes(whole, sem):
    pltpu.make_async_copy(whole, whole, sem).wait()


def attention_kernel(
    me_ref, *refs
):
    quads = refs[:4]
    x_ref, seg_row, mixed_ref, ctx_ref, lse_ref, vec_ref, w, mask, bias, sems = refs[4:]
    hg, mb = pl.program_id(0), pl.program_id(1)
    me = me_ref[0]

    @pl.when((hg == 0) & (mb == 0))
    def _():
        start_pieces(me, quads, w, sems.at[0])

    @pl.when(hg == 0)
    def _():
        mask[mb] = segment_mask(seg_row)

    @pl.when((hg == 0) & (mb == 0))
    def _():
        wait_bytes(w, sems.at[0])
        vec = w[0, HG * PIECE_ROWS :, :].astype(jnp.float32)
        for place in range(1, PIECES):
            vec = vec + w[place, HG * PIECE_ROWS :, :].astype(jnp.float32)
        vec_ref[...] = vec
        for group in range(HG):
            columns = slice(group * QCOLS, (group + 1) * QCOLS)
            none = jnp.zeros((1, QCOLS), jnp.float32)
            bias[group] = jnp.concatenate([vec[0:1, columns], none, vec[1:2, columns]], axis=1)

    mixed = (rows_dot(x_ref[...], block_of(w, hg)) + bias[hg]).astype(low_type)
    mixed_ref[...] = mixed.reshape(mixed_ref.shape)
    v_t = jnp.transpose(mixed[:, 2 * QCOLS :])
    outs, totals = [], []

    def scores_of(head):
        here = slice(head * HD, (head + 1) * HD)
        q, k = mixed[:, here], mixed[:, QCOLS + head * HD : QCOLS + (head + 1) * HD]
        return contract_cols(k, q)

    ahead = scores_of(0)
    for head in range(HEADS):
        here = slice(head * HD, (head + 1) * HD)
        scores = ahead * (attention_scale * log2e) + mask[mb]
        if head + 1 < HEADS:
            ahead = scores_of(head + 1)
        largest = jnp.max(scores, axis=0, keepdims=True)
        expo = jnp.exp2(scores - largest)
        summed = jnp.sum(expo, axis=0, keepdims=True)
        probs = expo.astype(low_type)
        outs.append((rows_dot(v_t[here], probs) * (1.0 / summed)).astype(low_type))
        totals.append(largest + jnp.log(summed) * log2e)
    ctx_ref[...] = jnp.transpose(jnp.concatenate(outs, axis=0))
    lse_ref[...] = jnp.concatenate(totals, axis=0).reshape(lse_ref.shape)


def attention_forward(me, quads, x_low, seg_row):
    return pl.pallas_call(
        attention_kernel,
        grid=(HG, MB),
        in_specs=[
            scalar_space,
            *[any_space] * 4,
            pl.BlockSpec((L, D), lambda g, m: (m, 0)),
            pl.BlockSpec((1, 1, L), lambda g, m: (m, 0, 0)),
        ],
        out_specs=[
            pl.BlockSpec((1, L, D), lambda g, m: (g, m, 0)),
            pl.BlockSpec((L, QCOLS), lambda g, m: (m, g)),
            pl.BlockSpec((1, HEADS, L), lambda g, m: (g * MB + m, 0, 0)),
            pl.BlockSpec((16, D), lambda g, m: (0, 0)),
        ],
        out_shape=[
            pltpu.HBM((HG, ROWS, D), low_type),
            pltpu.HBM((ROWS, D), low_type),
            jax.ShapeDtypeStruct((HG * MB, HEADS, L), jnp.float32),
            jax.ShapeDtypeStruct((16, D), jnp.float32),
        ],
        scratch_shapes=[
            pltpu.VMEM((PIECES, HG * PIECE_ROWS + 16, D), low_type),
            pltpu.VMEM((MB, L, L), jnp.float32),
            pltpu.VMEM((HG, 1, D), jnp.float32),
            pltpu.SemaphoreType.DMA((1,)),
        ],
        compiler_params=params(40),
        cost_estimate=cost(2 * ROWS * D * 3 * D + 8 * MB * H * L * L * HD, 12e6, MB * H * L * L),
        name="mixed_attention",
    )(me, *quads, x_low, seg_row)


def up_kernel(
    me_ref,
    quad_0,
    quad_1,
    quad_2,
    quad_3,
    last_0,
    last_1,
    last_2,
    last_3,
    ctx_hbm,
    x_hbm,
    vec,
    normed_hbm,
    inverse_ref,
    hidden_hbm,
    active_ref,
    slope_ref,
    w,
    ctx,
    x,
    normed,
    hidden,
    sems,
):
    step = pl.program_id(0)
    me = me_ref[0]
    quads, quads_last = (quad_0, quad_1, quad_2, quad_3), (last_0, last_1, last_2, last_3)
    ctx_in = pltpu.make_async_copy(ctx_hbm, ctx, sems.at[1])
    x_in = pltpu.make_async_copy(x_hbm, x, sems.at[2])
    normed_out = pltpu.make_async_copy(normed, normed_hbm, sems.at[3])
    hidden_out = pltpu.make_async_copy(hidden, hidden_hbm, sems.at[4])

    @pl.when(step == 0)
    def _():
        start_up(me, quads, quads_last, w, sems.at[0])
        ctx_in.start()
        x_in.start()
        wait_bytes(w, sems.at[0])
        ctx_in.wait()
        x_in.wait()
        for first in range(0, ROWS, 256):
            part = slice(first, first + 256)
            branch = rows_dot(ctx[part, :], block_of(w, 3)) + vec[2:3, :]
            n, inv = layer_stats(x[part, :].astype(jnp.float32) + branch)
            normed[part, :] = n
            inverse_ref[part, :] = inv
            hidden[part, :] = (n * vec[3:4, :] + vec[4:5, :]).astype(low_type)
        normed_out.start()
        hidden_out.start()

    bias = vec[pl.ds(5 + step, 1), :]
    for first in range(0, ROWS, 256):
        part = slice(first, first + 256)
        pre = rows_dot(hidden[part, :], up_block_of(w, step)) + bias
        active, slope = gelu_parts(pre)
        active_ref[part, :] = active.astype(low_type)
        slope_ref[part, :] = slope.astype(low_type)

    @pl.when(step == 3)
    def _():
        normed_out.wait()
        hidden_out.wait()


def up_forward(me, quads, quads_last, context, x_low, vec):
    return pl.pallas_call(
        up_kernel,
        grid=(4,),
        in_specs=[scalar_space, *[any_space] * 10, vmem_space],
        out_specs=[
            any_space,
            pl.BlockSpec((ROWS, 1), lambda s: (0, 0)),
            any_space,
            pl.BlockSpec((ROWS, D), lambda s: (0, s)),
            pl.BlockSpec((ROWS, D), lambda s: (0, s)),
        ],
        out_shape=[
            pltpu.HBM((ROWS, D), jnp.float32),
            jax.ShapeDtypeStruct((ROWS, 1), jnp.float32),
            pltpu.HBM((ROWS, D), low_type),
            pltpu.HBM((ROWS, FF), low_type),
            pltpu.HBM((ROWS, FF), low_type),
        ],
        scratch_shapes=[
            pltpu.VMEM((PIECES, 5 * PIECE_ROWS, D), low_type),
            pltpu.VMEM((ROWS, D), low_type),
            pltpu.VMEM((ROWS, D), low_type),
            pltpu.VMEM((ROWS, D), jnp.float32),
            pltpu.VMEM((ROWS, D), low_type),
            pltpu.SemaphoreType.DMA((5,)),
        ],
        compiler_params=params(44),
        cost_estimate=cost(2 * ROWS * D * (FF + D), 24e6, 2 * ROWS * FF),
        name="out_up",
    )(me, *quads, *quads_last, context, x_low, vec)


def down_kernel(
    me_ref,
    quad_0,
    quad_1,
    quad_2,
    quad_3,
    active_hbm,
    normed_one_hbm,
    vec,
    table_ref,
    normed_hbm,
    inverse_ref,
    output_hbm,
    cls_ref,
    w,
    active,
    normed_one,
    normed,
    output,
    sems,
):
    me = me_ref[0]
    start_pieces(me, (quad_0, quad_1, quad_2, quad_3), w, sems.at[0])
    arrivals, departures = [], []
    for index in range(4):
        part = pl.ds(index * 256, 256)
        arrivals.append(
            (
                pltpu.make_async_copy(
                    active_hbm.at[part, :], active.at[part, :], sems.at[1 + index]
                ),
                pltpu.make_async_copy(
                    normed_one_hbm.at[part, :], normed_one.at[part, :], sems.at[5 + index]
                ),
            )
        )
        departures.append(
            (
                pltpu.make_async_copy(
                    normed.at[part, :], normed_hbm.at[part, :], sems.at[9 + index]
                ),
                pltpu.make_async_copy(
                    output.at[part, :], output_hbm.at[part, :], sems.at[13 + index]
                ),
            )
        )
        for arrival in arrivals[index]:
            arrival.start()
    wait_bytes(w, sems.at[0])
    for index in range(4):
        for arrival in arrivals[index]:
            arrival.wait()
        part = slice(index * 256, (index + 1) * 256)
        ffn = rows_dot(active[part, :], w[...].reshape(FF, D)) + vec[9:10, :]
        residual = normed_one[part, :] * vec[3:4, :] + vec[4:5, :]
        n, inv = layer_stats(residual + ffn)
        normed[part, :] = n
        inverse_ref[part, :] = inv
        output[part, :] = (n * vec[10:11, :] + vec[11:12, :]).astype(low_type)
        for departure in departures[index]:
            departure.start()
    cls_ref[...] = rows_dot(table_ref[...], output[...]).astype(low_type)
    for pair in departures:
        for departure in pair:
            departure.wait()


def down_forward(me, quads, active, normed_one, vec, table):
    return pl.pallas_call(
        down_kernel,
        in_specs=[scalar_space, *[any_space] * 6, vmem_space, vmem_space],
        out_specs=[any_space, vmem_space, any_space, vmem_space],
        out_shape=[
            pltpu.HBM((ROWS, D), jnp.float32),
            jax.ShapeDtypeStruct((ROWS, 1), jnp.float32),
            pltpu.HBM((ROWS, D), low_type),
            jax.ShapeDtypeStruct((MB * SEGS, D), low_type),
        ],
        scratch_shapes=[
            pltpu.VMEM((PIECES, 4 * PIECE_ROWS, D), low_type),
            pltpu.VMEM((ROWS, FF), low_type),
            pltpu.VMEM((ROWS, D), jnp.float32),
            pltpu.VMEM((ROWS, D), jnp.float32),
            pltpu.VMEM((ROWS, D), low_type),
            pltpu.SemaphoreType.DMA((17,)),
        ],
        compiler_params=params(40),
        cost_estimate=cost(2 * ROWS * D * FF, 19e6),
        name="down",
    )(me, *quads, kept_in_hbm(active), kept_in_hbm(normed_one), vec, table)


def contrast_kernel(flag_ref, all_ref, positive_ref, ids_ref, grad_ref):
    passage_here = flag_ref[0] == 1
    for batch in range(MB):
        mine, theirs = all_ref[0, batch], all_ref[1, batch]
        queries = jnp.where(passage_here, theirs, mine)
        passages = jnp.where(passage_here, mine, theirs)
        contrast = contract_cols(queries, passages) * score_scale
        top = jnp.max(contrast, axis=-1, keepdims=True)
        expo = jnp.exp(contrast - top)
        probs = expo / jnp.sum(expo, axis=-1, keepdims=True)
        chosen = (positive_ref[batch] == ids_ref[...]).astype(jnp.float32)
        grad = (contrast_weight * (probs - chosen)).astype(low_type)
        for_query = rows_dot(grad[:16], passages) * score_scale
        for_query = for_query.astype(low_type).astype(jnp.float32)
        for_passage = contract_rows(grad, queries)[:16] * score_scale
        taken = jnp.where(passage_here, for_passage, for_query)
        grad_ref[batch * SEGS : (batch + 1) * SEGS, :] = taken[:SEGS]


def contrast_back(flag, everyone, cls_positives, cls_ids):
    return pl.pallas_call(
        contrast_kernel,
        in_specs=[scalar_space, vmem_space, vmem_space, vmem_space],
        out_specs=vmem_space,
        out_shape=jax.ShapeDtypeStruct((MB * SEGS, D), jnp.float32),
        compiler_params=params(48),
        name="contrast",
    )(flag, everyone, cls_positives, cls_ids)


def down_back_kernel(
    me_ref,
    token_grad_hbm,
    grad_cls,
    table3_ref,
    normed_hbm,
    inverse_ref,
    vec,
    active_ref,
    residual_hbm,
    low_ref,
    sums_ref,
    keep,
    send,
    low,
    token_grad,
    normed,
    residual,
    staged,
    sems,
):
    step = pl.program_id(0)
    me = me_ref[0]
    residual_out = pltpu.make_async_copy(residual, residual_hbm, sems.at[8])

    @pl.when(step == 0)
    def _():
        arrivals = []
        for index in range(4):
            part = pl.ds(index * 256, 256)
            arrivals.append(
                (
                    pltpu.make_async_copy(
                        token_grad_hbm.at[part, :], token_grad.at[part, :], sems.at[index]
                    ),
                    pltpu.make_async_copy(
                        normed_hbm.at[part, :], normed.at[part, :], sems.at[4 + index]
                    ),
                )
            )
            for arrival in arrivals[index]:
                arrival.start()
        grads = grad_cls[...]
        upper = grads.astype(low_type)
        rest = grads - upper.astype(jnp.float32)
        middle = rest.astype(low_type)
        lower = (rest - middle.astype(jnp.float32)).astype(low_type)
        stacked = jnp.concatenate([upper, middle, lower], axis=0)
        gains = jnp.zeros((1, D), jnp.float32)
        shifts = jnp.zeros((1, D), jnp.float32)
        biases = jnp.zeros((1, D), jnp.float32)
        for index in range(4):
            part = slice(index * 256, (index + 1) * 256)
            for arrival in arrivals[index]:
                arrival.wait()
            upstream = token_grad[part, :] + contract_rows(table3_ref[:, part], stacked)
            n = normed[part, :]
            gains = gains + column_sum(upstream * n)
            shifts = shifts + column_sum(upstream)
            grad = norm_back(upstream, n, inverse_ref[part, :], vec[10:11, :])
            residual[part, :] = grad
            rounded = grad.astype(low_type)
            biases = biases + column_sum(rounded)
            low[part, :] = rounded
        residual_out.start()
        low_ref[...] = low[...]
        sums_ref[...] = jnp.concatenate([biases, gains, shifts, jnp.zeros((5, D), jnp.float32)])

    for first in range(4):
        at = first * 4 * PIECE_ROWS
        staged[4 * step + first] = contract_rows(
            active_ref[:, at : at + 4 * PIECE_ROWS], low[...]
        ).astype(low_type)

    @pl.when(step == 3)
    def _():
        start_owners(me, staged, keep, send, sems.at[9])
        residual_out.wait()
        wait_bytes(staged, sems.at[9])


def down_back(me, token_grad, grad_cls, table3, normed, inverse, vec, active):
    half = jax.ShapeDtypeStruct((8, 4 * PIECE_ROWS, D), low_type)
    return pl.pallas_call(
        down_back_kernel,
        grid=(4,),
        in_specs=[
            scalar_space,
            any_space,
            vmem_space,
            vmem_space,
            any_space,
            vmem_space,
            vmem_space,
            pl.BlockSpec((ROWS, D), lambda s: (0, s)),
        ],
        out_specs=[any_space] + [vmem_space] * 2 + [any_space] * 2,
        out_shape=[
            pltpu.HBM((ROWS, D), jnp.float32),
            jax.ShapeDtypeStruct((ROWS, D), low_type),
            jax.ShapeDtypeStruct((8, D), jnp.float32),
            half,
            half,
        ],
        scratch_shapes=[
            pltpu.VMEM((ROWS, D), low_type),
            pltpu.VMEM((ROWS, D), jnp.float32),
            pltpu.VMEM((ROWS, D), jnp.float32),
            pltpu.VMEM((ROWS, D), jnp.float32),
            pltpu.VMEM((PIECES, 4 * PIECE_ROWS, D), low_type),
            pltpu.SemaphoreType.DMA((10,)),
        ],
        compiler_params=params(44),
        cost_estimate=cost(2 * ROWS * D * FF, 25e6),
        name="down_back",
    )(
        me,
        kept_in_hbm(token_grad),
        grad_cls,
        table3,
        kept_in_hbm(normed),
        inverse,
        vec,
        kept_in_hbm(active),
    )


def up_back_kernel(
    me_ref,
    up_0,
    up_1,
    up_2,
    up_3,
    last_0,
    last_1,
    last_2,
    last_3,
    down_0,
    down_1,
    down_2,
    down_3,
    low_ref,
    slope_ref,
    hidden_ref,
    residual_hbm,
    normed_hbm,
    inverse_ref,
    ctx_hbm,
    vec,
    grad_one_hbm,
    grad_ctx_ref,
    sums_ref,
    keep,
    send,
    keep_out,
    send_out,
    up_w,
    down_w,
    normed,
    ctx,
    total,
    staged,
    staged_out,
    bias_sums,
    sems,
):
    step = pl.program_id(0)
    me = me_ref[0]
    residual_in = pltpu.make_async_copy(residual_hbm, total, sems.at[2])
    normed_in = pltpu.make_async_copy(normed_hbm, normed, sems.at[3])
    ctx_in = pltpu.make_async_copy(ctx_hbm, ctx, sems.at[4])

    @pl.when(step == 0)
    def _():
        start_pieces(me, (down_0, down_1, down_2, down_3), down_w, sems.at[0])
        last = (last_0, last_1, last_2, last_3)
        start_up(me, (up_0, up_1, up_2, up_3), last, up_w, sems.at[1])
        residual_in.start()
        normed_in.start()
        ctx_in.start()
        wait_bytes(down_w, sems.at[0])

    down_block = down_w[pl.ds(4 * step, 4)].reshape(D, D)
    biases = jnp.zeros((1, D), jnp.float32)
    grads = []
    for first in range(0, ROWS, 256):
        part = slice(first, first + 256)
        active_grad = contract_cols(low_ref[part, :], down_block)
        grad = (active_grad * slope_ref[part, :].astype(jnp.float32)).astype(low_type)
        biases = biases + column_sum(grad)
        grads.append(grad)
    grad = jnp.concatenate(grads, axis=0)

    @pl.when(step == 0)
    def _():
        wait_bytes(up_w, sems.at[1])
        residual_in.wait()

    total[...] += contract_cols(grad, up_block_of(up_w, step))
    at = pl.multiple_of(step * PIECE_ROWS, 16)
    for first in range(0, PIECES, 4):
        columns = slice(first * PIECE_ROWS, (first + 4) * PIECE_ROWS)
        terms = contract_rows(hidden_ref[:, columns], grad).astype(low_type)
        staged[first : first + 4, pl.ds(at, PIECE_ROWS), :] = terms.reshape(4, PIECE_ROWS, D)
    bias_sums[step] = biases

    @pl.when(step == 3)
    def _():
        start_owners(me, staged, keep, send, sems.at[5])
        normed_in.wait()
        ctx_in.wait()
        gains = jnp.zeros((1, D), jnp.float32)
        shifts = jnp.zeros((1, D), jnp.float32)
        out_biases = jnp.zeros((1, D), jnp.float32)
        lows, departures = [], []
        for first in range(0, ROWS, 256):
            part = slice(first, first + 256)
            upstream = total[part, :]
            n = normed[part, :]
            gains = gains + column_sum(upstream * n)
            shifts = shifts + column_sum(upstream)
            grad_one = norm_back(upstream, n, inverse_ref[part, :], vec[3:4, :])
            total[part, :] = grad_one
            departures.append(
                pltpu.make_async_copy(
                    total.at[part, :], grad_one_hbm.at[part, :], sems.at[7 + first // 256]
                )
            )
            departures[-1].start()
            rounded = grad_one.astype(low_type)
            out_biases = out_biases + column_sum(rounded)
            grad_ctx_ref[part, :] = contract_cols(rounded, block_of(up_w, 3)).astype(low_type)
            lows.append(rounded)
        sums_ref[...] = jnp.concatenate(
            [bias_sums[block] for block in range(4)]
            + [out_biases, gains, shifts, jnp.zeros((1, D), jnp.float32)]
        )
        rounded = jnp.concatenate(lows, axis=0)
        for first in range(0, PIECES, 4):
            columns = slice(first * PIECE_ROWS, (first + 4) * PIECE_ROWS)
            terms = contract_rows(ctx[:, columns], rounded).astype(low_type)
            staged_out[first : first + 4] = terms.reshape(4, PIECE_ROWS, D)
        start_owners(me, staged_out, keep_out, send_out, sems.at[6])
        wait_bytes(staged, sems.at[5])
        wait_bytes(staged_out, sems.at[6])
        for departure in departures:
            departure.wait()


def up_back(
    me, up_quads, up_last, down_quads, low, slope, hidden, residual, normed, inverse, ctx, vec
):
    half = jax.ShapeDtypeStruct((8, 4 * PIECE_ROWS, D), low_type)
    half_out = jax.ShapeDtypeStruct((8, PIECE_ROWS, D), low_type)
    return pl.pallas_call(
        up_back_kernel,
        grid=(4,),
        in_specs=[scalar_space]
        + [any_space] * 12
        + [
            vmem_space,
            pl.BlockSpec((ROWS, D), lambda s: (0, s)),
            vmem_space,
            any_space,
            any_space,
            vmem_space,
            any_space,
            vmem_space,
        ],
        out_specs=[any_space] + [vmem_space] * 2 + [any_space] * 4,
        out_shape=[
            pltpu.HBM((ROWS, D), jnp.float32),
            jax.ShapeDtypeStruct((ROWS, D), low_type),
            jax.ShapeDtypeStruct((8, D), jnp.float32),
            half,
            half,
            half_out,
            half_out,
        ],
        scratch_shapes=[
            pltpu.VMEM((PIECES, 5 * PIECE_ROWS, D), low_type),
            pltpu.VMEM((PIECES, 4 * PIECE_ROWS, D), low_type),
            pltpu.VMEM((ROWS, D), jnp.float32),
            pltpu.VMEM((ROWS, D), low_type),
            pltpu.VMEM((ROWS, D), jnp.float32),
            pltpu.VMEM((PIECES, 4 * PIECE_ROWS, D), low_type),
            pltpu.VMEM((PIECES, PIECE_ROWS, D), low_type),
            pltpu.VMEM((4, 1, D), jnp.float32),
            pltpu.SemaphoreType.DMA((11,)),
        ],
        compiler_params=params(56),
        cost_estimate=cost(2 * ROWS * D * (3 * FF + 2 * D), 40e6),
        name="up_back",
    )(
        me,
        *up_quads,
        *up_last,
        *down_quads,
        low,
        slope,
        hidden,
        residual,
        normed,
        inverse,
        ctx,
        vec,
    )


def attention_back_kernel(
    me_ref,
    x_ref,
    seg_row,
    mixed_ref,
    lse_ref,
    grad_ctx_ref,
    *refs,
):
    others, (grad_mixed_ref, sums_ref, keep, send, weight_grad, staged, sem) = refs[:-7], refs[-7:]
    mb = pl.program_id(0)
    me = me_ref[0]
    mask = segment_mask(seg_row)
    mixed = mixed_ref[...].reshape(L, D)
    lse = lse_ref[...].reshape(HEADS, L)
    k_t = jnp.transpose(mixed[:, QCOLS : 2 * QCOLS])
    grad_q, grad_k, grad_v = [], [], []

    def products_of(head):
        here = slice(head * HD, (head + 1) * HD)
        q, k = mixed[:, here], mixed[:, QCOLS + head * HD : QCOLS + (head + 1) * HD]
        v = mixed[:, 2 * QCOLS + head * HD : 2 * QCOLS + (head + 1) * HD]
        return (contract_cols(k, q), contract_cols(v, grad_ctx_ref[:, here]))

    ahead = products_of(0)
    for head in range(HEADS):
        here = slice(head * HD, (head + 1) * HD)
        scores, grad_probs = ahead
        if head + 1 < HEADS:
            ahead = products_of(head + 1)
        scores = scores * (attention_scale * log2e) + mask
        probs = jnp.exp2(scores - lse[head : head + 1])
        inner = jnp.sum(probs * grad_probs, axis=0, keepdims=True)
        grad_scores = (probs * (grad_probs - inner)).astype(low_type)
        grad_v.append(rows_dot(probs.astype(low_type), grad_ctx_ref[:, here]).astype(low_type))
        grad_q.append((rows_dot(k_t[here], grad_scores) * attention_scale).astype(low_type))
        grad_k.append((rows_dot(grad_scores, mixed[:, here]) * attention_scale).astype(low_type))
    grad_mixed = jnp.concatenate(
        [jnp.transpose(jnp.concatenate(grad_q, axis=0))] + grad_k + grad_v, axis=1
    )

    grad_mixed_ref[...] = grad_mixed
    bias = column_sum(grad_mixed)
    terms = contract_rows(x_ref[...], grad_mixed)

    @pl.when(mb == 0)
    def _():
        weight_grad[...] = terms
        sums_ref[0:1, :] = bias

    @pl.when(mb == 1)
    def _():
        sums_ref[0:1, :] += bias
        grads = (weight_grad[...] + terms).astype(low_type)
        staged[:, :PIECE_ROWS, :] = grads.reshape(PIECES, PIECE_ROWS, D)
        if others:
            mixed_a, mixed_b, up, down = (other[...] for other in others)
            mixed_sums = (mixed_a[0:1], mixed_b[0:1], sums_ref[0:1, :])
            vectors = jnp.concatenate(
                [
                    jnp.concatenate([s[:, :QCOLS] for s in mixed_sums], axis=1),
                    jnp.concatenate([s[:, 2 * QCOLS :] for s in mixed_sums], axis=1),
                    up[4:7],
                    up[0:4],
                    down[0:3],
                    jnp.zeros((4, D), jnp.float32),
                ],
                axis=0,
            )
            for place in range(PIECES):
                staged[place, PIECE_ROWS:, :] = vectors.astype(low_type)
        start_owners(me, staged, keep, send, sem)
        wait_bytes(staged, sem)


def attention_back(me, x_low, seg_row, mixed, lse, grad_ctx, group, *others):
    rows = PIECE_ROWS + (16 if others else 0)
    half = jax.ShapeDtypeStruct((8, rows, D), low_type)
    return pl.pallas_call(
        attention_back_kernel,
        grid=(MB,),
        in_specs=[
            scalar_space,
            pl.BlockSpec((L, D), lambda m: (m, 0)),
            pl.BlockSpec((1, 1, L), lambda m: (m, 0, 0)),
            pl.BlockSpec((1, L, D), lambda m: (group, m, 0)),
            pl.BlockSpec((1, HEADS, L), lambda m: (group * MB + m, 0, 0)),
            pl.BlockSpec((L, QCOLS), lambda m: (m, group)),
            *[vmem_space] * len(others),
        ],
        out_specs=[pl.BlockSpec((L, D), lambda m: (m, 0)), vmem_space, any_space, any_space],
        out_shape=[
            jax.ShapeDtypeStruct((ROWS, D), low_type),
            jax.ShapeDtypeStruct((8, D), jnp.float32),
            half,
            half,
        ],
        scratch_shapes=[
            pltpu.VMEM((D, D), jnp.float32),
            pltpu.VMEM((PIECES, rows, D), low_type),
            pltpu.SemaphoreType.DMA,
        ],
        compiler_params=params(40),
        cost_estimate=cost(
            2 * ROWS * D * D + 20 * MB * HEADS * L * L * HD, 12e6, MB * HEADS * L * L
        ),
        name=f"attention_back_{group}",
    )(me, x_low, seg_row, kept_in_hbm(mixed), lse, grad_ctx, *others)


def input_back_kernel(
    me_ref, quad_0, quad_1, quad_2, quad_3, one_ref, grad_0, grad_1, grad_2, input_ref, w, sem
):
    @pl.when(pl.program_id(0) == 0)
    def _():
        start_pieces(me_ref[0], (quad_0, quad_1, quad_2, quad_3), w, sem)
        wait_bytes(w, sem)

    total = one_ref[...]
    for block, grad in enumerate((grad_0, grad_1, grad_2)):
        total = total + contract_cols(grad[...], block_of(w, block))
    input_ref[...] = total


def input_back(me, quads, grad_one, grads):
    rows = pl.BlockSpec((256, D), lambda s: (s, 0))
    return pl.pallas_call(
        input_back_kernel,
        grid=(ROWS // 256,),
        in_specs=[scalar_space] + [any_space] * 4 + [rows] * 4,
        out_specs=rows,
        out_shape=jax.ShapeDtypeStruct((ROWS, D), jnp.float32),
        scratch_shapes=[
            pltpu.VMEM((PIECES, HG * PIECE_ROWS + 16, D), low_type),
            pltpu.SemaphoreType.DMA,
        ],
        compiler_params=params(24),
        cost_estimate=cost(6 * ROWS * D * D, 14e6),
        name="input_back",
    )(me, *quads, grad_one, *grads)


def adam_kernel(norm_ref, down_ref, up_ref, out_mix, mix_bc, vec_ref, *refs):
    ins, outs, held, sems = refs[:15], refs[15:30], refs[30:45], refs[45]
    arrivals = [
        pltpu.make_async_copy(ins[i], held[i], sems.at[i]) for i in range(15)
    ]
    departures = [
        pltpu.make_async_copy(held[i], outs[i], sems.at[i]) for i in range(15)
    ]
    order = (3, 2, 0, 1, 4)
    for index in order:
        for i in (index, 5 + index, 10 + index):
            arrivals[i].start()
    factor = jnp.minimum(1.0, clip_norm / (jnp.sqrt(norm_ref[0:1, 0:1]) + 1e-06))[0, 0]

    def update(index, at, grad, rate):
        master, first, second = held[index], held[5 + index], held[10 + index]
        clipped = grad * factor
        first_new = beta_first * first[at] + (1.0 - beta_first) * clipped
        second_new = beta_second * second[at] + (1.0 - beta_second) * clipped * clipped
        root = jnp.sqrt(second_new / (1.0 - beta_second**STEP)) + adam_eps
        step = first_new / (1.0 - beta_first**STEP) / root
        old = master[at]
        master[at] = old - rate * (step + weight_decay * old)
        first[at] = first_new
        second[at] = second_new

    for index in order:
        for i in (index, 5 + index, 10 + index):
            arrivals[i].wait()
        if index == 0:
            one, two = PIECE_ROWS, 2 * PIECE_ROWS
            parts = (out_mix[one:two, :], mix_bc[:one, :], mix_bc[one:two, :])
            for group, share in enumerate(parts):
                for third in range(3):
                    column = third * D + group * QCOLS
                    grad = share[:, third * QCOLS : (third + 1) * QCOLS]
                    update(0, (slice(None), slice(column, column + QCOLS)), grad, matrix_rate)
        elif index == 1:
            update(1, (slice(None), slice(0, D)), out_mix[:PIECE_ROWS, :], matrix_rate)
        elif index == 2:
            for block in range(4):
                grad = up_ref[block * PIECE_ROWS : (block + 1) * PIECE_ROWS, :]
                columns = slice(block * D, (block + 1) * D)
                update(2, (slice(None), columns), grad, matrix_rate)
        elif index == 3:
            update(3, (slice(None), slice(0, D)), down_ref[...], matrix_rate)
        else:
            update(4, ..., vec_ref[...], vector_rate)
        for i in (index, 5 + index, 10 + index):
            departures[i].start()
    for departure in departures:
        departure.wait()


def adam_all(norm, shares, arrays):
    return pl.pallas_call(
        adam_kernel,
        in_specs=[vmem_space] * 6 + [any_space] * 15,
        out_specs=[any_space] * 15,
        out_shape=[jax.ShapeDtypeStruct(a.shape, jnp.float32) for a in arrays],
        scratch_shapes=[pltpu.VMEM(a.shape, jnp.float32) for a in arrays]
        + [pltpu.SemaphoreType.DMA((15,))],
        compiler_params=params(40),
        cost_estimate=cost(40e6, 25e6),
        name="adam",
    )(norm, *shares, *arrays)


def by_heads(matrix):
    shaped = matrix.reshape(matrix.shape[0], 3, HG, D // HG)
    return jnp.transpose(shaped, (2, 0, 1, 3)).reshape(HG, matrix.shape[0], D)


def from_heads(blocks):
    rows = blocks.shape[1]
    shaped = blocks.reshape(HG, rows, 3, D // HG)
    return jnp.transpose(shaped, (1, 2, 0, 3)).reshape(rows, 3 * D)


def by_columns(matrix):
    return jnp.transpose(matrix.reshape(matrix.shape[0], 4, D), (1, 0, 2))


def from_columns(blocks):
    return jnp.transpose(blocks, (1, 0, 2)).reshape(blocks.shape[1], 4 * D)


def adam_update(master, grad_share, first, second, rate, factor):
    clipped = grad_share * factor
    first_new = beta_first * first + (1.0 - beta_first) * clipped
    second_new = beta_second * second + (1.0 - beta_second) * clipped * clipped
    first_hat = first_new / (1.0 - beta_first**STEP)
    second_hat = second_new / (1.0 - beta_second**STEP)
    master_new = master - rate * (
        first_hat / (jnp.sqrt(second_hat) + adam_eps) + weight_decay * master
    )
    return (master_new[None], first_new[None], second_new[None])


def quads_of(matrix_rows):
    k = matrix_rows.shape[0]
    shaped = matrix_rows.reshape(k, 2, 2, 2, 2, -1, D)
    pieces = jnp.transpose(shaped, (4, 3, 2, 1, 0, 5, 6)).reshape(4, 4, -1, D)
    return tuple(pieces[i] for i in range(4))


def whole_rows(keep, send, k):
    shaped = jnp.concatenate([keep, send]).reshape(2, 2, 2, 2, k, -1, D)
    return jnp.transpose(shaped, (4, 3, 2, 1, 0, 5, 6)).reshape(k, -1, D)


def beside(sends, *work):
    received = [swapped(value, mask) for value, mask in sends]
    done = lax.optimization_barrier((received, work))
    return (done[0], *done[1])


def across(value, tower_mask, dp_mask):
    owners = lax.axis_size("dp")
    flip = tower_mask * owners + dp_mask
    pairs = [(i, i ^ flip) for i in range(2 * owners)]
    return lax.ppermute(value, ("tower", "dp"), pairs)


def joined(pieces, received):
    return jnp.concatenate([pieces, received])


def parted(keep, received):
    half = keep.shape[0] // 2
    return (
        added(keep[:half], received[:half]).astype(low_type),
        added(keep[half:], received[half:]).astype(low_type),
    )


def body(
    tokens,
    segments,
    positives,
    token_grad,
    mix_weight,
    out_weight,
    up_weight,
    down_weight,
    vectors,
    first_mix,
    first_out,
    first_up,
    first_down,
    first_vectors,
    second_mix,
    second_out,
    second_up,
    second_down,
    second_vectors,
):
    owners = lax.axis_size("dp")
    fast = owners == PIECES
    index = lax.axis_index("dp")
    flag = lax.axis_index("tower").astype(jnp.int32).reshape(1)
    masters = (mix_weight[0], out_weight[0], up_weight[0], down_weight[0], vectors[0])
    low_mix, low_out, low_up, low_down, low_vec = (m.astype(low_type) for m in masters)
    share = low_vec.shape[1]
    queries_all = owners * SEGS

    if fast:
        me = index.astype(jnp.int32).reshape(1)
        extra = jnp.zeros((16, D), low_type)
        extra = extra.at[12:14, :SEGS].set(positives.astype(low_type))
        extra = lax.dynamic_update_slice(extra, low_vec, (0, index * share))
        pack_mix = jnp.concatenate([by_heads(low_mix).reshape(-1, D), extra])
        low_blocks = by_columns(low_up)
        pack_up = jnp.concatenate([low_blocks[:3].reshape(-1, D), low_out])
        mix, up, last, down = pack_mix[None], pack_up[None], low_blocks[3:], low_down[None]
        ((got_mix, got_last),) = beside([(mix, 8), (last, 2)])
        mix, last = joined(mix, got_mix), joined(last, got_last)
        ((got_mix, got_up),) = beside([(mix, 4), (up, 8)])
        mix, up = joined(mix, got_mix), joined(up, got_up)
        ((mix_y, mix_core, got_up, got_last, got_down),) = beside(
            [(mix, 2), (mix, 1), (up, 4), (last, 8), (down, 8)]
        )
        up, last, down = joined(up, got_up), joined(last, got_last), joined(down, got_down)
        mix_quads = (mix, mix_y, mix_core, swapped(mix_y, 1))
        extras = jnp.concatenate([quad[:, 156:158, :SEGS] for quad in mix_quads])
        cls_positives = jnp.transpose(extras.astype(jnp.int32), (1, 0, 2))
        cls_positives = cls_positives.reshape(MB, queries_all, 1)
        relative = relative_of(jnp.arange(PIECES, dtype=jnp.int32))
        cls_ids = ((relative ^ index)[:, None] * SEGS + jnp.arange(SEGS)[None, :]).reshape(1, -1)
    else:
        me = jnp.zeros((1,), jnp.int32)
        mix_quads = quads_of(by_heads(lax.all_gather(low_mix, "dp", axis=0, tiled=True)))
        up_blocks = by_columns(lax.all_gather(low_up, "dp", axis=0, tiled=True))
        out_block = lax.all_gather(low_out, "dp", axis=0, tiled=True)[None]
        up_quads = quads_of(jnp.concatenate([up_blocks[:3], out_block]))
        up_last = jnp.concatenate(quads_of(up_blocks[3:]))
        up_last = jnp.stack(
            [up_last[relative_of(relative_y_first(place))] for place in range(PIECES)]
        ).reshape(4, 4, PIECE_ROWS, D)
        up_last = tuple(up_last[i] for i in range(4))
        down_quads = quads_of(lax.all_gather(low_down, "dp", axis=0, tiled=True)[None])
        vec_low = lax.all_gather(low_vec, "dp", axis=1, tiled=True)
        extra = jnp.zeros((PIECES, 16, D), low_type).at[0, :12].set(vec_low)
        mix_quads = tuple(
            jnp.concatenate([quad, extra[4 * i : 4 * i + 4]], axis=1)
            for i, quad in enumerate(mix_quads)
        )
        cls_positives = lax.all_gather(positives, "dp", axis=1, tiled=True)
        cls_positives = jnp.roll(cls_positives, -index * SEGS, axis=1)[:, :, None]
        cls_ids = jnp.roll(jnp.arange(queries_all, dtype=jnp.int32), -index * SEGS)[None]

    x_low = tokens[0].reshape(ROWS, D)
    seg_rows = segments[0].reshape(MB, L)
    seg_row = seg_rows.reshape(MB, 1, L)
    before = jnp.concatenate([jnp.full((MB, 1), -1, jnp.int32), seg_rows[:, :-1]], axis=1)
    numbers = jnp.where(seg_rows != before, seg_rows, -1)
    numbers = jnp.where(numbers >= 0, numbers + SEGS * jnp.arange(MB)[:, None], -1).reshape(1, ROWS)
    table = (jnp.arange(MB * SEGS)[:, None] == numbers).astype(low_type)
    mixed, context, lse, vec_f = attention_forward(me, mix_quads, x_low, seg_row)
    if fast:
        (up_y, up_core, last_z, last_core, got_down), mixed, context, lse, vec_f = beside(
            [(up, 2), (up, 1), (last, 4), (last, 1), (down, 4)], mixed, context, lse, vec_f
        )
        down = joined(down, got_down)
        up_quads = (up, up_y, up_core, swapped(up_y, 1))
        up_last = (last, last_z, last_core, swapped(last_z, 1))
    normed_one, inverse_one, hidden, active, slope = up_forward(
        me, up_quads, up_last, context, x_low, vec_f
    )
    if fast:
        (down_y, down_core), normed_one, hidden, active, slope = beside(
            [(down, 2), (down, 1)], normed_one, hidden, active, slope
        )
        down_quads = (down, down_y, down_core, swapped(down_y, 1))
    normed_two, inverse_two, output, cls_low = down_forward(
        me, down_quads, active, normed_one, vec_f, table
    )

    if fast:
        first = [cls_low] + [across(cls_low, t, m) for t, m in ((0, 8), (1, 0), (1, 8))]
        four = jnp.stack(first).reshape(2, 2, MB, SEGS, D)
        second = [four] + [across(four, 0, m) for m in (4, 2, 6)]
        eight = jnp.stack(second)
        everyone = jnp.stack([eight, across(eight, 0, 1)])
        everyone = jnp.transpose(everyone, (2, 4, 0, 1, 3, 5, 6))
    else:
        both = jnp.concatenate([cls_low, tower_swapped(cls_low)])
        everyone = jnp.roll(lax.all_gather(both, "dp", axis=0, tiled=False), -index, axis=0)
        everyone = jnp.transpose(everyone.reshape(owners, 2, MB, SEGS, D), (1, 2, 0, 3, 4))
    everyone = everyone.reshape(2, MB, queries_all, D)
    grad_cls = contrast_back(flag, everyone, cls_positives, cls_ids)

    residual, grad_ffn, sums_two, keep_down, send_down = down_back(
        me,
        token_grad[0].reshape(ROWS, D),
        grad_cls,
        jnp.concatenate([table] * 3),
        normed_two,
        inverse_two,
        vec_f,
        active,
    )
    if fast:
        (got_down,), residual, grad_ffn = beside([(send_down, 1)], residual, grad_ffn)
        keep_down, send_down = parted(keep_down, got_down)
    grad_one, grad_ctx, sums_one, keep_up, send_up, keep_out, send_out = up_back(
        me,
        up_quads,
        up_last,
        down_quads,
        grad_ffn,
        slope,
        hidden,
        residual,
        normed_one,
        inverse_one,
        context,
        vec_f,
    )
    if fast:
        (got_down,), grad_one, grad_ctx, send_up, send_out = beside(
            [(send_down, 2)], grad_one, grad_ctx, send_up, send_out
        )
        keep_down, send_down = parted(keep_down, got_down)
    back = partial(attention_back, me, x_low, seg_row, mixed, lse)
    grad_a, sums_a, keep_a, send_a = back(grad_ctx, 0)
    if fast:
        (got_down, got_up, got_out), grad_ctx, send_a = beside(
            [(send_down, 4), (send_up, 1), (send_out, 1)], grad_ctx, send_a
        )
        keep_down, send_down = parted(keep_down, got_down)
        keep_up, send_up = parted(keep_up, got_up)
        keep_out, send_out = parted(keep_out, got_out)
    grad_b, sums_b, keep_b, send_b = back(grad_ctx, 1)
    grad_c, sums_c, keep_c, send_c = back(grad_ctx, 2, sums_a, sums_b, sums_one, sums_two)
    if fast:
        (got_down, got_up, got_a), grad_b, grad_c, send_b, send_c = beside(
            [(send_down, 8), (send_up, 2), (send_a, 1)], grad_b, grad_c, send_b, send_c
        )
        share_down = added(keep_down[0], got_down[0])
        keep_up, send_up = parted(keep_up, got_up)
        two_a = parted(keep_a, got_a)
        keep_oa = jnp.concatenate([keep_out, two_a[0]], axis=1)
        send_oa = jnp.concatenate([send_out, two_a[1]], axis=1)
    if fast:
        (got_up, got_oa, got_b, got_c), grad_c = beside(
            [(send_up, 4), (send_oa, 2), (send_b, 1), (send_c, 1)], grad_c
        )
        keep_up, send_up = parted(keep_up, got_up)
        keep_oa, send_oa = parted(keep_oa, got_oa)
        two_b, two_c = parted(keep_b, got_b), parted(keep_c, got_c)
        keep_bc = jnp.concatenate([two_b[0], two_c[0]], axis=1)
        send_bc = jnp.concatenate([two_b[1], two_c[1]], axis=1)
    input_grad = input_back(me, mix_quads, grad_one, (grad_a, grad_b, grad_c))
    if fast:
        (got_up, got_oa, got_bc), input_grad = beside(
            [(send_up, 8), (send_oa, 4), (send_bc, 2)], input_grad
        )
        share_up = added(keep_up[0], got_up[0])
        keep_oa, send_oa = parted(keep_oa, got_oa)
        keep_bc, send_bc = parted(keep_bc, got_bc)
        ((got_oa, got_bc),) = beside([(send_oa, 8), (send_bc, 4)])
        share_oa = added(keep_oa[0], got_oa[0])
        keep_bc, send_bc = parted(keep_bc, got_bc)
        share_bc = added(keep_bc[0], swapped(send_bc, 8)[0])
        share_vec = lax.dynamic_slice(share_bc[96:108], (0, index * share), (12, share))
        shares = (share_down, share_up, share_oa, share_bc, share_vec[:, None, :])
        norm_shares = shares[:3] + (share_bc[:96], share_vec)
    else:

        def scattered(matrix):
            return lax.psum_scatter(
                matrix.astype(jnp.float32), "dp", scatter_dimension=0, tiled=True
            )

        mix_blocks = jnp.concatenate(
            [
                whole_rows(keep[:, :48], send[:, :48], 1)
                for keep, send in ((keep_a, send_a), (keep_b, send_b), (keep_c, send_c))
            ]
        )
        bias_mixed = jnp.concatenate([sums_a[:1], sums_b[:1], sums_c[:1]]).reshape(HG, 3, QCOLS)
        grad_vec = jnp.concatenate(
            [
                bias_mixed[:, 0].reshape(1, D),
                bias_mixed[:, 2].reshape(1, D),
                sums_one[4:7],
                sums_one[0:4],
                sums_two[0:3],
            ],
            axis=0,
        )
        shares = (
            scattered(from_heads(mix_blocks)),
            scattered(whole_rows(keep_out, send_out, 1)[0]),
            scattered(from_columns(whole_rows(keep_up, send_up, 4))),
            scattered(whole_rows(keep_down, send_down, 1)[0]),
            lax.psum_scatter(grad_vec, "dp", scatter_dimension=1, tiled=True),
        )
        norm_shares = shares

    local_square = sum(jnp.sum(s * s) for s in norm_shares)
    firsts = (first_mix[0], first_out[0], first_up[0], first_down[0], first_vectors[0])
    seconds = (second_mix[0], second_out[0], second_up[0], second_down[0], second_vectors[0])
    if fast:
        norm = jnp.broadcast_to(local_square, (8, 128))
        norm = (norm + across(norm, 0, 8)) + (across(norm, 1, 0) + across(norm, 1, 8))
        norm = (norm + across(norm, 0, 4)) + (across(norm, 0, 2) + across(norm, 0, 6))
        norm = norm + across(norm, 0, 1)
        grad_square = norm[0, 0]
        arrays = [
            pltpu.with_memory_space_constraint(a, pltpu.HBM)
            for group in (masters, firsts, seconds)
            for a in group[:4] + (group[4][:, None, :],)
        ]
        updated = adam_all(norm, shares, arrays)
        updated = tuple(
            jnp.swapaxes(u, 0, 1) if i % 5 == 4 else u[None] for i, u in enumerate(updated)
        )
    else:
        grad_square = lax.psum(local_square, ("tower", "dp"))
        factor = jnp.minimum(1.0, clip_norm / (jnp.sqrt(grad_square) + 1e-06))
        rates = (matrix_rate, matrix_rate, matrix_rate, matrix_rate, vector_rate)
        results = [
            adam_update(masters[i], shares[i], firsts[i], seconds[i], rates[i], factor)
            for i in range(5)
        ]
        updated = tuple(r[i] for i in range(3) for r in results)
    return (
        output.reshape(1, MB, 1, L, D),
        input_grad.reshape(1, MB, 1, L, D),
        *updated,
        grad_square,
    )


def solution(mesh):
    rows = P("tower", None, "dp", None, None)
    shards = (P("tower", "dp", None),) * 4 + (P("tower", None, "dp"),)
    in_specs = (rows, P("tower", None, "dp", None), P(None, "dp"), rows) + shards * 3
    out_specs = (rows, rows) + shards * 3 + (P(),)
    return jax.shard_map(body, mesh=mesh, in_specs=in_specs, out_specs=out_specs, check_vma=False)
```

```python
from functools import partial

import jax
import jax.numpy as jnp
from jax import lax
from jax.experimental import pallas as pl
from jax.experimental.pallas import tpu as pltpu
from jax.sharding import PartitionSpec as P

D = 768
FF = 3072
H = 12
HD = 64
L = 512
SEGS = 8
MB = 2
STEP = 5
HG = 3
PIECES = 16
PIECE_ROWS = D // PIECES

norm_eps = 1e-05
attention_scale = 0.125
score_scale = 0.0625
contrast_weight = 16.0
clip_norm = 1.0
beta_first = 0.9
beta_second = 0.999
adam_eps = 1e-08
weight_decay = 0.01
matrix_rate = 0.05
vector_rate = 0.5
masked_score = -1e30

low_type = jnp.bfloat16
highest = lax.Precision.HIGHEST


def swapped(value, mask):
    pairs = [(i, i ^ mask) for i in range(lax.axis_size("dp"))]
    return lax.ppermute(value, "dp", pairs)


def tower_swapped(value):
    return lax.ppermute(value, "tower", [(0, 1), (1, 0)])


def relative_of(place):
    return ((place & 1) << 3) | ((place & 2) << 1) | ((place & 4) >> 1) | (place >> 3)


def relative_y_first(place):
    return ((place & 1) << 1) | ((place & 2) << 2) | (place & 4) | (place >> 3)


def gather_pieces(own):
    pieces = own[None]
    for mask in (8, 4, 2, 1):
        pieces = jnp.concatenate([pieces, swapped(pieces, mask)])
    return pieces


def added(first, second):
    return first.astype(jnp.float32) + second.astype(jnp.float32)


def rows_dot(first_op, second_op):
    return jnp.dot(first_op, second_op, preferred_element_type=jnp.float32)


def contract_rows(first_op, second_op):
    return lax.dot_general(
        first_op, second_op, (((0,), (0,)), ((), ())), preferred_element_type=jnp.float32
    )


def contract_cols(first_op, second_op):
    return lax.dot_general(
        first_op, second_op, (((1,), (1,)), ((), ())), preferred_element_type=jnp.float32
    )


def layer_stats(values):
    centred = values - jnp.mean(values, axis=-1, keepdims=True)
    inverse = lax.rsqrt(jnp.mean(centred * centred, axis=-1, keepdims=True) + norm_eps)
    return (centred * inverse, inverse)


def norm_back(upstream, normed, inverse, gain_row):
    gained = upstream * gain_row
    return inverse * (
        gained
        - jnp.mean(gained, axis=-1, keepdims=True)
        - normed * jnp.mean(gained * normed, axis=-1, keepdims=True)
    )


def column_sum(values):
    return jnp.sum(values.astype(jnp.float32), axis=0, keepdims=True)


def gelu_parts(pre):
    below = 1.0 + (0.3275911 * 0.7071067811865476) * jnp.abs(pre)
    inner = pl.reciprocal(below, approx=True)
    inner = inner * (2.0 - below * inner)
    series = (0.5 * 1.061405429) * inner - (0.5 * 1.453152027)
    series = series * inner + (0.5 * 1.421413741)
    series = series * inner - (0.5 * 0.284496736)
    series = (series * inner + (0.5 * 0.254829592)) * inner
    bell = jnp.exp2(pre * pre * (-0.5 * log2e))
    half_tail = series * bell
    cumulative = jnp.where(pre >= 0.0, 1.0 - half_tail, half_tail)
    return (pre * cumulative, cumulative + pre * (bell * 0.3989422804014327))


log2e = 1.4426950408889634
ROWS = MB * L
QCOLS = D // HG
HEADS = H // HG
any_space = pl.BlockSpec(memory_space=pltpu.HBM)
scalar_space = pl.BlockSpec(memory_space=pltpu.SMEM)
vmem_space = pl.BlockSpec(memory_space=pltpu.VMEM)


def kept_in_hbm(array):
    return pltpu.with_memory_space_constraint(array, pltpu.HBM)


def params(megabytes):
    return pltpu.CompilerParams(vmem_limit_bytes=megabytes * 1024 * 1024)


def cost(flops, moved, exps=0):
    return pl.CostEstimate(flops=int(flops), bytes_accessed=int(moved), transcendentals=int(exps))


def start_pieces(me, quads, target, sem, order=relative_of, at=0):
    count = quads[0].shape[1]
    for place in range(PIECES):
        pltpu.make_async_copy(
            quads[place // 4].at[place % 4],
            target.at[me ^ order(place), pl.ds(at, count), :],
            sem,
        ).start()


def start_up(me, quads, quads_last, target, sem):
    start_pieces(me, quads, target, sem)
    start_pieces(me, quads_last, target, sem, relative_y_first, 4 * PIECE_ROWS)


def up_block_of(pieces, step):
    return block_of(pieces, step + step // 3)


def start_owners(me, source, keep, send, sem):
    for place in range(PIECES):
        held = keep if place < 8 else send
        pltpu.make_async_copy(
            source.at[me ^ relative_of(place)], held.at[place % 8], sem
        ).start()


def block_of(pieces, index):
    at = pl.multiple_of(index * PIECE_ROWS, 16)
    return pieces[:, pl.ds(at, PIECE_ROWS), :].reshape(D, D)


def segment_mask(seg_row):
    numbers = seg_row[...].reshape(1, L)
    columns = jnp.transpose(jnp.broadcast_to(numbers, (8, L)))[:, :1]
    return jnp.where(columns == numbers, 0.0, masked_score)


def wait_bytes(whole, sem):
    pltpu.make_async_copy(whole, whole, sem).wait()


def attention_kernel(
    me_ref, *refs
):
    quads = refs[:4]
    x_ref, seg_row, mixed_ref, ctx_ref, lse_ref, vec_ref, w, mask, bias, sems = refs[4:]
    hg, mb = pl.program_id(0), pl.program_id(1)
    me = me_ref[0]

    @pl.when((hg == 0) & (mb == 0))
    def _():
        start_pieces(me, quads, w, sems.at[0])

    @pl.when(hg == 0)
    def _():
        mask[mb] = segment_mask(seg_row)

    @pl.when((hg == 0) & (mb == 0))
    def _():
        wait_bytes(w, sems.at[0])
        vec = w[0, HG * PIECE_ROWS :, :].astype(jnp.float32)
        for place in range(1, PIECES):
            vec = vec + w[place, HG * PIECE_ROWS :, :].astype(jnp.float32)
        vec_ref[...] = vec
        for group in range(HG):
            columns = slice(group * QCOLS, (group + 1) * QCOLS)
            none = jnp.zeros((1, QCOLS), jnp.float32)
            bias[group] = jnp.concatenate([vec[0:1, columns], none, vec[1:2, columns]], axis=1)

    mixed = (rows_dot(x_ref[...], block_of(w, hg)) + bias[hg]).astype(low_type)
    mixed_ref[...] = mixed.reshape(mixed_ref.shape)
    v_t = jnp.transpose(mixed[:, 2 * QCOLS :])
    outs, totals = [], []

    def scores_of(head):
        here = slice(head * HD, (head + 1) * HD)
        q, k = mixed[:, here], mixed[:, QCOLS + head * HD : QCOLS + (head + 1) * HD]
        return contract_cols(k, q)

    ahead = scores_of(0)
    for head in range(HEADS):
        here = slice(head * HD, (head + 1) * HD)
        scores = ahead * (attention_scale * log2e) + mask[mb]
        if head + 1 < HEADS:
            ahead = scores_of(head + 1)
        largest = jnp.max(scores, axis=0, keepdims=True)
        expo = jnp.exp2(scores - largest)
        summed = jnp.sum(expo, axis=0, keepdims=True)
        probs = expo.astype(low_type)
        outs.append((rows_dot(v_t[here], probs) * (1.0 / summed)).astype(low_type))
        totals.append(largest + jnp.log(summed) * log2e)
    ctx_ref[...] = jnp.transpose(jnp.concatenate(outs, axis=0))
    lse_ref[...] = jnp.concatenate(totals, axis=0).reshape(lse_ref.shape)


def attention_forward(me, quads, x_low, seg_row):
    return pl.pallas_call(
        attention_kernel,
        grid=(HG, MB),
        in_specs=[
            scalar_space,
            *[any_space] * 4,
            pl.BlockSpec((L, D), lambda g, m: (m, 0)),
            pl.BlockSpec((1, 1, L), lambda g, m: (m, 0, 0)),
        ],
        out_specs=[
            pl.BlockSpec((1, L, D), lambda g, m: (g, m, 0)),
            pl.BlockSpec((L, QCOLS), lambda g, m: (m, g)),
            pl.BlockSpec((1, HEADS, L), lambda g, m: (g * MB + m, 0, 0)),
            pl.BlockSpec((16, D), lambda g, m: (0, 0)),
        ],
        out_shape=[
            pltpu.HBM((HG, ROWS, D), low_type),
            pltpu.HBM((ROWS, D), low_type),
            jax.ShapeDtypeStruct((HG * MB, HEADS, L), jnp.float32),
            jax.ShapeDtypeStruct((16, D), jnp.float32),
        ],
        scratch_shapes=[
            pltpu.VMEM((PIECES, HG * PIECE_ROWS + 16, D), low_type),
            pltpu.VMEM((MB, L, L), jnp.float32),
            pltpu.VMEM((HG, 1, D), jnp.float32),
            pltpu.SemaphoreType.DMA((1,)),
        ],
        compiler_params=params(40),
        cost_estimate=cost(2 * ROWS * D * 3 * D + 8 * MB * H * L * L * HD, 12e6, MB * H * L * L),
        name="mixed_attention",
    )(me, *quads, x_low, seg_row)


def up_kernel(
    me_ref,
    quad_0,
    quad_1,
    quad_2,
    quad_3,
    last_0,
    last_1,
    last_2,
    last_3,
    ctx_hbm,
    x_hbm,
    vec,
    normed_hbm,
    inverse_ref,
    hidden_hbm,
    active_ref,
    slope_ref,
    w,
    ctx,
    x,
    normed,
    hidden,
    sems,
):
    step = pl.program_id(0)
    me = me_ref[0]
    quads, quads_last = (quad_0, quad_1, quad_2, quad_3), (last_0, last_1, last_2, last_3)
    ctx_in = pltpu.make_async_copy(ctx_hbm, ctx, sems.at[1])
    x_in = pltpu.make_async_copy(x_hbm, x, sems.at[2])
    normed_out = pltpu.make_async_copy(normed, normed_hbm, sems.at[3])
    hidden_out = pltpu.make_async_copy(hidden, hidden_hbm, sems.at[4])

    @pl.when(step == 0)
    def _():
        start_up(me, quads, quads_last, w, sems.at[0])
        ctx_in.start()
        x_in.start()
        wait_bytes(w, sems.at[0])
        ctx_in.wait()
        x_in.wait()
        for first in range(0, ROWS, 256):
            part = slice(first, first + 256)
            branch = rows_dot(ctx[part, :], block_of(w, 3)) + vec[2:3, :]
            n, inv = layer_stats(x[part, :].astype(jnp.float32) + branch)
            normed[part, :] = n
            inverse_ref[part, :] = inv
            hidden[part, :] = (n * vec[3:4, :] + vec[4:5, :]).astype(low_type)
        normed_out.start()
        hidden_out.start()

    bias = vec[pl.ds(5 + step, 1), :]
    for first in range(0, ROWS, 128):
        part = slice(first, first + 128)
        pre = rows_dot(hidden[part, :], up_block_of(w, step)) + bias
        active, slope = gelu_parts(pre)
        active_ref[part, :] = active.astype(low_type)
        slope_ref[part, :] = slope.astype(low_type)

    @pl.when(step == 3)
    def _():
        normed_out.wait()
        hidden_out.wait()


def up_forward(me, quads, quads_last, context, x_low, vec):
    return pl.pallas_call(
        up_kernel,
        grid=(4,),
        in_specs=[scalar_space, *[any_space] * 10, vmem_space],
        out_specs=[
            any_space,
            pl.BlockSpec((ROWS, 1), lambda s: (0, 0)),
            any_space,
            pl.BlockSpec((ROWS, D), lambda s: (0, s)),
            pl.BlockSpec((ROWS, D), lambda s: (0, s)),
        ],
        out_shape=[
            pltpu.HBM((ROWS, D), jnp.float32),
            jax.ShapeDtypeStruct((ROWS, 1), jnp.float32),
            pltpu.HBM((ROWS, D), low_type),
            pltpu.HBM((ROWS, FF), low_type),
            pltpu.HBM((ROWS, FF), low_type),
        ],
        scratch_shapes=[
            pltpu.VMEM((PIECES, 5 * PIECE_ROWS, D), low_type),
            pltpu.VMEM((ROWS, D), low_type),
            pltpu.VMEM((ROWS, D), low_type),
            pltpu.VMEM((ROWS, D), jnp.float32),
            pltpu.VMEM((ROWS, D), low_type),
            pltpu.SemaphoreType.DMA((5,)),
        ],
        compiler_params=params(44),
        cost_estimate=cost(2 * ROWS * D * (FF + D), 24e6, 2 * ROWS * FF),
        name="out_up",
    )(me, *quads, *quads_last, context, x_low, vec)


def down_kernel(
    me_ref,
    quad_0,
    quad_1,
    quad_2,
    quad_3,
    active_hbm,
    normed_one_hbm,
    vec,
    table_ref,
    normed_hbm,
    inverse_ref,
    output_hbm,
    cls_ref,
    w,
    active,
    normed_one,
    normed,
    output,
    sems,
):
    me = me_ref[0]
    start_pieces(me, (quad_0, quad_1, quad_2, quad_3), w, sems.at[0])
    arrivals, departures = [], []
    for index in range(4):
        part = pl.ds(index * 256, 256)
        arrivals.append(
            (
                pltpu.make_async_copy(
                    active_hbm.at[part, :], active.at[part, :], sems.at[1 + index]
                ),
                pltpu.make_async_copy(
                    normed_one_hbm.at[part, :], normed_one.at[part, :], sems.at[5 + index]
                ),
            )
        )
        departures.append(
            (
                pltpu.make_async_copy(
                    normed.at[part, :], normed_hbm.at[part, :], sems.at[9 + index]
                ),
                pltpu.make_async_copy(
                    output.at[part, :], output_hbm.at[part, :], sems.at[13 + index]
                ),
            )
        )
        for arrival in arrivals[index]:
            arrival.start()
    wait_bytes(w, sems.at[0])
    for index in range(4):
        for arrival in arrivals[index]:
            arrival.wait()
        part = slice(index * 256, (index + 1) * 256)
        ffn = rows_dot(active[part, :], w[...].reshape(FF, D)) + vec[9:10, :]
        residual = normed_one[part, :] * vec[3:4, :] + vec[4:5, :]
        n, inv = layer_stats(residual + ffn)
        normed[part, :] = n
        inverse_ref[part, :] = inv
        output[part, :] = (n * vec[10:11, :] + vec[11:12, :]).astype(low_type)
        for departure in departures[index]:
            departure.start()
    cls_ref[...] = rows_dot(table_ref[...], output[...]).astype(low_type)
    for pair in departures:
        for departure in pair:
            departure.wait()


def down_forward(me, quads, active, normed_one, vec, table):
    return pl.pallas_call(
        down_kernel,
        in_specs=[scalar_space, *[any_space] * 6, vmem_space, vmem_space],
        out_specs=[any_space, vmem_space, any_space, vmem_space],
        out_shape=[
            pltpu.HBM((ROWS, D), jnp.float32),
            jax.ShapeDtypeStruct((ROWS, 1), jnp.float32),
            pltpu.HBM((ROWS, D), low_type),
            jax.ShapeDtypeStruct((MB * SEGS, D), low_type),
        ],
        scratch_shapes=[
            pltpu.VMEM((PIECES, 4 * PIECE_ROWS, D), low_type),
            pltpu.VMEM((ROWS, FF), low_type),
            pltpu.VMEM((ROWS, D), jnp.float32),
            pltpu.VMEM((ROWS, D), jnp.float32),
            pltpu.VMEM((ROWS, D), low_type),
            pltpu.SemaphoreType.DMA((17,)),
        ],
        compiler_params=params(40),
        cost_estimate=cost(2 * ROWS * D * FF, 19e6),
        name="down",
    )(me, *quads, kept_in_hbm(active), kept_in_hbm(normed_one), vec, table)


def contrast_kernel(flag_ref, all_ref, positive_ref, ids_ref, grad_ref):
    passage_here = flag_ref[0] == 1
    for batch in range(MB):
        mine, theirs = all_ref[0, batch], all_ref[1, batch]
        queries = jnp.where(passage_here, theirs, mine)
        passages = jnp.where(passage_here, mine, theirs)
        contrast = contract_cols(queries, passages) * score_scale
        top = jnp.max(contrast, axis=-1, keepdims=True)
        expo = jnp.exp(contrast - top)
        probs = expo / jnp.sum(expo, axis=-1, keepdims=True)
        chosen = (positive_ref[batch] == ids_ref[...]).astype(jnp.float32)
        grad = (contrast_weight * (probs - chosen)).astype(low_type)
        for_query = rows_dot(grad[:16], passages) * score_scale
        for_query = for_query.astype(low_type).astype(jnp.float32)
        for_passage = contract_rows(grad, queries)[:16] * score_scale
        taken = jnp.where(passage_here, for_passage, for_query)
        grad_ref[batch * SEGS : (batch + 1) * SEGS, :] = taken[:SEGS]


def contrast_back(flag, everyone, cls_positives, cls_ids):
    return pl.pallas_call(
        contrast_kernel,
        in_specs=[scalar_space, vmem_space, vmem_space, vmem_space],
        out_specs=vmem_space,
        out_shape=jax.ShapeDtypeStruct((MB * SEGS, D), jnp.float32),
        compiler_params=params(48),
        name="contrast",
    )(flag, everyone, cls_positives, cls_ids)


def down_back_kernel(
    me_ref,
    token_grad_hbm,
    grad_cls,
    table3_ref,
    normed_hbm,
    inverse_ref,
    vec,
    active_ref,
    residual_hbm,
    low_ref,
    sums_ref,
    keep,
    send,
    low,
    token_grad,
    normed,
    residual,
    staged,
    sems,
):
    step = pl.program_id(0)
    me = me_ref[0]
    residual_out = pltpu.make_async_copy(residual, residual_hbm, sems.at[8])

    @pl.when(step == 0)
    def _():
        arrivals = []
        for index in range(4):
            part = pl.ds(index * 256, 256)
            arrivals.append(
                (
                    pltpu.make_async_copy(
                        token_grad_hbm.at[part, :], token_grad.at[part, :], sems.at[index]
                    ),
                    pltpu.make_async_copy(
                        normed_hbm.at[part, :], normed.at[part, :], sems.at[4 + index]
                    ),
                )
            )
            for arrival in arrivals[index]:
                arrival.start()
        grads = grad_cls[...]
        upper = grads.astype(low_type)
        rest = grads - upper.astype(jnp.float32)
        middle = rest.astype(low_type)
        lower = (rest - middle.astype(jnp.float32)).astype(low_type)
        stacked = jnp.concatenate([upper, middle, lower], axis=0)
        gains = jnp.zeros((1, D), jnp.float32)
        shifts = jnp.zeros((1, D), jnp.float32)
        biases = jnp.zeros((1, D), jnp.float32)
        for index in range(4):
            part = slice(index * 256, (index + 1) * 256)
            for arrival in arrivals[index]:
                arrival.wait()
            upstream = token_grad[part, :] + contract_rows(table3_ref[:, part], stacked)
            n = normed[part, :]
            gains = gains + column_sum(upstream * n)
            shifts = shifts + column_sum(upstream)
            grad = norm_back(upstream, n, inverse_ref[part, :], vec[10:11, :])
            residual[part, :] = grad
            rounded = grad.astype(low_type)
            biases = biases + column_sum(rounded)
            low[part, :] = rounded
        residual_out.start()
        low_ref[...] = low[...]
        sums_ref[...] = jnp.concatenate([biases, gains, shifts, jnp.zeros((5, D), jnp.float32)])

    for first in range(4):
        at = first * 4 * PIECE_ROWS
        staged[4 * step + first] = contract_rows(
            active_ref[:, at : at + 4 * PIECE_ROWS], low[...]
        ).astype(low_type)

    @pl.when(step == 3)
    def _():
        start_owners(me, staged, keep, send, sems.at[9])
        residual_out.wait()
        wait_bytes(staged, sems.at[9])


def down_back(me, token_grad, grad_cls, table3, normed, inverse, vec, active):
    half = jax.ShapeDtypeStruct((8, 4 * PIECE_ROWS, D), low_type)
    return pl.pallas_call(
        down_back_kernel,
        grid=(4,),
        in_specs=[
            scalar_space,
            any_space,
            vmem_space,
            vmem_space,
            any_space,
            vmem_space,
            vmem_space,
            pl.BlockSpec((ROWS, D), lambda s: (0, s)),
        ],
        out_specs=[any_space] + [vmem_space] * 2 + [any_space] * 2,
        out_shape=[
            pltpu.HBM((ROWS, D), jnp.float32),
            jax.ShapeDtypeStruct((ROWS, D), low_type),
            jax.ShapeDtypeStruct((8, D), jnp.float32),
            half,
            half,
        ],
        scratch_shapes=[
            pltpu.VMEM((ROWS, D), low_type),
            pltpu.VMEM((ROWS, D), jnp.float32),
            pltpu.VMEM((ROWS, D), jnp.float32),
            pltpu.VMEM((ROWS, D), jnp.float32),
            pltpu.VMEM((PIECES, 4 * PIECE_ROWS, D), low_type),
            pltpu.SemaphoreType.DMA((10,)),
        ],
        compiler_params=params(44),
        cost_estimate=cost(2 * ROWS * D * FF, 25e6),
        name="down_back",
    )(
        me,
        kept_in_hbm(token_grad),
        grad_cls,
        table3,
        kept_in_hbm(normed),
        inverse,
        vec,
        kept_in_hbm(active),
    )


def up_back_kernel(
    me_ref,
    up_0,
    up_1,
    up_2,
    up_3,
    last_0,
    last_1,
    last_2,
    last_3,
    down_0,
    down_1,
    down_2,
    down_3,
    low_ref,
    slope_ref,
    hidden_ref,
    residual_hbm,
    normed_hbm,
    inverse_ref,
    ctx_hbm,
    vec,
    grad_one_hbm,
    grad_ctx_ref,
    sums_ref,
    keep,
    send,
    keep_out,
    send_out,
    up_w,
    down_w,
    normed,
    ctx,
    total,
    staged,
    staged_out,
    bias_sums,
    sems,
):
    step = pl.program_id(0)
    me = me_ref[0]
    residual_in = pltpu.make_async_copy(residual_hbm, total, sems.at[2])
    normed_in = pltpu.make_async_copy(normed_hbm, normed, sems.at[3])
    ctx_in = pltpu.make_async_copy(ctx_hbm, ctx, sems.at[4])

    @pl.when(step == 0)
    def _():
        start_pieces(me, (down_0, down_1, down_2, down_3), down_w, sems.at[0])
        last = (last_0, last_1, last_2, last_3)
        start_up(me, (up_0, up_1, up_2, up_3), last, up_w, sems.at[1])
        residual_in.start()
        normed_in.start()
        ctx_in.start()
        wait_bytes(down_w, sems.at[0])

    down_block = down_w[pl.ds(4 * step, 4)].reshape(D, D)
    biases = jnp.zeros((1, D), jnp.float32)
    grads = []
    for first in range(0, ROWS, 512):
        part = slice(first, first + 512)
        active_grad = contract_cols(low_ref[part, :], down_block)
        grad = (active_grad * slope_ref[part, :].astype(jnp.float32)).astype(low_type)
        biases = biases + column_sum(grad)
        grads.append(grad)
    grad = jnp.concatenate(grads, axis=0)

    @pl.when(step == 0)
    def _():
        wait_bytes(up_w, sems.at[1])
        residual_in.wait()

    total[...] += contract_cols(grad, up_block_of(up_w, step))
    at = pl.multiple_of(step * PIECE_ROWS, 16)
    for first in range(0, PIECES, 4):
        columns = slice(first * PIECE_ROWS, (first + 4) * PIECE_ROWS)
        terms = contract_rows(hidden_ref[:, columns], grad).astype(low_type)
        staged[first : first + 4, pl.ds(at, PIECE_ROWS), :] = terms.reshape(4, PIECE_ROWS, D)
    bias_sums[step] = biases

    @pl.when(step == 3)
    def _():
        start_owners(me, staged, keep, send, sems.at[5])
        normed_in.wait()
        ctx_in.wait()
        gains = jnp.zeros((1, D), jnp.float32)
        shifts = jnp.zeros((1, D), jnp.float32)
        out_biases = jnp.zeros((1, D), jnp.float32)
        lows, departures = [], []
        for first in range(0, ROWS, 256):
            part = slice(first, first + 256)
            upstream = total[part, :]
            n = normed[part, :]
            gains = gains + column_sum(upstream * n)
            shifts = shifts + column_sum(upstream)
            grad_one = norm_back(upstream, n, inverse_ref[part, :], vec[3:4, :])
            total[part, :] = grad_one
            departures.append(
                pltpu.make_async_copy(
                    total.at[part, :], grad_one_hbm.at[part, :], sems.at[7 + first // 256]
                )
            )
            departures[-1].start()
            rounded = grad_one.astype(low_type)
            out_biases = out_biases + column_sum(rounded)
            grad_ctx_ref[part, :] = contract_cols(rounded, block_of(up_w, 3)).astype(low_type)
            lows.append(rounded)
        sums_ref[...] = jnp.concatenate(
            [bias_sums[block] for block in range(4)]
            + [out_biases, gains, shifts, jnp.zeros((1, D), jnp.float32)]
        )
        rounded = jnp.concatenate(lows, axis=0)
        for first in range(0, PIECES, 4):
            columns = slice(first * PIECE_ROWS, (first + 4) * PIECE_ROWS)
            terms = contract_rows(ctx[:, columns], rounded).astype(low_type)
            staged_out[first : first + 4] = terms.reshape(4, PIECE_ROWS, D)
        start_owners(me, staged_out, keep_out, send_out, sems.at[6])
        wait_bytes(staged, sems.at[5])
        wait_bytes(staged_out, sems.at[6])
        for departure in departures:
            departure.wait()


def up_back(
    me, up_quads, up_last, down_quads, low, slope, hidden, residual, normed, inverse, ctx, vec
):
    half = jax.ShapeDtypeStruct((8, 4 * PIECE_ROWS, D), low_type)
    half_out = jax.ShapeDtypeStruct((8, PIECE_ROWS, D), low_type)
    return pl.pallas_call(
        up_back_kernel,
        grid=(4,),
        in_specs=[scalar_space]
        + [any_space] * 12
        + [
            vmem_space,
            pl.BlockSpec((ROWS, D), lambda s: (0, s)),
            vmem_space,
            any_space,
            any_space,
            vmem_space,
            any_space,
            vmem_space,
        ],
        out_specs=[any_space] + [vmem_space] * 2 + [any_space] * 4,
        out_shape=[
            pltpu.HBM((ROWS, D), jnp.float32),
            jax.ShapeDtypeStruct((ROWS, D), low_type),
            jax.ShapeDtypeStruct((8, D), jnp.float32),
            half,
            half,
            half_out,
            half_out,
        ],
        scratch_shapes=[
            pltpu.VMEM((PIECES, 5 * PIECE_ROWS, D), low_type),
            pltpu.VMEM((PIECES, 4 * PIECE_ROWS, D), low_type),
            pltpu.VMEM((ROWS, D), jnp.float32),
            pltpu.VMEM((ROWS, D), low_type),
            pltpu.VMEM((ROWS, D), jnp.float32),
            pltpu.VMEM((PIECES, 4 * PIECE_ROWS, D), low_type),
            pltpu.VMEM((PIECES, PIECE_ROWS, D), low_type),
            pltpu.VMEM((4, 1, D), jnp.float32),
            pltpu.SemaphoreType.DMA((11,)),
        ],
        compiler_params=params(56),
        cost_estimate=cost(2 * ROWS * D * (3 * FF + 2 * D), 40e6),
        name="up_back",
    )(
        me,
        *up_quads,
        *up_last,
        *down_quads,
        low,
        slope,
        hidden,
        residual,
        normed,
        inverse,
        ctx,
        vec,
    )


def attention_back_kernel(
    me_ref,
    x_ref,
    seg_row,
    mixed_ref,
    lse_ref,
    grad_ctx_ref,
    *refs,
):
    others, (grad_mixed_ref, sums_ref, keep, send, weight_grad, staged, sem) = refs[:-7], refs[-7:]
    mb = pl.program_id(0)
    me = me_ref[0]
    mask = segment_mask(seg_row)
    mixed = mixed_ref[...].reshape(L, D)
    lse = lse_ref[...].reshape(HEADS, L)
    k_t = jnp.transpose(mixed[:, QCOLS : 2 * QCOLS])
    grad_q, grad_k, grad_v = [], [], []

    def products_of(head):
        here = slice(head * HD, (head + 1) * HD)
        q, k = mixed[:, here], mixed[:, QCOLS + head * HD : QCOLS + (head + 1) * HD]
        v = mixed[:, 2 * QCOLS + head * HD : 2 * QCOLS + (head + 1) * HD]
        return (contract_cols(k, q), contract_cols(v, grad_ctx_ref[:, here]))

    ahead = products_of(0)
    for head in range(HEADS):
        here = slice(head * HD, (head + 1) * HD)
        scores, grad_probs = ahead
        if head + 1 < HEADS:
            ahead = products_of(head + 1)
        scores = scores * (attention_scale * log2e) + mask
        probs = jnp.exp2(scores - lse[head : head + 1])
        inner = jnp.sum(probs * grad_probs, axis=0, keepdims=True)
        grad_scores = (probs * (grad_probs - inner)).astype(low_type)
        grad_v.append(rows_dot(probs.astype(low_type), grad_ctx_ref[:, here]).astype(low_type))
        grad_q.append((rows_dot(k_t[here], grad_scores) * attention_scale).astype(low_type))
        grad_k.append((rows_dot(grad_scores, mixed[:, here]) * attention_scale).astype(low_type))
    grad_mixed = jnp.concatenate(
        [jnp.transpose(jnp.concatenate(grad_q, axis=0))] + grad_k + grad_v, axis=1
    )

    grad_mixed_ref[...] = grad_mixed
    bias = column_sum(grad_mixed)
    terms = contract_rows(x_ref[...], grad_mixed)

    @pl.when(mb == 0)
    def _():
        weight_grad[...] = terms
        sums_ref[0:1, :] = bias

    @pl.when(mb == 1)
    def _():
        sums_ref[0:1, :] += bias
        grads = (weight_grad[...] + terms).astype(low_type)
        staged[:, :PIECE_ROWS, :] = grads.reshape(PIECES, PIECE_ROWS, D)
        if others:
            mixed_a, mixed_b, up, down = (other[...] for other in others)
            mixed_sums = (mixed_a[0:1], mixed_b[0:1], sums_ref[0:1, :])
            vectors = jnp.concatenate(
                [
                    jnp.concatenate([s[:, :QCOLS] for s in mixed_sums], axis=1),
                    jnp.concatenate([s[:, 2 * QCOLS :] for s in mixed_sums], axis=1),
                    up[4:7],
                    up[0:4],
                    down[0:3],
                    jnp.zeros((4, D), jnp.float32),
                ],
                axis=0,
            )
            for place in range(PIECES):
                staged[place, PIECE_ROWS:, :] = vectors.astype(low_type)
        start_owners(me, staged, keep, send, sem)
        wait_bytes(staged, sem)


def attention_back(me, x_low, seg_row, mixed, lse, grad_ctx, group, *others):
    rows = PIECE_ROWS + (16 if others else 0)
    half = jax.ShapeDtypeStruct((8, rows, D), low_type)
    return pl.pallas_call(
        attention_back_kernel,
        grid=(MB,),
        in_specs=[
            scalar_space,
            pl.BlockSpec((L, D), lambda m: (m, 0)),
            pl.BlockSpec((1, 1, L), lambda m: (m, 0, 0)),
            pl.BlockSpec((1, L, D), lambda m: (group, m, 0)),
            pl.BlockSpec((1, HEADS, L), lambda m: (group * MB + m, 0, 0)),
            pl.BlockSpec((L, QCOLS), lambda m: (m, group)),
            *[vmem_space] * len(others),
        ],
        out_specs=[pl.BlockSpec((L, D), lambda m: (m, 0)), vmem_space, any_space, any_space],
        out_shape=[
            jax.ShapeDtypeStruct((ROWS, D), low_type),
            jax.ShapeDtypeStruct((8, D), jnp.float32),
            half,
            half,
        ],
        scratch_shapes=[
            pltpu.VMEM((D, D), jnp.float32),
            pltpu.VMEM((PIECES, rows, D), low_type),
            pltpu.SemaphoreType.DMA,
        ],
        compiler_params=params(40),
        cost_estimate=cost(
            2 * ROWS * D * D + 20 * MB * HEADS * L * L * HD, 12e6, MB * HEADS * L * L
        ),
        name=f"attention_back_{group}",
    )(me, x_low, seg_row, kept_in_hbm(mixed), lse, grad_ctx, *others)


def input_back_kernel(
    me_ref, quad_0, quad_1, quad_2, quad_3, one_ref, grad_0, grad_1, grad_2, input_ref, w, sem
):
    @pl.when(pl.program_id(0) == 0)
    def _():
        start_pieces(me_ref[0], (quad_0, quad_1, quad_2, quad_3), w, sem)
        wait_bytes(w, sem)

    total = one_ref[...]
    for block, grad in enumerate((grad_0, grad_1, grad_2)):
        total = total + contract_cols(grad[...], block_of(w, block))
    input_ref[...] = total


def input_back(me, quads, grad_one, grads):
    rows = pl.BlockSpec((256, D), lambda s: (s, 0))
    return pl.pallas_call(
        input_back_kernel,
        grid=(ROWS // 256,),
        in_specs=[scalar_space] + [any_space] * 4 + [rows] * 4,
        out_specs=rows,
        out_shape=jax.ShapeDtypeStruct((ROWS, D), jnp.float32),
        scratch_shapes=[
            pltpu.VMEM((PIECES, HG * PIECE_ROWS + 16, D), low_type),
            pltpu.SemaphoreType.DMA,
        ],
        compiler_params=params(24),
        cost_estimate=cost(6 * ROWS * D * D, 14e6),
        name="input_back",
    )(me, *quads, grad_one, *grads)


def adam_kernel(norm_ref, down_ref, up_ref, out_mix, mix_bc, vec_ref, *refs):
    ins, outs, held, sems = refs[:15], refs[15:30], refs[30:45], refs[45]
    arrivals = [
        pltpu.make_async_copy(ins[i], held[i], sems.at[i]) for i in range(15)
    ]
    departures = [
        pltpu.make_async_copy(held[i], outs[i], sems.at[i]) for i in range(15)
    ]
    order = (3, 2, 0, 1, 4)
    for index in order:
        for i in (index, 5 + index, 10 + index):
            arrivals[i].start()
    factor = jnp.minimum(1.0, clip_norm / (jnp.sqrt(norm_ref[0:1, 0:1]) + 1e-06))[0, 0]

    def update(index, at, grad, rate):
        master, first, second = held[index], held[5 + index], held[10 + index]
        clipped = grad * factor
        first_new = beta_first * first[at] + (1.0 - beta_first) * clipped
        second_new = beta_second * second[at] + (1.0 - beta_second) * clipped * clipped
        root = jnp.sqrt(second_new / (1.0 - beta_second**STEP)) + adam_eps
        step = first_new / (1.0 - beta_first**STEP) / root
        old = master[at]
        master[at] = old - rate * (step + weight_decay * old)
        first[at] = first_new
        second[at] = second_new

    for index in order:
        for i in (index, 5 + index, 10 + index):
            arrivals[i].wait()
        if index == 0:
            one, two = PIECE_ROWS, 2 * PIECE_ROWS
            parts = (out_mix[one:two, :], mix_bc[:one, :], mix_bc[one:two, :])
            for group, share in enumerate(parts):
                for third in range(3):
                    column = third * D + group * QCOLS
                    grad = share[:, third * QCOLS : (third + 1) * QCOLS]
                    update(0, (slice(None), slice(column, column + QCOLS)), grad, matrix_rate)
        elif index == 1:
            update(1, (slice(None), slice(0, D)), out_mix[:PIECE_ROWS, :], matrix_rate)
        elif index == 2:
            for block in range(4):
                grad = up_ref[block * PIECE_ROWS : (block + 1) * PIECE_ROWS, :]
                columns = slice(block * D, (block + 1) * D)
                update(2, (slice(None), columns), grad, matrix_rate)
        elif index == 3:
            update(3, (slice(None), slice(0, D)), down_ref[...], matrix_rate)
        else:
            update(4, ..., vec_ref[...], vector_rate)
        for i in (index, 5 + index, 10 + index):
            departures[i].start()
    for departure in departures:
        departure.wait()


def adam_all(norm, shares, arrays):
    return pl.pallas_call(
        adam_kernel,
        in_specs=[vmem_space] * 6 + [any_space] * 15,
        out_specs=[any_space] * 15,
        out_shape=[jax.ShapeDtypeStruct(a.shape, jnp.float32) for a in arrays],
        scratch_shapes=[pltpu.VMEM(a.shape, jnp.float32) for a in arrays]
        + [pltpu.SemaphoreType.DMA((15,))],
        compiler_params=params(40),
        cost_estimate=cost(40e6, 25e6),
        name="adam",
    )(norm, *shares, *arrays)


def by_heads(matrix):
    shaped = matrix.reshape(matrix.shape[0], 3, HG, D // HG)
    return jnp.transpose(shaped, (2, 0, 1, 3)).reshape(HG, matrix.shape[0], D)


def from_heads(blocks):
    rows = blocks.shape[1]
    shaped = blocks.reshape(HG, rows, 3, D // HG)
    return jnp.transpose(shaped, (1, 2, 0, 3)).reshape(rows, 3 * D)


def by_columns(matrix):
    return jnp.transpose(matrix.reshape(matrix.shape[0], 4, D), (1, 0, 2))


def from_columns(blocks):
    return jnp.transpose(blocks, (1, 0, 2)).reshape(blocks.shape[1], 4 * D)


def adam_update(master, grad_share, first, second, rate, factor):
    clipped = grad_share * factor
    first_new = beta_first * first + (1.0 - beta_first) * clipped
    second_new = beta_second * second + (1.0 - beta_second) * clipped * clipped
    first_hat = first_new / (1.0 - beta_first**STEP)
    second_hat = second_new / (1.0 - beta_second**STEP)
    master_new = master - rate * (
        first_hat / (jnp.sqrt(second_hat) + adam_eps) + weight_decay * master
    )
    return (master_new[None], first_new[None], second_new[None])


def quads_of(matrix_rows):
    k = matrix_rows.shape[0]
    shaped = matrix_rows.reshape(k, 2, 2, 2, 2, -1, D)
    pieces = jnp.transpose(shaped, (4, 3, 2, 1, 0, 5, 6)).reshape(4, 4, -1, D)
    return tuple(pieces[i] for i in range(4))


def whole_rows(keep, send, k):
    shaped = jnp.concatenate([keep, send]).reshape(2, 2, 2, 2, k, -1, D)
    return jnp.transpose(shaped, (4, 3, 2, 1, 0, 5, 6)).reshape(k, -1, D)


def beside(sends, *work):
    received = [swapped(value, mask) for value, mask in sends]
    done = lax.optimization_barrier((received, work))
    return (done[0], *done[1])


def across(value, tower_mask, dp_mask):
    owners = lax.axis_size("dp")
    flip = tower_mask * owners + dp_mask
    pairs = [(i, i ^ flip) for i in range(2 * owners)]
    return lax.ppermute(value, ("tower", "dp"), pairs)


def joined(pieces, received):
    return jnp.concatenate([pieces, received])


def parted(keep, received):
    half = keep.shape[0] // 2
    return (
        added(keep[:half], received[:half]).astype(low_type),
        added(keep[half:], received[half:]).astype(low_type),
    )


def body(
    tokens,
    segments,
    positives,
    token_grad,
    mix_weight,
    out_weight,
    up_weight,
    down_weight,
    vectors,
    first_mix,
    first_out,
    first_up,
    first_down,
    first_vectors,
    second_mix,
    second_out,
    second_up,
    second_down,
    second_vectors,
):
    owners = lax.axis_size("dp")
    fast = owners == PIECES
    index = lax.axis_index("dp")
    flag = lax.axis_index("tower").astype(jnp.int32).reshape(1)
    masters = (mix_weight[0], out_weight[0], up_weight[0], down_weight[0], vectors[0])
    low_mix, low_out, low_up, low_down, low_vec = (m.astype(low_type) for m in masters)
    share = low_vec.shape[1]
    queries_all = owners * SEGS

    if fast:
        me = index.astype(jnp.int32).reshape(1)
        extra = jnp.zeros((16, D), low_type)
        extra = extra.at[12:14, :SEGS].set(positives.astype(low_type))
        extra = lax.dynamic_update_slice(extra, low_vec, (0, index * share))
        pack_mix = jnp.concatenate([by_heads(low_mix).reshape(-1, D), extra])
        low_blocks = by_columns(low_up)
        pack_up = jnp.concatenate([low_blocks[:3].reshape(-1, D), low_out])
        mix, up, last, down = pack_mix[None], pack_up[None], low_blocks[3:], low_down[None]
        ((got_mix, got_last),) = beside([(mix, 8), (last, 2)])
        mix, last = joined(mix, got_mix), joined(last, got_last)
        ((got_mix, got_up),) = beside([(mix, 4), (up, 8)])
        mix, up = joined(mix, got_mix), joined(up, got_up)
        ((mix_y, mix_core, got_up, got_last, got_down),) = beside(
            [(mix, 2), (mix, 1), (up, 4), (last, 8), (down, 8)]
        )
        up, last, down = joined(up, got_up), joined(last, got_last), joined(down, got_down)
        mix_quads = (mix, mix_y, mix_core, swapped(mix_y, 1))
        extras = jnp.concatenate([quad[:, 156:158, :SEGS] for quad in mix_quads])
        cls_positives = jnp.transpose(extras.astype(jnp.int32), (1, 0, 2))
        cls_positives = cls_positives.reshape(MB, queries_all, 1)
        relative = relative_of(jnp.arange(PIECES, dtype=jnp.int32))
        cls_ids = ((relative ^ index)[:, None] * SEGS + jnp.arange(SEGS)[None, :]).reshape(1, -1)
    else:
        me = jnp.zeros((1,), jnp.int32)
        mix_quads = quads_of(by_heads(lax.all_gather(low_mix, "dp", axis=0, tiled=True)))
        up_blocks = by_columns(lax.all_gather(low_up, "dp", axis=0, tiled=True))
        out_block = lax.all_gather(low_out, "dp", axis=0, tiled=True)[None]
        up_quads = quads_of(jnp.concatenate([up_blocks[:3], out_block]))
        up_last = jnp.concatenate(quads_of(up_blocks[3:]))
        up_last = jnp.stack(
            [up_last[relative_of(relative_y_first(place))] for place in range(PIECES)]
        ).reshape(4, 4, PIECE_ROWS, D)
        up_last = tuple(up_last[i] for i in range(4))
        down_quads = quads_of(lax.all_gather(low_down, "dp", axis=0, tiled=True)[None])
        vec_low = lax.all_gather(low_vec, "dp", axis=1, tiled=True)
        extra = jnp.zeros((PIECES, 16, D), low_type).at[0, :12].set(vec_low)
        mix_quads = tuple(
            jnp.concatenate([quad, extra[4 * i : 4 * i + 4]], axis=1)
            for i, quad in enumerate(mix_quads)
        )
        cls_positives = lax.all_gather(positives, "dp", axis=1, tiled=True)
        cls_positives = jnp.roll(cls_positives, -index * SEGS, axis=1)[:, :, None]
        cls_ids = jnp.roll(jnp.arange(queries_all, dtype=jnp.int32), -index * SEGS)[None]

    x_low = tokens[0].reshape(ROWS, D)
    seg_rows = segments[0].reshape(MB, L)
    seg_row = seg_rows.reshape(MB, 1, L)
    before = jnp.concatenate([jnp.full((MB, 1), -1, jnp.int32), seg_rows[:, :-1]], axis=1)
    numbers = jnp.where(seg_rows != before, seg_rows, -1)
    numbers = jnp.where(numbers >= 0, numbers + SEGS * jnp.arange(MB)[:, None], -1).reshape(1, ROWS)
    table = (jnp.arange(MB * SEGS)[:, None] == numbers).astype(low_type)
    mixed, context, lse, vec_f = attention_forward(me, mix_quads, x_low, seg_row)
    if fast:
        (up_y, up_core, last_z, last_core, got_down), mixed, context, lse, vec_f = beside(
            [(up, 2), (up, 1), (last, 4), (last, 1), (down, 4)], mixed, context, lse, vec_f
        )
        down = joined(down, got_down)
        up_quads = (up, up_y, up_core, swapped(up_y, 1))
        up_last = (last, last_z, last_core, swapped(last_z, 1))
    normed_one, inverse_one, hidden, active, slope = up_forward(
        me, up_quads, up_last, context, x_low, vec_f
    )
    if fast:
        (down_y, down_core), normed_one, hidden, active, slope = beside(
            [(down, 2), (down, 1)], normed_one, hidden, active, slope
        )
        down_quads = (down, down_y, down_core, swapped(down_y, 1))
    normed_two, inverse_two, output, cls_low = down_forward(
        me, down_quads, active, normed_one, vec_f, table
    )

    if fast:
        first = [cls_low] + [across(cls_low, t, m) for t, m in ((0, 8), (1, 0), (1, 8))]
        four = jnp.stack(first).reshape(2, 2, MB, SEGS, D)
        second = [four] + [across(four, 0, m) for m in (4, 2, 6)]
        eight = jnp.stack(second)
        everyone = jnp.stack([eight, across(eight, 0, 1)])
        everyone = jnp.transpose(everyone, (2, 4, 0, 1, 3, 5, 6))
    else:
        both = jnp.concatenate([cls_low, tower_swapped(cls_low)])
        everyone = jnp.roll(lax.all_gather(both, "dp", axis=0, tiled=False), -index, axis=0)
        everyone = jnp.transpose(everyone.reshape(owners, 2, MB, SEGS, D), (1, 2, 0, 3, 4))
    everyone = everyone.reshape(2, MB, queries_all, D)
    grad_cls = contrast_back(flag, everyone, cls_positives, cls_ids)

    residual, grad_ffn, sums_two, keep_down, send_down = down_back(
        me,
        token_grad[0].reshape(ROWS, D),
        grad_cls,
        jnp.concatenate([table] * 3),
        normed_two,
        inverse_two,
        vec_f,
        active,
    )
    if fast:
        (got_down,), residual, grad_ffn = beside([(send_down, 1)], residual, grad_ffn)
        keep_down, send_down = parted(keep_down, got_down)
    grad_one, grad_ctx, sums_one, keep_up, send_up, keep_out, send_out = up_back(
        me,
        up_quads,
        up_last,
        down_quads,
        grad_ffn,
        slope,
        hidden,
        residual,
        normed_one,
        inverse_one,
        context,
        vec_f,
    )
    if fast:
        (got_down,), grad_one, grad_ctx, send_up, send_out = beside(
            [(send_down, 2)], grad_one, grad_ctx, send_up, send_out
        )
        keep_down, send_down = parted(keep_down, got_down)
    back = partial(attention_back, me, x_low, seg_row, mixed, lse)
    grad_a, sums_a, keep_a, send_a = back(grad_ctx, 0)
    if fast:
        (got_down, got_up, got_out), grad_ctx, send_a = beside(
            [(send_down, 4), (send_up, 1), (send_out, 1)], grad_ctx, send_a
        )
        keep_down, send_down = parted(keep_down, got_down)
        keep_up, send_up = parted(keep_up, got_up)
        keep_out, send_out = parted(keep_out, got_out)
    grad_b, sums_b, keep_b, send_b = back(grad_ctx, 1)
    grad_c, sums_c, keep_c, send_c = back(grad_ctx, 2, sums_a, sums_b, sums_one, sums_two)
    if fast:
        (got_down, got_up, got_a), grad_b, grad_c, send_b, send_c = beside(
            [(send_down, 8), (send_up, 2), (send_a, 1)], grad_b, grad_c, send_b, send_c
        )
        share_down = added(keep_down[0], got_down[0])
        keep_up, send_up = parted(keep_up, got_up)
        two_a = parted(keep_a, got_a)
        keep_oa = jnp.concatenate([keep_out, two_a[0]], axis=1)
        send_oa = jnp.concatenate([send_out, two_a[1]], axis=1)
    if fast:
        (got_up, got_oa, got_b, got_c), grad_c = beside(
            [(send_up, 4), (send_oa, 2), (send_b, 1), (send_c, 1)], grad_c
        )
        keep_up, send_up = parted(keep_up, got_up)
        keep_oa, send_oa = parted(keep_oa, got_oa)
        two_b, two_c = parted(keep_b, got_b), parted(keep_c, got_c)
        keep_bc = jnp.concatenate([two_b[0], two_c[0]], axis=1)
        send_bc = jnp.concatenate([two_b[1], two_c[1]], axis=1)
    input_grad = input_back(me, mix_quads, grad_one, (grad_a, grad_b, grad_c))
    if fast:
        (got_up, got_oa, got_bc), input_grad = beside(
            [(send_up, 8), (send_oa, 4), (send_bc, 2)], input_grad
        )
        share_up = added(keep_up[0], got_up[0])
        keep_oa, send_oa = parted(keep_oa, got_oa)
        keep_bc, send_bc = parted(keep_bc, got_bc)
        ((got_oa, got_bc),) = beside([(send_oa, 8), (send_bc, 4)])
        share_oa = added(keep_oa[0], got_oa[0])
        keep_bc, send_bc = parted(keep_bc, got_bc)
        share_bc = added(keep_bc[0], swapped(send_bc, 8)[0])
        share_vec = lax.dynamic_slice(share_bc[96:108], (0, index * share), (12, share))
        shares = (share_down, share_up, share_oa, share_bc, share_vec[:, None, :])
        norm_shares = shares[:3] + (share_bc[:96], share_vec)
    else:

        def scattered(matrix):
            return lax.psum_scatter(
                matrix.astype(jnp.float32), "dp", scatter_dimension=0, tiled=True
            )

        mix_blocks = jnp.concatenate(
            [
                whole_rows(keep[:, :48], send[:, :48], 1)
                for keep, send in ((keep_a, send_a), (keep_b, send_b), (keep_c, send_c))
            ]
        )
        bias_mixed = jnp.concatenate([sums_a[:1], sums_b[:1], sums_c[:1]]).reshape(HG, 3, QCOLS)
        grad_vec = jnp.concatenate(
            [
                bias_mixed[:, 0].reshape(1, D),
                bias_mixed[:, 2].reshape(1, D),
                sums_one[4:7],
                sums_one[0:4],
                sums_two[0:3],
            ],
            axis=0,
        )
        shares = (
            scattered(from_heads(mix_blocks)),
            scattered(whole_rows(keep_out, send_out, 1)[0]),
            scattered(from_columns(whole_rows(keep_up, send_up, 4))),
            scattered(whole_rows(keep_down, send_down, 1)[0]),
            lax.psum_scatter(grad_vec, "dp", scatter_dimension=1, tiled=True),
        )
        norm_shares = shares

    local_square = sum(jnp.sum(s * s) for s in norm_shares)
    firsts = (first_mix[0], first_out[0], first_up[0], first_down[0], first_vectors[0])
    seconds = (second_mix[0], second_out[0], second_up[0], second_down[0], second_vectors[0])
    if fast:
        norm = jnp.broadcast_to(local_square, (8, 128))
        norm = (norm + across(norm, 0, 8)) + (across(norm, 1, 0) + across(norm, 1, 8))
        norm = (norm + across(norm, 0, 4)) + (across(norm, 0, 2) + across(norm, 0, 6))
        norm = norm + across(norm, 0, 1)
        grad_square = norm[0, 0]
        arrays = [
            pltpu.with_memory_space_constraint(a, pltpu.HBM)
            for group in (masters, firsts, seconds)
            for a in group[:4] + (group[4][:, None, :],)
        ]
        updated = adam_all(norm, shares, arrays)
        updated = tuple(
            jnp.swapaxes(u, 0, 1) if i % 5 == 4 else u[None] for i, u in enumerate(updated)
        )
    else:
        grad_square = lax.psum(local_square, ("tower", "dp"))
        factor = jnp.minimum(1.0, clip_norm / (jnp.sqrt(grad_square) + 1e-06))
        rates = (matrix_rate, matrix_rate, matrix_rate, matrix_rate, vector_rate)
        results = [
            adam_update(masters[i], shares[i], firsts[i], seconds[i], rates[i], factor)
            for i in range(5)
        ]
        updated = tuple(r[i] for i in range(3) for r in results)
    return (
        output.reshape(1, MB, 1, L, D),
        input_grad.reshape(1, MB, 1, L, D),
        *updated,
        grad_square,
    )


def solution(mesh):
    rows = P("tower", None, "dp", None, None)
    shards = (P("tower", "dp", None),) * 4 + (P("tower", None, "dp"),)
    in_specs = (rows, P("tower", None, "dp", None), P(None, "dp"), rows) + shards * 3
    out_specs = (rows, rows) + shards * 3 + (P(),)
    return jax.shard_map(body, mesh=mesh, in_specs=in_specs, out_specs=out_specs, check_vma=False)
```
